32 devices in a mesh: dp: 4 (over x, core), expert: 8 (over z, y).
Axes of the slice: x: 2, y: 2, z: 4, core: 2. Of those that a mesh axis runs over, the one named last changes fastest.
Arguments:
- tokens: bfloat16 [8192, 1024], P(('dp', 'expert')), may hold values from -6 to 6
- gain_attn: bfloat16 [1024], P(('dp', 'expert')), may hold values from 0.5 to 1.5
- w_query: bfloat16 [1024, 1024], P(('dp', 'expert')), may hold values from -0.1875 to 0.1875
- w_key: bfloat16 [1024, 1024], P(('dp', 'expert')), may hold values from -0.1875 to 0.1875
- w_value: bfloat16 [1024, 1024], P(('dp', 'expert')), may hold values from -0.1875 to 0.1875
- w_output: bfloat16 [1024, 1024], P(('dp', 'expert')), may hold values from -1.5 to 1.5
- rel_bias: float32 [32, 16], replicated, may hold values from -4 to 4
- gain_ffn: bfloat16 [1024], P(('dp', 'expert')), may hold values from 0.5 to 1.5
- w_router: bfloat16 [1024, 8], P(('dp', 'expert')), may hold values from -0.125 to 0.125
- expert_gate: bfloat16 [8, 1024, 2816], P('expert', 'dp'), may hold values from -0.1875 to 0.1875
- expert_up: bfloat16 [8, 1024, 2816], P('expert', 'dp'), may hold values from -0.1875 to 0.1875
- expert_down: bfloat16 [8, 2816, 1024], P('expert', 'dp'), may hold values from -0.21875 to 0.21875
- routes: int32 [8192, 2], P(('dp', 'expert')), may hold values from 0 to 7, all different within a row; in each aligned block of 256 rows (0 to 255, 256 to 511, ...) at most 80 rows name the same one
- doc_lengths: int32 [4, 4], replicated, may hold values from 1 to 1792, 2048 in all within a row
- seq_valid: int32 [4], replicated, may hold values from 1536 to 2048
- grad_output: bfloat16 [8192, 1024], P(('dp', 'expert')), may hold values from -6 to 6
Outputs:
- mixed: bfloat16 [8192, 1024], P(('dp', 'expert'))
- grad_tokens: float32 [8192, 1024], P(('dp', 'expert'))
- grad_gain_attn: float32 [1024], P(('dp', 'expert'))
- grad_query: float32 [1024, 1024], P(('dp', 'expert'))
- grad_key: float32 [1024, 1024], P(('dp', 'expert'))
- grad_value: float32 [1024, 1024], P(('dp', 'expert'))
- grad_w_output: float32 [1024, 1024], P(('dp', 'expert'))
- grad_rel_bias: float32 [32, 16], replicated
- grad_gain_ffn: float32 [1024], P(('dp', 'expert'))
- grad_router: float32 [1024, 8], P(('dp', 'expert'))
- grad_expert_gate: float32 [8, 1024, 2816], P('expert', 'dp')
- grad_expert_up: float32 [8, 1024, 2816], P('expert', 'dp')
- grad_expert_down: float32 [8, 2816, 1024], P('expert', 'dp')
- head_factor: float32 [16], replicated
The draws below stay inside these ranges and needn't reach their ends.
Inputs may be any that keep to these rules, and one draw needn't show every extreme that they name: `routes`: each row names 2 different experts; among the tokens of one device no expert is named more than 80 times, and some device names some expert exactly 80 times. `doc_lengths`: each row sums to 2048.
All inputs are finite; a program needn't handle non-finite values.
Results may differ from the reference program's by a relative error of at most 0.015.
Values may be sent and summed in bfloat16 or wider, within the bound.
No kernel may reach another device: no remote copies, remote signals or barrier semaphores. Data moves between devices by JAX's collectives and lax.ppermute only.
A program may use at most 448 MiB of HBM per device.

```python
import math
import jax
import jax.numpy as jnp
import numpy as np
from jax import lax

D = 1024
HEADS = 16
HDIM = 64
FF = 2816
BUCKETS = 32
WINDOW = 1024
SEQ = 2048
DOCS = 4
TOP = 2
TOK_DEV = 256
EXPERTS = 8
CAP = 80
TOKENS = 8192
SEQS_ALL = 4
DEVICES = 32


def plant(drawn, key, smallest, top_value):
    spot = [jax.random.randint(jax.random.fold_in(key, axis), (), 0, length) for axis, length in enumerate(drawn.shape)]
    longest = drawn.shape.index(max(drawn.shape))
    neighbour = spot[:longest] + [(spot[longest] + 1) % drawn.shape[longest]] + spot[longest + 1:]
    return drawn.at[tuple(spot)].set(smallest).at[tuple(neighbour)].set(top_value)


def shard_levels(stream_key, dims, cuts, least, high):
    level = 1.0
    for axis_at, shards_of in cuts:
        heights = jax.random.uniform(jax.random.fold_in(jax.random.fold_in(stream_key, 6), axis_at), (shards_of,), jnp.float32, least / len(cuts), high / len(cuts))
        level = level * jnp.repeat(jnp.exp(heights), dims[axis_at] // shards_of).reshape((-1,) + (1,) * (len(dims) - 1 - axis_at))
    return level


def split_up(number_of, total, limit, skew):
    weights = [(1 << 20) // math.isqrt(rank ** skew) + 1 for rank in range(2, number_of + 1)]
    rest, counts = total - limit - (number_of - 1), [1] * (number_of - 1)
    while rest > 0:
        candidates = [i for i in range(number_of - 1) if counts[i] < limit]
        mass, remaining = sum([weights[i] for i in candidates]), rest
        for i in candidates:
            addition = min(limit - counts[i], max(1, remaining * weights[i] // mass), rest)
            counts[i] = counts[i] + addition
            rest = rest - addition
    return np.array([limit] + counts)


def ragged_sizes(stream_key, count, total, limit, skew):
    if count == 2:
        one = jax.random.randint(stream_key, (), max(1, total - limit), min(limit, total - 1) + 1)
        return jnp.stack([one, total - one])
    sizes = jnp.asarray(split_up(count, total, limit, skew), jnp.int32)
    couples = (count - 1) // 2
    donor, sink = sizes[1:1 + 2 * couples:2], sizes[2:2 + 2 * couples:2]
    room = jnp.minimum(donor - 1, limit - sink)
    shifted = jax.random.randint(jax.random.fold_in(stream_key, 1), (couples,), 0, 1 << 20) % (room + 1)
    sizes = sizes.at[1:1 + 2 * couples:2].set(donor - shifted).at[2:2 + 2 * couples:2].set(sink + shifted)
    return sizes[jax.random.permutation(jax.random.fold_in(stream_key, 2), count)]


def shared_out(key, own, number, rows, count, top, bound, lean):
    sequence = jax.random.permutation(key, count)
    packed, common = load_shares(count, rows * top, bound, lean, True), load_shares(count, rows * top, bound, lean, False)
    places = jnp.arange(count)

    def named(sizes, offset_by):
        used = int((sizes > 0).sum())
        fixed = max(1, used // 4)
        moved = fixed + (places - fixed + offset_by * (used - fixed)) % max(1, count - fixed)
        return jnp.zeros((count,), jnp.int32).at[sequence[jnp.where(places < fixed, places, moved)]].set(jnp.asarray(sizes, jnp.int32))

    sizes = jnp.where(number % 4 == 0, named(packed, number // 4), named(common, number - number // 4 - 1))
    mixed = jax.random.permutation(jax.random.fold_in(own, 3), count)
    source_of, sink = mixed[0:count // 2 * 2:2], mixed[1:count // 2 * 2:2]
    margin = jnp.minimum(sizes[source_of] - 1, bound - sizes[sink]) // 2
    margin = jnp.where((source_of == sequence[0]) | (sink == sequence[0]) | (sizes[sink] == 0), 0, jnp.maximum(margin, 0))
    moved = jax.random.randint(jax.random.fold_in(own, 4), (count // 2,), 0, 1 << 20) % (margin + 1)
    sizes = sizes.at[source_of].add(-moved).at[sink].add(moved)
    members = jnp.searchsorted(jnp.cumsum(sizes), jnp.arange(rows * top), side="right").astype(jnp.int32)
    listing = members.reshape(top, rows).T
    listing = listing[jax.random.permutation(jax.random.fold_in(own, 1), rows)]
    offset_by = jax.random.randint(jax.random.fold_in(own, 2), (rows, 1), 0, top)
    return jnp.take_along_axis(listing, (jnp.arange(top)[None, :] + offset_by) % top, axis=1)


def load_shares(number_of, total, reach, skew, full):
    loads = [(1 << 20) // math.isqrt(rank ** skew) + 1 for rank in range(1, number_of + 1)]
    largest = reach if full else min(reach, max(-(-total // number_of), total * loads[0] // sum(loads)))
    least = 1 if total - largest >= number_of - 1 else 0
    given, surplus = [largest] + [least] * (number_of - 1), total - largest - least * (number_of - 1)
    while surplus > 0:
        movable = [i for i in range(1, number_of) if given[i] < largest] or [i for i in range(1, number_of) if given[i] < reach]
        pool, remaining = sum([loads[i] for i in movable]), surplus
        for i in movable:
            extra = min(reach - given[i], max(1, remaining * loads[i] // pool), surplus)
            given[i] = given[i] + extra
            surplus = surplus - extra
    return np.array(given)


def centred(key, dims, deviation, most, shards=(), kind=jnp.bfloat16):
    result = deviation * jax.random.normal(key, dims, jnp.float32)
    if shards:
        result = result * shard_levels(key, dims, shards, -0.22, 0.18)
    return jnp.clip(result, -most, most).astype(kind)


def setup_inputs(seed: int = 0) -> dict:
    streams_of = jax.random.split(jax.random.key(seed), 17)
    tokens = centred(streams_of[0], (TOKENS, D), 1.0, 6.0, ((0, 32),))
    gain_attn = jnp.clip(1.0 + 0.1 * jax.random.normal(streams_of[1], (D,), jnp.float32), 0.5, 1.5).astype(jnp.bfloat16)
    w_query = centred(streams_of[2], (D, D), D ** -0.5, 0.1875, ((0, 32),))
    w_key = centred(streams_of[3], (D, D), D ** -0.5, 0.1875, ((0, 32),))
    w_value = centred(streams_of[4], (D, D), D ** -0.5, 0.1875, ((0, 32),))
    w_output = centred(streams_of[5], (D, D), (D // 64) ** -0.5, 1.5, ((0, 32),))
    rel_bias = centred(streams_of[6], (BUCKETS, HEADS), 1.0, 4.0, (), jnp.float32)
    gain_ffn = jnp.clip(1.0 + 0.1 * jax.random.normal(streams_of[7], (D,), jnp.float32), 0.5, 1.5).astype(jnp.bfloat16)
    w_router = centred(streams_of[8], (D, EXPERTS), (2 * D) ** -0.5, 0.125, ((0, 32),))
    expert_gate = centred(streams_of[9], (EXPERTS, D, FF), D ** -0.5, 0.1875, ((0, 8), (1, 4)))
    expert_up = centred(streams_of[10], (EXPERTS, D, FF), D ** -0.5, 0.1875, ((0, 8), (1, 4)))
    expert_down = centred(streams_of[11], (EXPERTS, FF, D), (FF // 4) ** -0.5, 0.21875, ((0, 8), (1, 4)))
    routes_keys = jax.random.split(jax.random.fold_in(streams_of[12], 1), TOKENS // TOK_DEV)
    routes_turns = jax.random.permutation(jax.random.fold_in(streams_of[12], 3), TOKENS // TOK_DEV)
    routes = jax.vmap(lambda own, number: shared_out(jax.random.fold_in(streams_of[12], 2), own, number, TOK_DEV, EXPERTS, TOP, CAP, 1))(routes_keys, routes_turns).reshape((TOKENS, TOP))
    doc_lengths = jax.vmap(lambda own: ragged_sizes(own, DOCS, SEQ, SEQ - SEQ // 8, 1))(jax.random.split(streams_of[13], SEQS_ALL)).reshape((SEQS_ALL, DOCS)).astype(jnp.int32)
    seq_valid = plant(jax.random.randint(streams_of[14], (SEQS_ALL,), SEQ - SEQ // 4, SEQ + 1), jax.random.fold_in(streams_of[14], 1), SEQ - SEQ // 4, SEQ).astype(jnp.int32)
    grad_output = centred(streams_of[15], (TOKENS, D), 1.0, 6.0, ((0, 32),))
    return dict(tokens=tokens, gain_attn=gain_attn, w_query=w_query, w_key=w_key, w_value=w_value, w_output=w_output, rel_bias=rel_bias, gain_ffn=gain_ffn, w_router=w_router, expert_gate=expert_gate, expert_up=expert_up, expert_down=expert_down, routes=routes, doc_lengths=doc_lengths, seq_valid=seq_valid, grad_output=grad_output)


epsilon = 1e-06
clip_level = 4.0

@jax.custom_vjp
def low(v):
    return lax.optimization_barrier(v.astype(jnp.bfloat16)).astype(jnp.float32)

@jax.custom_vjp
def low_back(v):
    return v

def low_keep(v):
    return (low(v), None)

def low_pass(kept, grad):
    return (grad,)

def back_keep(v):
    return (v, None)

def back_low(kept, grad):
    return (low(grad),)
low.defvjp(low_keep, low_pass)
low_back.defvjp(back_keep, back_low)

def both(values):
    return low(low_back(values))

def highest(left, right):
    return jnp.dot(left, right, precision=lax.Precision.HIGHEST)

def bucket_table(span, buckets):
    distance = np.arange(span) * 1.0
    exact = buckets // 2
    safe = np.maximum(distance, 1.0)
    spread = exact + np.floor(np.log(safe / exact) / np.log(128.0 / exact) * (buckets - exact))
    chosen = np.where(distance < exact, distance, np.minimum(spread, buckets - 1.0))
    marks = np.arange(buckets) * 1.0
    return jnp.asarray((chosen[:, None] == marks[None, :]).astype(np.float32))

def norm_rows(values, gain):
    return values * lax.rsqrt(lax.optimization_barrier(jnp.mean(values * values, axis=-1, keepdims=True)) + epsilon) * gain

def gelu_product(gate_pre, up_pre):
    return jax.nn.gelu(gate_pre, approximate=True) * up_pre

def gate_values(logits, chosen):
    probs = jax.nn.softmax(logits, axis=-1)
    picked = lax.optimization_barrier(jnp.sum(probs[:, None, :] * chosen, axis=2))
    return picked / lax.optimization_barrier(jnp.sum(picked, axis=1, keepdims=True))

def slot_places(routes, experts, capacity):
    chosen = (routes[:, :, None] == jnp.arange(experts, dtype=jnp.int32)[None, None, :]).astype(jnp.int32)
    order = jnp.swapaxes(chosen, 0, 1).reshape(-1, experts)
    before = jnp.cumsum(order, axis=0) - order
    slots = lax.optimization_barrier(jnp.sum(before * order, axis=1)).reshape(TOP, -1).T
    return routes * capacity + slots

def sequence_attention(pieces, dist_bias):
    query_seq, key_seq, value_seq, lengths, valid_len = pieces
    places = jnp.arange(SEQ, dtype=jnp.int32)
    ends = jnp.cumsum(lengths)
    label = lax.optimization_barrier(jnp.sum((places[:, None] >= ends[None, :]).astype(jnp.int32), axis=1))
    keep = places < valid_len
    key_label = jnp.concatenate([jnp.full((WINDOW,), -1, jnp.int32), label])
    key_keep = jnp.concatenate([jnp.zeros((WINDOW,), dtype=bool), keep])
    front = jnp.zeros((WINDOW, query_seq.shape[1]), jnp.float32)
    keys_ext = jnp.concatenate([front, key_seq], axis=0)
    values_ext = jnp.concatenate([front, value_seq], axis=0)
    rows = min(512, TOK_DEV)
    wide = WINDOW + rows
    scale = 1.0 / math.sqrt(HDIM)

    def one_block(index):
        start = index * rows
        query_rows = lax.dynamic_slice_in_dim(query_seq, start, rows, 0).reshape(rows, HEADS, HDIM)
        key_rows = lax.dynamic_slice_in_dim(keys_ext, start, wide, 0).reshape(wide, HEADS, HDIM)
        value_rows = lax.dynamic_slice_in_dim(values_ext, start, wide, 0).reshape(wide, HEADS, HDIM)
        query_mark = lax.dynamic_slice_in_dim(label, start, rows, 0)
        key_mark = lax.dynamic_slice_in_dim(key_label, start, wide, 0)
        key_good = lax.dynamic_slice_in_dim(key_keep, start, wide, 0)
        gap = jnp.arange(rows, dtype=jnp.int32)[:, None] + WINDOW - jnp.arange(wide, dtype=jnp.int32)[None, :]
        inside = (gap >= 0) & (gap < WINDOW) & (query_mark[:, None] == key_mark[None, :]) & key_good[None, :]
        allowed = inside | (gap == 0)
        clipped = jnp.clip(gap, 0, WINDOW - 1)
        scores = jnp.einsum('qhd,khd->hqk', query_rows, key_rows, precision=lax.Precision.HIGHEST) * scale
        scores = low_back(scores + jnp.take(dist_bias, clipped, axis=1))
        masked = jnp.where(allowed[None], scores, -1e+30)
        top = lax.optimization_barrier(jnp.max(masked, axis=2, keepdims=True))
        raised = jnp.exp(masked - top)
        attend_low = low(raised / lax.optimization_barrier(jnp.sum(raised, axis=2, keepdims=True)))
        heads_out = jnp.einsum('hqk,khd->qhd', attend_low, value_rows, precision=lax.Precision.HIGHEST)
        return (heads_out.reshape(rows, HEADS * HDIM), lax.optimization_barrier(jnp.max(top[..., 0], axis=1)))
    outputs, tops = lax.map(jax.checkpoint(one_block), jnp.arange(SEQ // rows))
    return (outputs.reshape(SEQ, HEADS * HDIM), lax.optimization_barrier(jnp.max(tops, axis=0)))

def expert_apply(pieces):
    rows, gate_w, up_w, down_w = pieces
    gate_pre = low_back(highest(rows, gate_w))
    up_pre = low_back(highest(rows, up_w))
    hidden = low(gelu_product(gate_pre, up_pre))
    return both(highest(hidden, down_w))

def forward(params, chosen, places, doc_lengths, seq_valid):
    inputs, gain_one, query_w, key_w, value_w, output_w, rel_w, gain_two, router_w, gate_w, up_w, down_w = params
    normed_one = low(norm_rows(inputs, gain_one))
    query_all = both(highest(normed_one, query_w))
    key_all = both(highest(normed_one, key_w))
    value_all = both(highest(normed_one, value_w))
    dist_bias = highest(bucket_table(WINDOW, BUCKETS), rel_w).T
    split = (SEQS_ALL, SEQ, D)
    attention, tops = lax.map(lambda pieces: sequence_attention(pieces, dist_bias), (query_all.reshape(split), key_all.reshape(split), value_all.reshape(split), doc_lengths, seq_valid))
    attention = both(attention.reshape(TOKENS, D))
    resid = inputs + low_back(highest(attention, output_w))
    normed_two = low(norm_rows(resid, gain_two))
    gates = gate_values(highest(normed_two, router_w), chosen)
    owner = jnp.repeat(jnp.arange(DEVICES, dtype=jnp.int32), TOK_DEV)[:, None]
    buffer = jnp.zeros((DEVICES, EXPERTS * CAP, D), jnp.float32)
    buffer = buffer.at[owner, places].add(jnp.broadcast_to(normed_two[:, None, :], (TOKENS, TOP, D)))
    buffer = low_back(buffer)
    expert_rows = buffer.reshape(DEVICES, EXPERTS, CAP, D).transpose(1, 0, 2, 3).reshape(EXPERTS, DEVICES * CAP, D)
    expert_out = lax.map(jax.checkpoint(expert_apply), (expert_rows, gate_w, up_w, down_w))
    returned = expert_out.reshape(EXPERTS, DEVICES, CAP, D).transpose(1, 0, 2, 3).reshape(DEVICES, EXPERTS * CAP, D)
    picked = returned[owner, places]
    final = resid + lax.optimization_barrier(jnp.sum(gates[:, :, None] * picked, axis=1))
    return (final, lax.optimization_barrier(jnp.max(tops, axis=0)))

def reference(tokens, gain_attn, w_query, w_key, w_value, w_output, rel_bias, gain_ffn, w_router, expert_gate, expert_up, expert_down, routes, doc_lengths, seq_valid, grad_output):
    params = tuple((value.astype(jnp.float32) for value in (tokens, gain_attn, w_query, w_key, w_value, w_output, rel_bias, gain_ffn, w_router, expert_gate, expert_up, expert_down)))
    local_routes = routes.reshape(DEVICES, TOK_DEV, TOP)
    places = jax.vmap(lambda part: slot_places(part, EXPERTS, CAP))(local_routes).reshape(TOKENS, TOP)
    chosen = (routes[:, :, None] == jnp.arange(EXPERTS, dtype=jnp.int32)[None, None, :]).astype(jnp.float32)
    final, pull, tops = jax.vjp(lambda *values: forward(values, chosen, places, doc_lengths, seq_valid), *params, has_aux=True)
    grads = pull(grad_output.astype(jnp.float32))
    head_factor = jnp.sqrt(clip_level / jnp.maximum(tops, 1.0))
    return (final.astype(jnp.bfloat16), grads[0], grads[1], grads[2], grads[3], grads[4], grads[5], grads[6], grads[7], grads[8], grads[9], grads[10], grads[11], head_factor)
```

```python
import jax
import jax.numpy as jnp
import numpy as np
from jax import lax
from jax.experimental import pallas as pl
from jax.experimental.pallas import tpu as pltpu
from jax.sharding import PartitionSpec as P

HEADS = 16
HDIM = 64
BUCKETS = 32
WINDOW = 1024
SEQ = 2048
DOCS = 4
TOP = 2

EPSILON = 1e-06
CLIP_LEVEL = 4.0
BF = jnp.bfloat16
F32 = jnp.float32
MASKED = -1e30
VMEM_BYTES = 56 * 1024 * 1024
AUX = 128
ROUTER_AT = 2
GAIN_AT = 63
BIAS_AT = 64
TOP_AT = 96
TOP_LOW_AT = 112


def dot(left, right, dims=((1,), (0,))):
    return lax.dot_general(left, right, (dims, ((), ())), preferred_element_type=F32)


def halves(values):
    high = values.astype(BF)
    return high, (values - high.astype(F32)).astype(BF)


def call(kernel, out_shape, flops, nbytes, **kwargs):
    return pl.pallas_call(
        kernel,
        out_shape=out_shape,
        compiler_params=pltpu.CompilerParams(vmem_limit_bytes=VMEM_BYTES),
        cost_estimate=pl.CostEstimate(
            flops=int(flops), bytes_accessed=int(nbytes), transcendentals=0
        ),
        **kwargs,
    )


def struct(shape, dtype):
    return jax.ShapeDtypeStruct(shape, dtype)


def bucket_of(span, buckets):
    distance = np.arange(span) * 1.0
    exact = buckets // 2
    safe = np.maximum(distance, 1.0)
    spread = exact + np.floor(np.log(safe / exact) / np.log(128.0 / exact) * (buckets - exact))
    return np.where(distance < exact, distance, np.minimum(spread, buckets - 1.0)).astype(np.int64)


def diagonal_tables(block, window, buckets):
    tiles = window // block + 1
    j = np.arange(2 * block)
    offset = np.where(j < block, -j, 2 * block - j)
    distance = np.arange(tiles)[:, None] * block + offset[None, :]
    inside = (distance >= 0) & (distance < window) & (j != block)[None, :]
    bucket = bucket_of(window, buckets)[np.clip(distance, 0, window - 1)]
    marks = (bucket[..., None] == np.arange(buckets)) & inside[..., None]
    return marks.astype(np.float32).reshape(-1, buckets), inside.reshape(-1)


def collect(parts, me, whole, arrived):
    for j, part in enumerate(parts):
        pltpu.make_async_copy(part, whole.at[me ^ j], arrived.at[j]).start()


def collected(parts, whole, arrived):
    for j, part in enumerate(parts):
        pltpu.make_async_copy(part, whole.at[0], arrived.at[j]).wait()


def part_copies(parts, source, first, rows, to, semaphore):
    cut = parts[-1].shape[0]
    if cut == parts[0].shape[0] or source < len(parts) - 2:
        return [pltpu.make_async_copy(parts[source].at[pl.ds(first, rows)], to, semaphore)]
    copies = []
    low = max(0, min(rows, cut - first))
    if low:
        copies.append(
            pltpu.make_async_copy(
                parts[source].at[pl.ds(first, low)], to.at[pl.ds(0, low)], semaphore
            )
        )
    if low < rows:
        copies.append(
            pltpu.make_async_copy(
                parts[source + 1].at[pl.ds(first + low - cut, rows - low)],
                to.at[pl.ds(low, rows - low)],
                semaphore,
            )
        )
    return copies


def gain_row(aux, at):
    rows = lax.broadcasted_iota(jnp.int32, (8, AUX), 0)
    lanes = lax.broadcasted_iota(jnp.int32, (8, AUX), 1)
    pick = jnp.where((rows == 0) & (lanes == at), 1.0, 0.0).astype(BF)
    return dot(pick, aux, ((1,), (1,)))[0:1]


def head_lanes(rows, lanes, head):
    lane = lax.broadcasted_iota(jnp.int32, (rows, lanes), 1)
    return lane // HDIM == head


def fold(values, combine):
    parts = [values[:, at : at + 128] for at in range(0, values.shape[1], 128)]
    total = parts[0]
    for part in parts[1:]:
        total = combine(total, part)
    return total


def attend_kernel(tiles, hp, sources, spread, pick_ref, me_ref, *refs):
    tok_refs = refs[:sources]
    w_refs = refs[sources : sources + spread]
    (diag_ref, ends_ref, normed_ref, qkv_ref, p_ref, out_ref, top_ref, aux_ref,
     bias, keys, values, tok, arrived, packed, w_arrived, gain) = refs[sources + spread :]
    i = pl.program_id(0)
    block, lanes = out_ref.shape
    width = normed_ref.shape[1]

    @pl.when(i == 0)
    def _():
        collect(w_refs, me_ref[0], packed, w_arrived)
        for at in range(tok.shape[0]):
            for source in range(sources - (tok_refs[-1].shape[0] != tok_refs[0].shape[0])):
                @pl.when(pick_ref[at] == source)
                def _():
                    for copy in part_copies(
                        tok_refs, source, 0, block, tok.at[at], arrived.at[at]
                    ):
                        copy.start()
        for h in range(hp):
            for m in range(tiles):
                at = h * tiles + m
                row = jnp.broadcast_to(diag_ref[at : at + 1, :], (block, 2 * block))
                at = (tiles - 1 - m) * block
                bias[h, :, at : at + block] = pltpu.roll(
                    row, 0, 1, stride=1, stride_axis=0
                )[:, :block]
        top_ref[...] = jnp.full_like(top_ref, MASKED)
        collected(w_refs, packed, w_arrived)
        aux_ref[...] = packed[:, :, 3 * lanes :].reshape(width, AUX)
        gain[...] = gain_row(aux_ref[...], 0)

    pltpu.make_async_copy(tok_refs[0].at[pl.ds(0, block)], tok.at[i], arrived.at[i]).wait()
    x = tok[i].astype(F32)
    r = lax.rsqrt(jnp.mean(x * x, axis=1, keepdims=True) + EPSILON)
    normed = (x * r * gain[...]).astype(BF)
    normed_ref[...] = normed
    w_cols = packed[:, :, : 3 * lanes].reshape(width, 3 * lanes)
    qkv = dot(normed, w_cols).astype(BF)
    qkv_ref[...] = qkv
    here = pl.multiple_of(i * block, block)
    keys[pl.ds(here, block), :] = qkv[:, lanes : 2 * lanes]
    values[pl.ds(here, block), :] = qkv[:, 2 * lanes :]
    query = qkv[:, :lanes] * jnp.asarray(HDIM ** -0.5, BF)
    masks = [head_lanes(block, lanes, h) for h in range(hp)]
    heads = [jnp.where(masks[h], query, jnp.zeros_like(query)) for h in range(hp)]

    def label_of(positions):
        label = jnp.zeros(positions.shape, jnp.int32)
        for at in range(DOCS):
            label += jnp.where(positions >= ends_ref[at], 1, 0)
        return label

    qlab = label_of(lax.broadcasted_iota(jnp.int32, (block, 1), 0) + i * block)

    def rows_of(span):
        wide = span * block
        first = pl.multiple_of((i - span + 1) * block, block)
        column = (tiles - span) * block
        key = keys[pl.ds(first, wide), :]
        value = values[pl.ds(first, wide), :]
        position = lax.broadcasted_iota(jnp.int32, (1, wide), 1) + first
        same = qlab == jnp.where(position < ends_ref[DOCS], label_of(position), -1)
        row = lax.broadcasted_iota(jnp.int32, (block, block), 0)
        diagonal = row == lax.broadcasted_iota(jnp.int32, (block, block), 1)
        out = None
        for h in range(hp):
            s = dot(heads[h], key, ((1,), (1,))) + bias[h, :, column:]
            last = wide - block
            own = jnp.where(same[:, last:] | diagonal, s[:, last:], MASKED)
            if span > 1:
                own = jnp.concatenate([jnp.where(same[:, :last], s[:, :last], MASKED), own], axis=1)
            best = jnp.max(own, axis=1, keepdims=True)
            top_ref[h : h + 1, :] = jnp.maximum(
                top_ref[h : h + 1, :], jnp.max(best, axis=0, keepdims=True)
            )
            p = jnp.exp(own - best)
            p = (p * (1.0 / jnp.sum(p, axis=1, keepdims=True))).astype(BF)
            p_ref[0, h, :, column:] = p
            part = dot(p, value)
            out = part if out is None else jnp.where(masks[h], part, out)
        out_ref[...] = out.astype(BF)

    for span in range(1, tiles):
        @pl.when(i == span - 1)
        def _():
            rows_of(span)

    @pl.when(i >= tiles - 1)
    def _():
        rows_of(tiles)


def attend(pick, me, parts, packed, diag, ends, hp, block):
    width = parts[0].shape[1]
    count = pick.shape[0]
    seq = count * block
    lanes = hp * HDIM
    tiles = diag.shape[0] // hp
    row = lambda i: (i, 0)
    fixed = lambda i: (0, 0)
    pairs = count * tiles * hp * block * block
    return call(
        lambda *refs: attend_kernel(tiles, hp, len(parts), len(packed), *refs),
        (
            struct((seq, width), BF),
            struct((seq, 3 * lanes), BF),
            struct((count, hp, block, tiles * block), BF),
            struct((seq, lanes), BF),
            struct((8, 128), F32),
            struct((width, AUX), BF),
        ),
        24e9,
        8 * seq * width + 2 * pairs,
        grid=(count,),
        in_specs=[pl.BlockSpec(memory_space=pltpu.SMEM)] * 2
        + [pl.BlockSpec(memory_space=pl.ANY)] * (len(parts) + len(packed))
        + [
            pl.BlockSpec(diag.shape, fixed),
            pl.BlockSpec(memory_space=pltpu.SMEM),
        ],
        out_specs=[
            pl.BlockSpec((block, width), row),
            pl.BlockSpec((block, 3 * lanes), row),
            pl.BlockSpec((1, hp, block, tiles * block), lambda i: (i, 0, 0, 0)),
            pl.BlockSpec((block, lanes), row),
            pl.BlockSpec((8, 128), fixed),
            pl.BlockSpec((width, AUX), fixed),
        ],
        scratch_shapes=[
            pltpu.VMEM((hp, block, tiles * block), F32),
            pltpu.VMEM((seq, lanes), BF),
            pltpu.VMEM((seq, lanes), BF),
            pltpu.VMEM((count, block, width), BF),
            pltpu.SemaphoreType.DMA((count,)),
            pltpu.VMEM((len(packed),) + packed[0].shape, BF),
            pltpu.SemaphoreType.DMA((len(packed),)),
            pltpu.VMEM((1, width), F32),
        ],
    )(pick, me, *parts, *packed, diag, ends)


def output_rows_kernel(sources, first, rows, pick_ref, *refs):
    parts = refs[:sources]
    out_ref, qkv_ref, arrived = refs[sources:]
    width = out_ref.shape[1]

    def place(at, number):
        here = pl.ds(at * rows, rows)
        if number == 0:
            return out_ref.at[here]
        return qkv_ref.at[here, pl.ds((number - 1) * width, width)]

    for at in range(pick_ref.shape[0]):
        for source in range(len(parts) - (parts[-1].shape[0] != parts[0].shape[0])):
            @pl.when(pick_ref[at] == source)
            def _():
                for number in range(4):
                    for copy in part_copies(
                        parts, source, first + number * rows, rows, place(at, number),
                        arrived.at[at, number],
                    ):
                        copy.start()
    for at in range(pick_ref.shape[0]):
        for number in range(4):
            pltpu.make_async_copy(
                parts[0].at[pl.ds(0, rows)], place(at, number), arrived.at[at, number]
            ).wait()


def attend_back_kernel(tiles, hp, me_ref, grad_ref, p_ref, qkv_ref, normed_ref, marks_ref, top_ref,
                       out_ref, kept_ref, away_ref, bias_grad, key_grad, value_grad):
    i = pl.program_id(0)
    block, lanes = grad_ref.shape

    @pl.when(i == 0)
    def _():
        bias_grad[...] = jnp.zeros_like(bias_grad)
        key_grad[...] = jnp.zeros_like(key_grad)
        value_grad[...] = jnp.zeros_like(value_grad)

    here = pl.multiple_of(i * block, block)
    query = qkv_ref[pl.ds(here, block), :lanes] * jnp.asarray(HDIM ** -0.5, BF)
    grad = grad_ref[...]
    masks = [head_lanes(block, lanes, h) for h in range(hp)]

    def rows_of(span):
        wide = span * block
        first = pl.multiple_of((i - span + 1) * block, block)
        column = (tiles - span) * block
        key = qkv_ref[pl.ds(first, wide), lanes : 2 * lanes]
        value = qkv_ref[pl.ds(first, wide), 2 * lanes :]
        out = key_part = value_part = None
        for h in range(hp):
            head = jnp.where(masks[h], query, jnp.zeros_like(query))
            head_grad = jnp.where(masks[h], grad, jnp.zeros_like(grad))
            weight = p_ref[0, h, :, column:]
            wide_weight = weight.astype(F32)
            t = wide_weight * dot(head_grad, value, ((1,), (1,)))
            s = t - wide_weight * jnp.sum(t, axis=1, keepdims=True)
            bias_grad[h, :, column:] += s
            s = s.astype(BF)
            part = dot(s, key)
            out = part if out is None else jnp.where(masks[h], part, out)
            part = dot(s, head, ((0,), (0,)))
            key_part = part if key_part is None else key_part + part
            part = dot(weight, head_grad, ((0,), (0,)))
            value_part = part if value_part is None else value_part + part
        key_grad[pl.ds(first, wide), :] += key_part
        value_grad[pl.ds(first, wide), :] += value_part
        out_ref[pl.ds(here, block), :lanes] = (out * HDIM ** -0.5).astype(BF)

    for span in range(1, tiles):
        @pl.when(i == span - 1)
        def _():
            rows_of(span)

    @pl.when(i >= tiles - 1)
    def _():
        rows_of(tiles)

    @pl.when(i == pl.num_programs(0) - 1)
    def _():
        out_ref[:, lanes : 2 * lanes] = key_grad[...].astype(BF)
        out_ref[:, 2 * lanes :] = value_grad[...].astype(BF)
        grad_cols = dot(normed_ref[...], out_ref[...], ((0,), (0,))).astype(BF)
        split_store(kept_ref, away_ref, me_ref[0], grad_cols)
        bins = marks_ref.shape[1]
        wide = 3 * lanes
        notes = []
        for h in range(hp):
            total = jnp.zeros((1, bins), F32)
            for m in range(tiles):
                at = (tiles - 1 - m) * block
                x = bias_grad[h, :, at : at + block]
                x = jnp.concatenate([x, jnp.zeros((block, block), F32)], axis=1)
                half = block // 2
                while half >= 1:
                    x = x[:half] + pltpu.roll(x[half : 2 * half], 2 * block - half, 1)
                    half //= 2
                high, low = halves(x)
                part = marks_ref[m * 2 * block : (m + 1) * 2 * block, :]
                total += dot(high, part) + dot(low, part)
            notes.append(jnp.concatenate([total, jnp.zeros((1, wide - bins), F32)], axis=1))
        spot = lax.broadcasted_iota(jnp.int32, (1, AUX), 1) == me_ref[0]
        for h in range(hp):
            top = top_ref[h : h + 1, :]
            high = top.astype(BF).astype(F32)
            notes.append(
                jnp.concatenate(
                    [jnp.where(spot, high, 0.0), jnp.where(spot, top - high, 0.0)]
                    + [jnp.zeros((1, wide - 2 * AUX), F32)],
                    axis=1,
                )
            )
        notes.append(jnp.zeros((16 - 2 * hp, wide), F32))
        notes = jnp.concatenate(notes, axis=0).astype(BF)
        for ref in (kept_ref, away_ref):
            for at in range(ref.shape[0]):
                ref[at, ref.shape[1] - 16 :] = notes


def attend_back(me, attention_grad, weights, qkv, normed, marks, top, hp, block, spread):
    seq, lanes = attention_grad.shape
    count = seq // block
    width = normed.shape[1]
    tiles = weights.shape[3] // block
    fixed = lambda i: (0, 0)
    pairs = count * tiles * hp * block * block
    owned = (spread // 2, width // spread + 16, 3 * lanes)
    return call(
        lambda *refs: attend_back_kernel(tiles, hp, *refs),
        (struct((seq, 3 * lanes), BF), struct(owned, BF), struct(owned, BF)),
        60e9,
        10 * seq * lanes + 2 * pairs,
        grid=(count,),
        in_specs=[
            pl.BlockSpec(memory_space=pltpu.SMEM),
            pl.BlockSpec((block, lanes), lambda i: (i, 0)),
            pl.BlockSpec((1, hp, block, tiles * block), lambda i: (i, 0, 0, 0)),
            pl.BlockSpec((seq, 3 * lanes), fixed),
            pl.BlockSpec((seq, width), fixed),
            pl.BlockSpec(marks.shape, fixed),
            pl.BlockSpec(top.shape, fixed),
        ],
        out_specs=[pl.BlockSpec((seq, 3 * lanes), fixed)]
        + [pl.BlockSpec(owned, lambda i: (0, 0, 0))] * 2,
        scratch_shapes=[
            pltpu.VMEM((hp, block, tiles * block), F32),
            pltpu.VMEM((seq, lanes), F32),
            pltpu.VMEM((seq, lanes), F32),
        ],
    )(me, attention_grad, weights, qkv, normed, marks, top)


def upstream_kernel(places_ref, other_ref, grad_ref, out_ref):
    experts, capacity, _ = out_ref.shape
    rows = grad_ref.shape[0]
    slots = experts * capacity
    other = other_ref[...]
    slot = lax.broadcasted_iota(jnp.int32, (slots, rows), 0)
    first = jnp.where(slot == places_ref[0:1, :], 1.0, 0.0).astype(BF)
    second = jnp.where(slot == places_ref[1:2, :], 1.0, 0.0).astype(BF)
    sent = dot(first + second, grad_ref[...]).astype(BF)
    named = (dot(first, other[0]) + dot(second, other[1])).astype(BF)
    for at in range(experts):
        here = slice(at * capacity, (at + 1) * capacity)
        out_ref[at, :, 128:] = sent[here]
        out_ref[at, :, :128] = named[here]


def token_front_kernel(spread, me_ref, attn_ref, tok_ref, aux_ref, places_ref, *refs):
    w_refs = refs[:spread]
    attention_ref, resid_ref, normed_ref = refs[spread : spread + 3]
    buffers = refs[spread + 3 : -2]
    whole, arrived = refs[-2:]
    collect(w_refs, me_ref[0], whole, arrived)
    blocks = attn_ref.shape[0]
    attention = jnp.concatenate([attn_ref[at] for at in range(blocks)], axis=1)
    attention_ref[...] = attention
    width = attention.shape[1]
    gain = gain_row(aux_ref[...], 1)
    collected(w_refs, whole, arrived)
    resid = tok_ref[...].astype(F32) + dot(attention, whole[...].reshape(width, width))
    resid_ref[...] = resid
    r = lax.rsqrt(jnp.mean(resid * resid, axis=1, keepdims=True) + EPSILON)
    normed = (resid * r * gain).astype(BF)
    normed_ref[...] = normed
    slots = buffers[0].shape[0]
    slot = lax.broadcasted_iota(jnp.int32, (slots * len(buffers), normed.shape[0]), 0)
    named = (slot == places_ref[2:3, :]) | (slot == places_ref[3:4, :])
    sent = dot(jnp.where(named, 1.0, 0.0).astype(BF), normed).astype(BF)
    for k, buffer in enumerate(buffers):
        buffer[...] = sent[k * slots : (k + 1) * slots]


def token_middle_kernel(returned_ref, resid_ref, normed_ref, aux_ref, ids_ref, grad_ref,
                        mixed_ref, logit_ref, route_ref):
    slots = returned_ref.shape[0]
    rows = resid_ref.shape[0]
    slot = lax.broadcasted_iota(jnp.int32, (rows, slots), 1)
    first = jnp.where(slot == ids_ref[:, 0:1], 1.0, 0.0).astype(BF)
    second = jnp.where(slot == ids_ref[:, 1:2], 1.0, 0.0).astype(BF)
    returned = returned_ref[...]
    first_out = dot(first, returned)
    second_out = dot(second, returned)
    normed = normed_ref[...]
    logits = dot(normed, aux_ref[...])
    lane = lax.broadcasted_iota(jnp.int32, logits.shape, 1) - ROUTER_AT
    at_first = lane == ids_ref[:, 2:3]
    at_second = lane == ids_ref[:, 3:4]
    gap = jnp.sum(
        jnp.where(at_first, logits, 0.0) - jnp.where(at_second, logits, 0.0),
        axis=1, keepdims=True,
    )
    gate_one = 1.0 / (1.0 + jnp.exp(-gap))
    gate_two = 1.0 / (1.0 + jnp.exp(gap))
    mixed_ref[...] = (resid_ref[...] + gate_one * first_out + gate_two * second_out).astype(BF)
    upstream = grad_ref[...].astype(F32)
    change = jnp.sum(upstream * (first_out - second_out), axis=1, keepdims=True)
    slope = gate_one * gate_two * change
    logit = jnp.where(at_first, slope, 0.0) - jnp.where(at_second, slope, 0.0)
    logit_ref[...] = logit
    high, low = halves(logit)
    route_ref[...] = dot(normed, high, ((0,), (0,))) + dot(normed, low, ((0,), (0,)))


def norm_back(values, gain, grad):
    r = lax.rsqrt(jnp.mean(values * values, axis=1, keepdims=True) + EPSILON)
    scaled = grad * gain
    slope = jnp.mean(values * scaled, axis=1, keepdims=True)
    return r * scaled - values * (r * r * r * slope), r


def token_back_kernel(spread, me_ref, logit_ref, aux_ref, ids_ref, resid_ref, grad_ref, back_ref,
                      *refs):
    w_refs = refs[:spread]
    attention_ref, route_ref = refs[spread : spread + 2]
    resid_grad_ref, attention_grad_ref, kept_ref, away_ref, whole, arrived = refs[-6:]
    collect(w_refs, me_ref[0], whole, arrived)
    resid = resid_ref[...]
    rows, width = resid.shape
    slots = back_ref.shape[0]
    slot = lax.broadcasted_iota(jnp.int32, (rows, slots), 1)
    named = (slot == ids_ref[:, 0:1]) | (slot == ids_ref[:, 1:2])
    normed_grad = dot(jnp.where(named, 1.0, 0.0).astype(BF), back_ref[...])
    high, low = halves(logit_ref[...])
    aux = aux_ref[...]
    gain = gain_row(aux, 1)
    normed_grad += dot(high, aux, ((1,), (1,))) + dot(low, aux, ((1,), (1,)))
    part, r = norm_back(resid, gain, normed_grad)
    resid_grad = grad_ref[...].astype(F32) + part
    resid_grad_ref[...] = resid_grad
    gain_grad = jnp.sum(normed_grad * resid * r, axis=0, keepdims=True)
    proj = resid_grad.astype(BF)
    blocks, _, lanes = attention_grad_ref.shape
    collected(w_refs, whole, arrived)
    grad = dot(proj, whole[...].reshape(width, width), ((1,), (1,))).astype(BF)
    for at in range(blocks):
        attention_grad_ref[at] = grad[:, at * lanes : (at + 1) * lanes]
    grad_proj = dot(attention_ref[...], proj, ((0,), (0,))).astype(BF)
    lane = lax.broadcasted_iota(jnp.int32, (width, AUX), 1)
    gain_grad = jnp.broadcast_to(gain_grad, (AUX, width)).T
    small = jnp.where(lane == GAIN_AT, gain_grad, route_ref[...]).astype(BF)
    split_store(kept_ref, away_ref, me_ref[0], jnp.concatenate([grad_proj, small], axis=1))


def token_last_kernel(blocks_ref, w_ref, tok_ref, aux_ref, resid_grad_ref, out_ref, grads, total):
    part = pl.program_id(0)
    blocks, _, wide = blocks_ref.shape
    lanes = wide // 3
    for number in range(3):
        @pl.when(part == number)
        def _():
            for at in range(blocks):
                grads[:, at * lanes : (at + 1) * lanes] = blocks_ref[
                    at, :, number * lanes : (number + 1) * lanes
                ]

    term = dot(grads[...], w_ref[...], ((1,), (1,)))

    @pl.when(part == 0)
    def _():
        total[...] = term

    @pl.when(part > 0)
    def _():
        total[...] += term

    @pl.when(part == 2)
    def _():
        change, _ = norm_back(tok_ref[...].astype(F32), gain_row(aux_ref[...], 0), total[...])
        out_ref[...] = resid_grad_ref[...] + change


def note_row(notes, hp, spread, head):
    lane = lax.broadcasted_iota(jnp.int32, (1, AUX), 1)
    rel = jnp.where(lane < BUCKETS, notes[head : head + 1, :AUX], 0.0)
    tops = notes[hp + head : hp + head + 1]
    high = jnp.where(lane < spread, tops[:, :AUX], 0.0)
    low = jnp.where(lane < spread, tops[:, AUX : 2 * AUX], 0.0)
    return rel, high, low


def join_kernel(hp, spread, own_ref, proj_kept_ref, proj_got_ref, cols_kept_ref, cols_got_ref,
                kept_ref, away_ref):
    rows, wide = proj_kept_ref.shape
    pairs, own_rows, _ = kept_ref.shape
    even = own_ref[0] % 2 == 0
    proj = proj_kept_ref[...].astype(F32) + proj_got_ref[...].astype(F32)
    cols = cols_kept_ref[...].astype(F32) + cols_got_ref[...].astype(F32)
    notes = cols[rows:]
    row = lax.broadcasted_iota(jnp.int32, (own_rows, AUX), 0)
    extra = jnp.zeros((own_rows, AUX), F32)
    for h in range(hp):
        rel, high, low = note_row(notes, hp, spread, h)
        line = pltpu.roll(rel, BIAS_AT, 1) + pltpu.roll(high, TOP_AT, 1)
        line += pltpu.roll(low, TOP_LOW_AT, 1)
        extra += jnp.where(row == h + hp * (own_ref[0] % 2), line, 0.0)
    extra = jnp.concatenate([jnp.zeros((own_rows, wide - AUX), F32), extra], axis=1)
    for pair in range(pairs):
        at = 2 * pair * own_rows
        one, two = slice(at, at + own_rows), slice(at + own_rows, at + 2 * own_rows)
        kept_ref[pair, :, :wide] = (jnp.where(even, proj[one], proj[two]) + extra).astype(BF)
        away_ref[pair, :, :wide] = (jnp.where(even, proj[two], proj[one]) + extra).astype(BF)
        kept_ref[pair, :, wide:] = jnp.where(even, cols[one], cols[two]).astype(BF)
        away_ref[pair, :, wide:] = jnp.where(even, cols[two], cols[one]).astype(BF)


def pair_kernel(wide, own_ref, kept_ref, got_ref, *sends):
    even = own_ref[0] % 2 == 0
    for k, send in enumerate(sends):
        pair = (own_ref[0] // 2) ^ k
        kept, got = kept_ref[pair], got_ref[pair]
        send[:, :wide] = (kept[:, :wide].astype(F32) + got[:, :wide].astype(F32)).astype(BF)
        columns = kept.shape[1] - wide
        send[:, wide : wide + columns] = jnp.where(even, kept[:, wide:], got[:, wide:])
        send[:, wide + columns :] = jnp.where(even, got[:, wide:], kept[:, wide:])


def join_plain(hp, spread, place, groups, proj_terms, cols_terms):
    proj, cols = joined(proj_terms), joined(cols_terms)
    rows, wide = proj.shape
    own_rows = rows // groups
    notes = cols[rows:]
    whole = jnp.concatenate([proj, cols[:rows]], axis=1).reshape(groups, own_rows, -1)
    lines = []
    for h in range(hp):
        rel, high, low = note_row(notes, hp, spread, h)
        line = jnp.roll(rel, BIAS_AT, 1) + jnp.roll(high, TOP_AT, 1) + jnp.roll(low, TOP_LOW_AT, 1)
        lines.append(line)
    extra = jnp.concatenate(lines, axis=0)
    extra = jnp.pad(extra, ((0, own_rows - hp), (wide - AUX, whole.shape[2] - wide)))
    whole = (whole + extra).astype(BF)
    return [
        lax.dynamic_index_in_dim(whole, place ^ k, axis=0, keepdims=False) for k in range(groups)
    ]


def owner_kernel(hp, sharers, spread, own_ref, q_ref, k_ref, v_ref, gain_ref, *refs):
    (proj_ref, route_ref, gain_two_ref, gq_ref, gk_ref, gv_ref, gain_one_ref, rel_ref,
     factor_ref, summary_ref) = refs[-10:]
    blocks = refs[:-10]
    experts = route_ref.shape[0]
    eye = lax.broadcasted_iota(jnp.int32, (proj_ref.shape[0],) * 2, 0)
    eye = eye == lax.broadcasted_iota(jnp.int32, eye.shape, 1)

    def as_row(column):
        return jnp.sum(jnp.where(eye, column, 0.0), axis=0, keepdims=True)

    width = proj_ref.shape[1]
    lanes = hp * HDIM
    sources = (blocks[0].shape[1] - width - AUX) // (3 * lanes)
    total = None
    for block in blocks:
        term = block[:, : width + AUX].astype(F32)
        total = term if total is None else total + term
    proj_ref[...] = total[:, :width]
    small = total[:, width:].T
    route_ref[...] = small[ROUTER_AT : ROUTER_AT + experts]
    gain_two_ref[...] = small[GAIN_AT : GAIN_AT + 1]
    outs = (gq_ref, gk_ref, gv_ref)
    for out in outs:
        out[...] = jnp.zeros_like(out)
    lane = lax.broadcasted_iota(jnp.int32, (1, 128), 1)
    summary_ref[...] = jnp.where(
        lax.broadcasted_iota(jnp.int32, summary_ref.shape, 1) == 64, MASKED, 0.0
    )
    for k, source in [(k, source) for k in range(len(blocks)) for source in range(sources)]:
        block = blocks[k]
        seat = (((own_ref[0] // sources) ^ k) * sources + source) % sharers
        at = pl.multiple_of(seat * lanes, lanes)
        for part, out in enumerate(outs):
            first = width + AUX + (3 * source + part) * lanes
            out[:, pl.ds(at, lanes)] += block[:, first : first + lanes].astype(F32)
        notes = block[:, width : width + AUX].astype(F32)
        for h in range(hp):
            note = notes[source * hp + h : source * hp + h + 1]
            rel = jnp.where(lane < BUCKETS, pltpu.roll(note, AUX - BIAS_AT, 1), 0.0)
            tops = pltpu.roll(note, AUX - TOP_AT, 1) + pltpu.roll(note, AUX - TOP_LOW_AT, 1)
            top = jnp.max(jnp.where(lane < spread, tops, MASKED), axis=1, keepdims=True)
            old = summary_ref[pl.ds(seat * hp + h, 1), :]
            new = jnp.where(lane == 64, jnp.maximum(old, top), old + rel)
            summary_ref[pl.ds(seat * hp + h, 1), :] = new
    rel_ref[...] = summary_ref[:, :BUCKETS]
    factor_ref[...] = jnp.sqrt(CLIP_LEVEL / jnp.maximum(summary_ref[...].T[64:65], 1.0))
    grad = jnp.zeros((proj_ref.shape[0], 1), F32)
    for out, w_ref in zip(outs, (q_ref, k_ref, v_ref)):
        grad += jnp.sum(out[...] * w_ref[...].astype(F32), axis=1, keepdims=True)
    gain_one_ref[...] = as_row(grad) / gain_ref[...]


GELU_A = 0.7978845608028654
GELU_B = 0.044715


def expert_kernel(groups, own_ref, upstream_ref, aux_ref, gate_ref, up_ref, down_ref, *refs):
    blocks = refs[:groups]
    (gate_pre_ref, up_pre_ref, out_ref, rows_ref, slot_grad_ref, grad_down_ref, total) = refs[groups:]
    f = pl.program_id(0)
    capacity, width = blocks[0].shape

    @pl.when(f == 0)
    def _():
        total[...] = jnp.zeros_like(total)
        for k, block in enumerate(blocks):
            rows_ref[k * capacity : (k + 1) * capacity, :] = block[...]
        all_logits = dot(rows_ref[...], aux_ref[...])
        for k in range(groups):
            here = slice(k * capacity, (k + 1) * capacity)
            logits = all_logits[here]
            lane = lax.broadcasted_iota(jnp.int32, logits.shape, 1) - ROUTER_AT
            upstream = upstream_ref[own_ref[0] ^ k]
            other = upstream[:, 0:1].astype(F32).astype(jnp.int32)
            gap = jnp.sum(
                jnp.where(lane == other, logits, 0.0) - jnp.where(lane == own_ref[0], logits, 0.0),
                axis=1, keepdims=True,
            )
            gate = 1.0 / (1.0 + jnp.exp(gap))
            slot_grad_ref[here, :] = (gate * upstream[:, 128:].astype(F32)).astype(BF)

    rows = rows_ref[...]
    gate_pre = dot(rows, gate_ref[...])
    up_pre = dot(rows, up_ref[...])
    gate_pre_ref[...] = gate_pre
    up_pre_ref[...] = up_pre
    inner = jnp.tanh(GELU_A * (gate_pre + GELU_B * gate_pre * gate_pre * gate_pre))
    hidden = (0.5 * gate_pre * (1.0 + inner) * up_pre).astype(BF)
    total[...] += dot(hidden, down_ref[...])
    grad_down_ref[...] = dot(hidden, slot_grad_ref[...], ((0,), (0,))).astype(BF)

    @pl.when(f == pl.num_programs(0) - 1)
    def _():
        for k in range(groups):
            out_ref[own_ref[0] ^ k] = total[k * capacity : (k + 1) * capacity, :].astype(BF)


def expert_forward(own, upstream, aux, blocks, gate, up, down, tile):
    groups = len(blocks)
    capacity, width = blocks[0].shape
    count = groups * capacity
    ff = gate.shape[1]
    fixed = lambda f: (0, 0)
    cols = lambda f: (0, f)
    return call(
        lambda *refs: expert_kernel(groups, *refs),
        (
            struct((count, ff), F32),
            struct((count, ff), F32),
            struct((groups, capacity, width), BF),
            struct((count, width), BF),
            struct((count, width), BF),
            struct((ff, width), BF),
        ),
        24e9,
        6 * width * ff + 10 * count * ff,
        grid=(ff // tile,),
        in_specs=[
            pl.BlockSpec(memory_space=pltpu.SMEM),
            pl.BlockSpec(upstream.shape, lambda f: (0, 0, 0)),
            pl.BlockSpec(aux.shape, fixed),
            pl.BlockSpec((width, tile), cols),
            pl.BlockSpec((width, tile), cols),
            pl.BlockSpec((tile, width), lambda f: (f, 0)),
        ]
        + [pl.BlockSpec((capacity, width), fixed)] * groups,
        out_specs=[
            pl.BlockSpec((count, tile), cols),
            pl.BlockSpec((count, tile), cols),
            pl.BlockSpec((groups, capacity, width), lambda f: (0, 0, 0)),
            pl.BlockSpec((count, width), fixed),
            pl.BlockSpec((count, width), fixed),
            pl.BlockSpec((tile, width), lambda f: (f, 0)),
        ],
        scratch_shapes=[pltpu.VMEM((count, width), F32)],
    )(own, upstream, aux, gate, up, down, *blocks)


def split_store(kept_ref, away_ref, me, values):
    rows = values.shape[0] // (2 * kept_ref.shape[0])
    for d in range(2 * kept_ref.shape[0]):
        block = values[d * rows : (d + 1) * rows]
        @pl.when(me % 2 == d % 2)
        def _():
            kept_ref[d // 2, :rows] = block

        @pl.when(me % 2 != d % 2)
        def _():
            away_ref[d // 2, :rows] = block


def expert_back_kernel(own_ref, me_ref, slot_grad_ref, rows_ref, gate_pre_ref, up_pre_ref, down_ref,
                       gate_ref, up_ref, row_grad_ref, grad_gate_ref, up_kept_ref, up_away_ref,
                       total, pre_grads, split_rows):
    f = pl.program_id(0)
    tiles = pl.num_programs(0) - 1
    tile = gate_ref.shape[1]
    groups, capacity, _ = row_grad_ref.shape

    def through_gelu(slot):
        hidden_grad = dot(slot_grad_ref[...], down_ref[...], ((1,), (1,)))
        v = gate_pre_ref[...]
        square = v * v
        inner = jnp.tanh(v * (GELU_A + GELU_A * GELU_B * square))
        half = 0.5 + 0.5 * inner
        slope = half + (0.5 * v) * (1.0 - inner * inner) * (
            GELU_A + 3.0 * GELU_A * GELU_B * square
        )
        pre_grads[slot, :, :tile] = (hidden_grad * up_pre_ref[...] * slope).astype(BF)
        pre_grads[slot, :, tile:] = (hidden_grad * (v * half)).astype(BF)

    def to_weights(slot):
        both = pre_grads[slot]
        weights = jnp.concatenate([gate_ref[...], up_ref[...]], axis=1)
        total[...] += dot(both, weights, ((1,), (1,)))
        grad_gate_ref[...] = dot(rows_ref[...], both[:, :tile], ((0,), (0,))).astype(BF)
        grads = dot(split_rows[...], both[:, tile:], ((0,), (0,))).astype(BF)
        half = grads.shape[0] // 2
        up_kept_ref[...] = grads[:half].reshape(up_kept_ref.shape)
        up_away_ref[...] = grads[half:].reshape(up_kept_ref.shape)

    @pl.when(f == 0)
    def _():
        total[...] = jnp.zeros_like(total)
        part = up_kept_ref.shape[1]
        half = rows_ref.shape[1] // 2
        even = me_ref[0] % 2 == 0
        for pair in range(up_kept_ref.shape[0]):
            one = rows_ref[:, 2 * pair * part : (2 * pair + 1) * part]
            two = rows_ref[:, (2 * pair + 1) * part : (2 * pair + 2) * part]
            at = pair * part
            split_rows[:, at : at + part] = jnp.where(even, one, two)
            split_rows[:, half + at : half + at + part] = jnp.where(even, two, one)
        through_gelu(0)

    @pl.when((f > 0) & (f < tiles))
    def _():
        to_weights((f - 1) % 2)
        through_gelu(f % 2)

    @pl.when(f == tiles)
    def _():
        to_weights((f - 1) % 2)
        for k in range(groups):
            row_grad_ref[own_ref[0] ^ k] = total[k * capacity : (k + 1) * capacity, :].astype(BF)


def expert_backward(own, me, slot_grad, rows, gate_pre, up_pre, gate, up, down, tile, groups,
                    spread):
    count, width = rows.shape
    ff = gate.shape[1]
    tiles = ff // tile
    fixed = lambda f: (0, 0)
    now = lambda f: (0, jnp.minimum(f, tiles - 1))
    before = lambda f: (0, jnp.maximum(f - 1, 0))
    owned = (spread // 2, width // spread)
    return call(
        expert_back_kernel,
        [
            struct((groups, count // groups, width), BF),
            struct((width, ff), BF),
        ]
        + [struct(owned + (ff,), BF)] * 2,
        30e9,
        12 * width * ff + 10 * count * ff,
        grid=(tiles + 1,),
        in_specs=[
            pl.BlockSpec(memory_space=pltpu.SMEM),
            pl.BlockSpec(memory_space=pltpu.SMEM),
            pl.BlockSpec((count, width), fixed),
            pl.BlockSpec((count, width), fixed),
            pl.BlockSpec((count, tile), now),
            pl.BlockSpec((count, tile), now),
            pl.BlockSpec((tile, width), lambda f: (jnp.minimum(f, tiles - 1), 0)),
            pl.BlockSpec((width, tile), before),
            pl.BlockSpec((width, tile), before),
        ],
        out_specs=[
            pl.BlockSpec((groups, count // groups, width), lambda f: (0, 0, 0)),
            pl.BlockSpec((width, tile), before),
        ]
        + [pl.BlockSpec(owned + (tile,), lambda f: (0, 0, jnp.maximum(f - 1, 0)))] * 2,
        scratch_shapes=[
            pltpu.VMEM((count, width), F32),
            pltpu.VMEM((2, count, 2 * tile), BF),
            pltpu.VMEM((count, width), BF),
        ],
    )(own, me, slot_grad, rows, gate_pre, up_pre, down, gate, up)


def slot_places(routes, experts, capacity):
    chosen = (routes[:, :, None] == jnp.arange(experts, dtype=jnp.int32)[None, None, :]).astype(
        jnp.int32
    )
    order = jnp.swapaxes(chosen, 0, 1).reshape(-1, experts)
    before = jnp.cumsum(order, axis=0) - order
    slots = jnp.sum(before * order, axis=1).reshape(TOP, -1).T
    return routes * capacity + slots


def flip(values, axis, mask):
    n = lax.axis_size(axis)
    return lax.ppermute(values, axis, [(k, k ^ mask) for k in range(n)])


def gather_parts(part, axis):
    return gather_rest({0: part}, axis, lax.axis_size(axis) // 2)


def gather_rest(held, axis, bit):
    while bit >= 1:
        held.update({j ^ bit: flip(values, axis, bit) for j, values in list(held.items())})
        bit //= 2
    return [held[j] for j in range(len(held))]


def swap_parts(parts, axis):
    return [parts[0]] + [flip(parts[k], axis, k) for k in range(1, len(parts))]


def ring_parts(tokens, before, between):
    devices = lax.axis_size("expert")
    line = list(range(0, devices, 2)) + list(range(devices - 1, 0, -2))
    spots = [line.index(k) for k in range(devices)]

    def move(values, step):
        pairs = [(line[k], line[(k + step) % devices]) for k in range(devices)]
        return lax.ppermute(values, "expert", pairs)

    ahead = [tokens]
    behind = [tokens]
    half = devices // 2
    for k in range(1, half):
        pair = (move(ahead[-1], 1), move(behind[-1], -1))
        if k == half - 2:
            *pair, first = lax.optimization_barrier((*pair, before[0]))
            before = (between(first),) + before[1:]
        elif k == half - 1:
            *pair, before = lax.optimization_barrier((*pair, before))
        else:
            pair = lax.optimization_barrier(pair)
        ahead.append(pair[0])
        behind.append(pair[1])
    cut = tokens.shape[0] // 2
    farthest = (move(ahead[-1][:cut], 1), move(behind[-1][cut:], -1))
    parts = ahead + behind[:0:-1] + list(farthest)
    spot = jnp.asarray(spots, jnp.int32)
    mine = jnp.sum(jnp.where(jnp.arange(devices) == lax.axis_index("expert"), spot, 0))
    gap = (mine - spot) % devices
    gap = jnp.where(gap == half, devices - 1, jnp.where(gap > half, gap - 1, gap))
    return gap.astype(jnp.int32), parts, before


def scatter_step(parts, axis, me, bit):
    pairs = parts.reshape((parts.shape[0] // 2, 2) + parts.shape[1:])
    mine = (me // bit) % 2
    away = lax.dynamic_index_in_dim(pairs, 1 - mine, axis=1, keepdims=False)
    kept = lax.dynamic_index_in_dim(pairs, mine, axis=1, keepdims=False)
    return kept, flip(away, axis, bit)


def joined(parts):
    return parts[0].astype(F32) + parts[1].astype(F32)


def scatter_rest(parts, axis):
    n = lax.axis_size(axis)
    me = lax.axis_index(axis)
    bit = 2
    while True:
        terms = scatter_step(parts, axis, me, bit)
        bit *= 2
        if bit >= n:
            return tuple(term[0] for term in terms)
        parts = joined(terms).astype(BF)


def body(tokens, gain_attn, w_query, w_key, w_value, w_output, rel_bias, gain_ffn, w_router,
         expert_gate, expert_up, expert_down, routes, doc_lengths, seq_valid, grad_output):
    length, width = tokens.shape
    groups = lax.axis_size("expert")
    spread = lax.axis_size("dp")
    place = lax.axis_index("expert")
    device = lax.axis_index("dp") * groups + place
    experts = w_router.shape[1]
    capacity = 5 * TOP * length // (4 * experts)
    slots = experts * capacity
    sharers = SEQ // length
    hp = HEADS // sharers
    lanes = hp * HDIM
    own_rows = w_query.shape[0]
    teams = None
    if groups != sharers:
        teams = [list(range(at, at + sharers)) for at in range(0, groups, sharers)]
    both = ("dp", "expert")

    def exchange(blocks):
        return lax.all_to_all(blocks, "expert", 0, 0, axis_index_groups=teams, tiled=True)

    def exchange_all(blocks):
        return lax.all_to_all(blocks, "expert", 0, 0, tiled=True)

    def columns(w):
        return w.reshape(own_rows, sharers, lanes).swapaxes(0, 1)

    extra = jnp.concatenate([gain_attn[:, None], gain_ffn[:, None], w_router], axis=1)
    extra = jnp.pad(extra, ((0, 0), (0, AUX - extra.shape[1])))
    sent = jnp.concatenate(
        [
            columns(w_query),
            columns(w_key),
            columns(w_value),
            jnp.broadcast_to(extra[None], (sharers, own_rows, AUX)),
        ],
        axis=2,
    )
    sent = jnp.tile(sent, (groups // sharers, 1, 1))
    gate_all = lax.all_gather(expert_gate[0], "dp", axis=0, tiled=True)
    up_all = lax.all_gather(expert_up[0], "dp", axis=0, tiled=True)
    down_all = lax.all_gather(expert_down[0], "dp", axis=0, tiled=True)

    places = slot_places(routes, experts, capacity)
    near_places = places + ((routes ^ place) - routes) * capacity
    ids = jnp.concatenate([places, routes, near_places], axis=1)
    ids = jnp.pad(ids, ((0, 0), (0, 128 - ids.shape[1])))
    places_row = jnp.pad(
        jnp.concatenate([places, near_places], axis=1).T, ((0, 4), (0, 0)), constant_values=-1
    )
    other = jnp.broadcast_to(routes.T[::-1, :, None], (TOP, length, 128)).astype(BF)
    upstream = call(
        upstream_kernel,
        struct((experts, capacity, width + 128), BF),
        3e9,
        4 * slots * width,
    )(places_row, other, grad_output)

    number = (device * length) // SEQ
    ends = jnp.cumsum(lax.dynamic_index_in_dim(doc_lengths, number, keepdims=False))
    ends = jnp.concatenate([ends, lax.dynamic_index_in_dim(seq_valid, number)]).astype(jnp.int32)
    block = length
    marks, inside = diagonal_tables(block, WINDOW, BUCKETS)
    head_at = (place % sharers) * hp
    own_bias = lax.dynamic_slice_in_dim(rel_bias, head_at, hp, axis=1)
    diag = jnp.dot(jnp.asarray(marks), own_bias, precision=lax.Precision.HIGHEST)
    diag = jnp.where(jnp.asarray(inside)[:, None], diag, MASKED)
    tiles = WINDOW // block + 1
    diag = diag.T.reshape(hp * tiles, 2 * block)
    packed = exchange_all(sent).reshape(groups * own_rows, 3 * lanes + AUX)
    mixed_rows = jnp.concatenate([tokens, w_output, w_query, w_key, w_value], axis=0)
    if teams is None:
        def between(values):
            return gather_parts(values, "dp")

        before = (packed, upstream, diag, ends, ids)
        pick, parts, before = ring_parts(mixed_rows, before, between)
        packed, upstream, diag, ends, ids = before
    else:
        whole = lax.all_gather(mixed_rows, "expert", axis=0, axis_index_groups=teams)
        pick = jnp.arange(sharers, dtype=jnp.int32)
        parts = [whole[at] for at in range(sharers)]
        packed = gather_parts(packed, "dp")
    me = lax.axis_index("dp").astype(jnp.int32).reshape(1)
    if teams is None:
        output_rows, qkv_rows = call(
            lambda *refs: output_rows_kernel(len(parts), length, own_rows, *refs),
            (struct((groups * own_rows, width), BF), struct((groups * own_rows, 3 * width), BF)),
            1e9,
            16 * groups * own_rows * width,
            in_specs=[pl.BlockSpec(memory_space=pltpu.SMEM)]
            + [pl.BlockSpec(memory_space=pl.ANY)] * len(parts),
            out_specs=[pl.BlockSpec(memory_space=pltpu.VMEM)] * 2,
            scratch_shapes=[pltpu.SemaphoreType.DMA((sharers, 4))],
        )(pick, *parts)
        output_rows, attend_parts = lax.optimization_barrier((output_rows, parts))
    else:
        output_rows = lax.all_gather(w_output, "expert", axis=0, tiled=True)
        qkv_rows = jnp.concatenate([w_query, w_key, w_value], axis=1)
        qkv_rows = lax.all_gather(qkv_rows, "expert", axis=0, tiled=True)
        attend_parts = parts
    output_parts = {0: output_rows, spread // 2: flip(output_rows, "dp", spread // 2)}

    upstream, _ = lax.optimization_barrier((upstream, parts))
    upstream = exchange_all(upstream)

    normed_one, qkv, weights, attn, top, aux = attend(
        pick, me, attend_parts, packed, diag, ends, hp, block
    )
    attn, upstream, output_parts = lax.optimization_barrier((attn, upstream, output_parts))
    output_parts = gather_rest(output_parts, "dp", spread // 4)
    attn_blocks = exchange(attn.reshape(sharers, length, lanes))

    vmem = pl.BlockSpec(memory_space=pltpu.VMEM)
    smem = pl.BlockSpec(memory_space=pltpu.SMEM)
    loose = pl.BlockSpec(memory_space=pl.ANY)
    gathered = [
        pltpu.VMEM((spread,) + output_parts[0].shape, BF),
        pltpu.SemaphoreType.DMA((spread,)),
    ]
    attention, resid, normed_two, *buffers = call(
        lambda *refs: token_front_kernel(spread, *refs),
        [
            struct((length, width), BF),
            struct((length, width), F32),
            struct((length, width), BF),
        ]
        + [struct((capacity, width), BF)] * groups,
        5e9,
        2 * width * width + 8 * length * width,
        in_specs=[smem] + [vmem] * 4 + [loose] * spread,
        scratch_shapes=gathered,
    )(me, attn_blocks, tokens, aux, places_row, *output_parts)
    rows = swap_parts(buffers, "expert")
    qkv_rows, _ = lax.optimization_barrier((qkv_rows, attn))
    qkv_all = lax.all_gather(qkv_rows, "dp", axis=0, tiled=True)

    tile = 256 if expert_gate.shape[2] % 256 == 0 else 128
    own = place.astype(jnp.int32).reshape(1)
    gate_pre, up_pre, expert_out, rows, slot_grad, grad_down = expert_forward(
        own, upstream, aux, rows, gate_all, up_all, down_all, tile
    )
    expert_out, qkv_all = lax.optimization_barrier((expert_out, qkv_all))
    returned = exchange_all(expert_out)
    row_grad, *expert_grads = expert_backward(
        own, me, slot_grad, rows, gate_pre, up_pre, gate_all, up_all, down_all, tile, groups,
        spread,
    )
    returned, row_grad, expert_grads = lax.optimization_barrier(
        (returned, row_grad, expert_grads)
    )
    grad_gate, up_kept, up_away = expert_grads
    up_first = joined((up_kept, flip(up_away, "dp", 1))).astype(BF)
    owned_down = lax.psum_scatter(grad_down, "dp", scatter_dimension=0, tiled=True)
    returned = returned.reshape(slots, width)
    back = exchange_all(row_grad)
    mixed, logit_grad, route_grad = call(
        token_middle_kernel,
        (
            struct((length, width), BF),
            struct((length, 128), F32),
            struct((width, 128), F32),
        ),
        5e9,
        2 * slots * width + 8 * length * width,
    )(returned, resid, normed_two, aux, ids, grad_output)
    back, owned_down = lax.optimization_barrier((back, owned_down))
    owned_down = owned_down.astype(F32)
    back = back.reshape(slots, width)
    cores = [list(range(core, spread, 2)) for core in range(2)]

    def scatter_chips(parts):
        parts = parts.reshape((-1,) + parts.shape[2:])
        return lax.psum_scatter(
            parts, "dp", scatter_dimension=0, axis_index_groups=cores, tiled=True
        )

    owned_gate = lax.psum_scatter(grad_gate, "dp", scatter_dimension=0, tiled=True)
    owned_up = scatter_chips(up_first)
    resid_grad, attention_grad, proj_kept, proj_away = call(
        lambda *refs: token_back_kernel(spread, *refs),
        (
            struct((length, width), F32),
            struct((sharers, length, lanes), BF),
            struct((spread // 2, width // spread, width + AUX), BF),
            struct((spread // 2, width // spread, width + AUX), BF),
        ),
        6e9,
        2 * width * width + 2 * slots * width + 8 * length * width,
        in_specs=[smem] + [vmem] * 6 + [loose] * spread + [vmem] * 2,
        scratch_shapes=gathered,
    )(me, logit_grad, aux, ids, resid, grad_output, back, *output_parts, attention, route_grad)
    attention_grad = exchange(attention_grad).reshape(SEQ, lanes)
    proj_first = proj_kept.astype(F32) + flip(proj_away, "dp", 1).astype(F32)
    attention_grad, proj_first, _ = lax.optimization_barrier(
        (attention_grad, proj_first.astype(BF), up_first)
    )
    proj_terms = scatter_rest(proj_first, "dp")

    grad_qkv_rows, cols_kept, cols_away = attend_back(
        me, attention_grad, weights, qkv, normed_one, jnp.asarray(marks, BF), top, hp, block, spread
    )
    grad_qkv_rows, cols_away, proj_terms, owned_gate = lax.optimization_barrier(
        (grad_qkv_rows, cols_away, proj_terms, owned_gate)
    )
    grads_here = exchange(grad_qkv_rows.reshape(sharers, length, 3 * lanes))
    owned_gate = owned_gate.astype(F32)
    fixed = lambda part: (0, 0)
    grad_tokens = call(
        token_last_kernel,
        struct((length, width), F32),
        60e9,
        6 * width * width + 12 * length * width,
        grid=(3,),
        in_specs=[
            pl.BlockSpec(grads_here.shape, lambda part: (0, 0, 0)),
            pl.BlockSpec((width, width), lambda part: (0, part)),
            pl.BlockSpec((length, width), fixed),
            pl.BlockSpec(aux.shape, fixed),
            pl.BlockSpec((length, width), fixed),
        ],
        out_specs=pl.BlockSpec((length, width), fixed),
        scratch_shapes=[pltpu.VMEM((length, width), BF), pltpu.VMEM((length, width), F32)],
    )(grads_here, qkv_all, tokens, aux, resid_grad)

    cols_first = cols_kept.astype(F32) + flip(cols_away, "dp", 1).astype(F32)
    cols_terms = scatter_rest(cols_first.astype(BF), "dp")
    if own_rows % 16 == 0:
        pairs = groups // 2
        blocks = struct((pairs, own_rows, width + AUX + 3 * lanes), BF)
        pairs_kept, pairs_away = call(
            lambda *refs: join_kernel(hp, spread, *refs),
            [blocks] * 2,
            1e9,
            8 * groups * own_rows * width,
            in_specs=[smem] + [vmem] * 4,
        )(own, *proj_terms, *cols_terms)
        sends = call(
            lambda *refs: pair_kernel(width + AUX, *refs),
            [struct((own_rows, width + AUX + 6 * lanes), BF)] * pairs,
            1e9,
            8 * groups * own_rows * width,
            in_specs=[smem] + [vmem] * 2,
        )(own, pairs_kept, flip(pairs_away, "expert", 1))
        owned = [sends[0]] + [flip(sends[k], "expert", 2 * k) for k in range(1, pairs)]
    else:
        sends = join_plain(hp, spread, place, groups, proj_terms, cols_terms)
        owned = swap_parts(sends, "expert")
    owned[1], owned_up = lax.optimization_barrier((owned[1], owned_up))
    owned_up = owned_up.astype(F32)
    *owned, grad_tokens = lax.optimization_barrier((*owned, grad_tokens))
    grad_proj, route, gain_two, grad_q, grad_k, grad_v, gain_one, rel, factor = call(
        lambda *refs: owner_kernel(hp, sharers, spread, *refs),
        (
            struct((own_rows, width), F32),
            struct((experts, own_rows), F32),
            struct((1, own_rows), F32),
            struct((own_rows, width), F32),
            struct((own_rows, width), F32),
            struct((own_rows, width), F32),
            struct((1, own_rows), F32),
            struct((HEADS, BUCKETS), F32),
            struct((1, HEADS), F32),
        ),
        2e9,
        8 * own_rows * width,
        in_specs=[smem] + [vmem] * (4 + len(owned)),
        scratch_shapes=[pltpu.VMEM((HEADS, 128), F32)],
    )(own, w_query, w_key, w_value, gain_attn.astype(F32)[None], *owned)
    return (
        mixed,
        grad_tokens,
        gain_one[0],
        grad_q,
        grad_k,
        grad_v,
        grad_proj,
        rel.T,
        gain_two[0],
        route.T,
        owned_gate[None],
        owned_up[None],
        owned_down[None],
        factor[0],
    )


def solution(mesh):
    rows = P(("dp", "expert"), None)
    vector = P(("dp", "expert"))
    expert = P("expert", "dp", None)
    return jax.shard_map(
        body,
        mesh=mesh,
        in_specs=(
            rows, vector, rows, rows, rows, rows, P(), vector, rows,
            expert, expert, expert, rows, P(), P(), rows,
        ),
        out_specs=(
            rows, rows, vector, rows, rows, rows, rows, P(), vector, rows,
            expert, expert, expert, P(),
        ),
        check_vma=False,
    )
```

```python
import jax
import jax.numpy as jnp
import numpy as np
from jax import lax
from jax.experimental import pallas as pl
from jax.experimental.pallas import tpu as pltpu
from jax.sharding import PartitionSpec as P

HEADS = 16
HDIM = 64
BUCKETS = 32
WINDOW = 1024
SEQ = 2048
DOCS = 4
TOP = 2

EPSILON = 1e-06
CLIP_LEVEL = 4.0
BF = jnp.bfloat16
F32 = jnp.float32
MASKED = -1e30
AUX = 128
ROUTER_AT = 2
GAIN_AT = 63
BIAS_AT = 64
TOP_AT = 96
TOP_LOW_AT = 112


def dot(left, right, dims=((1,), (0,))):
    return lax.dot_general(left, right, (dims, ((), ())), preferred_element_type=F32)


def halves(values):
    high = values.astype(BF)
    return high, (values - high.astype(F32)).astype(BF)


def call(kernel, out_shape, flops, nbytes, mib=56, **kwargs):
    return pl.pallas_call(
        kernel,
        out_shape=out_shape,
        compiler_params=pltpu.CompilerParams(vmem_limit_bytes=mib * 1024 * 1024),
        cost_estimate=pl.CostEstimate(
            flops=int(flops), bytes_accessed=int(nbytes), transcendentals=0
        ),
        **kwargs,
    )


def struct(shape, dtype):
    return jax.ShapeDtypeStruct(shape, dtype)


def bucket_of(span, buckets):
    distance = np.arange(span) * 1.0
    exact = buckets // 2
    safe = np.maximum(distance, 1.0)
    spread = exact + np.floor(np.log(safe / exact) / np.log(128.0 / exact) * (buckets - exact))
    return np.where(distance < exact, distance, np.minimum(spread, buckets - 1.0)).astype(np.int64)


def diagonal_tables(block, window, buckets):
    tiles = window // block + 1
    j = np.arange(2 * block)
    offset = np.where(j < block, -j, 2 * block - j)
    distance = np.arange(tiles)[:, None] * block + offset[None, :]
    inside = (distance >= 0) & (distance < window) & (j != block)[None, :]
    bucket = bucket_of(window, buckets)[np.clip(distance, 0, window - 1)]
    marks = (bucket[..., None] == np.arange(buckets)) & inside[..., None]
    return marks.astype(np.float32).reshape(-1, buckets), inside.reshape(-1)


def collect(parts, me, whole, arrived):
    for j, part in enumerate(parts):
        pltpu.make_async_copy(part, whole.at[me ^ j], arrived.at[j]).start()


def collected(parts, whole, arrived):
    for j, part in enumerate(parts):
        pltpu.make_async_copy(part, whole.at[0], arrived.at[j]).wait()


def part_copies(parts, source, first, rows, to, semaphore):
    cut = parts[-1].shape[0]
    if cut == parts[0].shape[0] or source < len(parts) - 2:
        return [pltpu.make_async_copy(parts[source].at[pl.ds(first, rows)], to, semaphore)]
    copies = []
    low = max(0, min(rows, cut - first))
    if low:
        copies.append(
            pltpu.make_async_copy(
                parts[source].at[pl.ds(first, low)], to.at[pl.ds(0, low)], semaphore
            )
        )
    if low < rows:
        copies.append(
            pltpu.make_async_copy(
                parts[source + 1].at[pl.ds(first + low - cut, rows - low)],
                to.at[pl.ds(low, rows - low)],
                semaphore,
            )
        )
    return copies


def gain_row(aux, at):
    rows = lax.broadcasted_iota(jnp.int32, (8, AUX), 0)
    lanes = lax.broadcasted_iota(jnp.int32, (8, AUX), 1)
    pick = jnp.where((rows == 0) & (lanes == at), 1.0, 0.0).astype(BF)
    return dot(pick, aux, ((1,), (1,)))[0:1]


def head_lanes(rows, lanes, head):
    lane = lax.broadcasted_iota(jnp.int32, (rows, lanes), 1)
    return lane // HDIM == head


def fold(values, combine):
    parts = [values[:, at : at + 128] for at in range(0, values.shape[1], 128)]
    total = parts[0]
    for part in parts[1:]:
        total = combine(total, part)
    return total


def attend_kernel(tiles, hp, sources, spread, pick_ref, me_ref, *refs):
    tok_refs = refs[:sources]
    w_refs = refs[sources : sources + spread]
    (diag_ref, ends_ref, normed_ref, qkv_ref, p_ref, out_ref, top_ref, aux_ref,
     bias, keys, values, tok, arrived, packed, w_arrived, gain) = refs[sources + spread :]
    i = pl.program_id(0)
    block, lanes = out_ref.shape
    width = normed_ref.shape[1]

    @pl.when(i == 0)
    def _():
        collect(w_refs, me_ref[0], packed, w_arrived)
        for at in range(tok.shape[0]):
            for source in range(sources - (tok_refs[-1].shape[0] != tok_refs[0].shape[0])):
                @pl.when(pick_ref[at] == source)
                def _():
                    for copy in part_copies(
                        tok_refs, source, 0, block, tok.at[at], arrived.at[at]
                    ):
                        copy.start()
        for h in range(hp):
            for m in range(tiles):
                at = h * tiles + m
                row = jnp.broadcast_to(diag_ref[at : at + 1, :], (block, 2 * block))
                at = (tiles - 1 - m) * block
                bias[h, :, at : at + block] = pltpu.roll(
                    row, 0, 1, stride=1, stride_axis=0
                )[:, :block]
        top_ref[...] = jnp.full_like(top_ref, MASKED)
        collected(w_refs, packed, w_arrived)
        aux_ref[...] = packed[:, :, 3 * lanes :].reshape(width, AUX)
        gain[...] = gain_row(aux_ref[...], 0)

    pltpu.make_async_copy(tok_refs[0].at[pl.ds(0, block)], tok.at[i], arrived.at[i]).wait()
    x = tok[i].astype(F32)
    r = lax.rsqrt(jnp.mean(x * x, axis=1, keepdims=True) + EPSILON)
    normed = (x * r * gain[...]).astype(BF)
    normed_ref[...] = normed
    w_cols = packed[:, :, : 3 * lanes].reshape(width, 3 * lanes)
    qkv = dot(normed, w_cols).astype(BF)
    qkv_ref[...] = qkv
    here = pl.multiple_of(i * block, block)
    keys[pl.ds(here, block), :] = qkv[:, lanes : 2 * lanes]
    values[pl.ds(here, block), :] = qkv[:, 2 * lanes :]
    query = qkv[:, :lanes] * jnp.asarray(HDIM ** -0.5, BF)
    masks = [head_lanes(block, lanes, h) for h in range(hp)]
    heads = [jnp.where(masks[h], query, jnp.zeros_like(query)) for h in range(hp)]

    def label_of(positions):
        label = jnp.zeros(positions.shape, jnp.int32)
        for at in range(DOCS):
            label += jnp.where(positions >= ends_ref[at], 1, 0)
        return label

    qlab = label_of(lax.broadcasted_iota(jnp.int32, (block, 1), 0) + i * block)

    def rows_of(span):
        wide = span * block
        first = pl.multiple_of((i - span + 1) * block, block)
        column = (tiles - span) * block
        key = keys[pl.ds(first, wide), :]
        value = values[pl.ds(first, wide), :]
        position = lax.broadcasted_iota(jnp.int32, (1, wide), 1) + first
        same = qlab == jnp.where(position < ends_ref[DOCS], label_of(position), -1)
        row = lax.broadcasted_iota(jnp.int32, (block, block), 0)
        diagonal = row == lax.broadcasted_iota(jnp.int32, (block, block), 1)
        out = None
        for h in range(hp):
            s = dot(heads[h], key, ((1,), (1,))) + bias[h, :, column:]
            last = wide - block
            own = jnp.where(same[:, last:] | diagonal, s[:, last:], MASKED)
            if span > 1:
                own = jnp.concatenate([jnp.where(same[:, :last], s[:, :last], MASKED), own], axis=1)
            best = jnp.max(own, axis=1, keepdims=True)
            top_ref[h : h + 1, :] = jnp.maximum(
                top_ref[h : h + 1, :], jnp.max(best, axis=0, keepdims=True)
            )
            p = jnp.exp(own - best)
            p = (p * (1.0 / jnp.sum(p, axis=1, keepdims=True))).astype(BF)
            p_ref[0, h, :, column:] = p
            part = dot(p, value)
            out = part if out is None else jnp.where(masks[h], part, out)
        out_ref[...] = out.astype(BF)

    for span in range(1, tiles):
        @pl.when(i == span - 1)
        def _():
            rows_of(span)

    @pl.when(i >= tiles - 1)
    def _():
        rows_of(tiles)


def attend(pick, me, parts, packed, diag, ends, hp, block):
    width = parts[0].shape[1]
    count = pick.shape[0]
    seq = count * block
    lanes = hp * HDIM
    tiles = diag.shape[0] // hp
    row = lambda i: (i, 0)
    fixed = lambda i: (0, 0)
    pairs = count * tiles * hp * block * block
    return call(
        lambda *refs: attend_kernel(tiles, hp, len(parts), len(packed), *refs),
        (
            struct((seq, width), BF),
            struct((seq, 3 * lanes), BF),
            struct((count, hp, block, tiles * block), BF),
            struct((seq, lanes), BF),
            struct((8, 128), F32),
            struct((width, AUX), BF),
        ),
        24e9,
        8 * seq * width + 2 * pairs,
        grid=(count,),
        in_specs=[pl.BlockSpec(memory_space=pltpu.SMEM)] * 2
        + [pl.BlockSpec(memory_space=pl.ANY)] * (len(parts) + len(packed))
        + [
            pl.BlockSpec(diag.shape, fixed),
            pl.BlockSpec(memory_space=pltpu.SMEM),
        ],
        out_specs=[
            pl.BlockSpec((block, width), row),
            pl.BlockSpec((block, 3 * lanes), row),
            pl.BlockSpec((1, hp, block, tiles * block), lambda i: (i, 0, 0, 0)),
            pl.BlockSpec((block, lanes), row),
            pl.BlockSpec((8, 128), fixed),
            pl.BlockSpec((width, AUX), fixed),
        ],
        scratch_shapes=[
            pltpu.VMEM((hp, block, tiles * block), F32),
            pltpu.VMEM((seq, lanes), BF),
            pltpu.VMEM((seq, lanes), BF),
            pltpu.VMEM((count, block, width), BF),
            pltpu.SemaphoreType.DMA((count,)),
            pltpu.VMEM((len(packed),) + packed[0].shape, BF),
            pltpu.SemaphoreType.DMA((len(packed),)),
            pltpu.VMEM((1, width), F32),
        ],
    )(pick, me, *parts, *packed, diag, ends)


def output_rows_kernel(sources, first, rows, pick_ref, *refs):
    parts = refs[:sources]
    out_ref, qkv_ref, arrived = refs[sources:]
    width = out_ref.shape[1]

    def place(at, number):
        here = pl.ds(at * rows, rows)
        if number == 0:
            return out_ref.at[here]
        return qkv_ref.at[here, pl.ds((number - 1) * width, width)]

    for at in range(pick_ref.shape[0]):
        for source in range(len(parts) - (parts[-1].shape[0] != parts[0].shape[0])):
            @pl.when(pick_ref[at] == source)
            def _():
                for number in range(4):
                    for copy in part_copies(
                        parts, source, first + number * rows, rows, place(at, number),
                        arrived.at[at, number],
                    ):
                        copy.start()
    for at in range(pick_ref.shape[0]):
        for number in range(4):
            pltpu.make_async_copy(
                parts[0].at[pl.ds(0, rows)], place(at, number), arrived.at[at, number]
            ).wait()


def attend_back_kernel(tiles, hp, me_ref, grad_ref, p_ref, qkv_ref, normed_ref, marks_ref, top_ref,
                       out_ref, kept_ref, away_ref, bias_grad, key_grad, value_grad):
    i = pl.program_id(0)
    block, lanes = grad_ref.shape

    @pl.when(i == 0)
    def _():
        bias_grad[...] = jnp.zeros_like(bias_grad)
        key_grad[...] = jnp.zeros_like(key_grad)
        value_grad[...] = jnp.zeros_like(value_grad)

    here = pl.multiple_of(i * block, block)
    query = qkv_ref[pl.ds(here, block), :lanes] * jnp.asarray(HDIM ** -0.5, BF)
    grad = grad_ref[...]
    masks = [head_lanes(block, lanes, h) for h in range(hp)]

    def rows_of(span):
        wide = span * block
        first = pl.multiple_of((i - span + 1) * block, block)
        column = (tiles - span) * block
        key = qkv_ref[pl.ds(first, wide), lanes : 2 * lanes]
        value = qkv_ref[pl.ds(first, wide), 2 * lanes :]
        out = key_part = value_part = None
        for h in range(hp):
            head = jnp.where(masks[h], query, jnp.zeros_like(query))
            head_grad = jnp.where(masks[h], grad, jnp.zeros_like(grad))
            weight = p_ref[0, h, :, column:]
            wide_weight = weight.astype(F32)
            t = wide_weight * dot(head_grad, value, ((1,), (1,)))
            s = t - wide_weight * jnp.sum(t, axis=1, keepdims=True)
            bias_grad[h, :, column:] += s
            s = s.astype(BF)
            part = dot(s, key)
            out = part if out is None else jnp.where(masks[h], part, out)
            part = dot(s, head, ((0,), (0,)))
            key_part = part if key_part is None else key_part + part
            part = dot(weight, head_grad, ((0,), (0,)))
            value_part = part if value_part is None else value_part + part
        key_grad[pl.ds(first, wide), :] += key_part
        value_grad[pl.ds(first, wide), :] += value_part
        out_ref[pl.ds(here, block), :lanes] = (out * HDIM ** -0.5).astype(BF)

    for span in range(1, tiles):
        @pl.when(i == span - 1)
        def _():
            rows_of(span)

    @pl.when(i >= tiles - 1)
    def _():
        rows_of(tiles)

    @pl.when(i == pl.num_programs(0) - 1)
    def _():
        out_ref[:, lanes : 2 * lanes] = key_grad[...].astype(BF)
        out_ref[:, 2 * lanes :] = value_grad[...].astype(BF)
        grad_cols = dot(normed_ref[...], out_ref[...], ((0,), (0,))).astype(BF)
        split_store(kept_ref, away_ref, me_ref[0], grad_cols)
        bins = marks_ref.shape[1]
        wide = 3 * lanes
        notes = []
        for h in range(hp):
            total = jnp.zeros((1, bins), F32)
            for m in range(tiles):
                at = (tiles - 1 - m) * block
                x = bias_grad[h, :, at : at + block]
                x = jnp.concatenate([x, jnp.zeros((block, block), F32)], axis=1)
                half = block // 2
                while half >= 1:
                    x = x[:half] + pltpu.roll(x[half : 2 * half], 2 * block - half, 1)
                    half //= 2
                high, low = halves(x)
                part = marks_ref[m * 2 * block : (m + 1) * 2 * block, :]
                total += dot(high, part) + dot(low, part)
            notes.append(jnp.concatenate([total, jnp.zeros((1, wide - bins), F32)], axis=1))
        spot = lax.broadcasted_iota(jnp.int32, (1, AUX), 1) == me_ref[0]
        for h in range(hp):
            top = top_ref[h : h + 1, :]
            high = top.astype(BF).astype(F32)
            notes.append(
                jnp.concatenate(
                    [jnp.where(spot, high, 0.0), jnp.where(spot, top - high, 0.0)]
                    + [jnp.zeros((1, wide - 2 * AUX), F32)],
                    axis=1,
                )
            )
        notes.append(jnp.zeros((16 - 2 * hp, wide), F32))
        notes = jnp.concatenate(notes, axis=0).astype(BF)
        for ref in (kept_ref, away_ref):
            for at in range(ref.shape[0]):
                ref[at, ref.shape[1] - 16 :] = notes


def attend_back(me, attention_grad, weights, qkv, normed, marks, top, hp, block, spread):
    seq, lanes = attention_grad.shape
    count = seq // block
    width = normed.shape[1]
    tiles = weights.shape[3] // block
    fixed = lambda i: (0, 0)
    pairs = count * tiles * hp * block * block
    owned = (spread // 2, width // spread + 16, 3 * lanes)
    return call(
        lambda *refs: attend_back_kernel(tiles, hp, *refs),
        (struct((seq, 3 * lanes), BF), struct(owned, BF), struct(owned, BF)),
        60e9,
        10 * seq * lanes + 2 * pairs,
        grid=(count,),
        in_specs=[
            pl.BlockSpec(memory_space=pltpu.SMEM),
            pl.BlockSpec((block, lanes), lambda i: (i, 0)),
            pl.BlockSpec((1, hp, block, tiles * block), lambda i: (i, 0, 0, 0)),
            pl.BlockSpec((seq, 3 * lanes), fixed),
            pl.BlockSpec((seq, width), fixed),
            pl.BlockSpec(marks.shape, fixed),
            pl.BlockSpec(top.shape, fixed),
        ],
        out_specs=[pl.BlockSpec((seq, 3 * lanes), fixed)]
        + [pl.BlockSpec(owned, lambda i: (0, 0, 0))] * 2,
        scratch_shapes=[
            pltpu.VMEM((hp, block, tiles * block), F32),
            pltpu.VMEM((seq, lanes), F32),
            pltpu.VMEM((seq, lanes), F32),
        ],
    )(me, attention_grad, weights, qkv, normed, marks, top)


def upstream_kernel(places_ref, other_ref, grad_ref, out_ref):
    experts, capacity, _ = out_ref.shape
    rows = grad_ref.shape[0]
    slots = experts * capacity
    other = other_ref[...]
    slot = lax.broadcasted_iota(jnp.int32, (slots, rows), 0)
    first = jnp.where(slot == places_ref[0:1, :], 1.0, 0.0).astype(BF)
    second = jnp.where(slot == places_ref[1:2, :], 1.0, 0.0).astype(BF)
    sent = dot(first + second, grad_ref[...]).astype(BF)
    named = (dot(first, other[0]) + dot(second, other[1])).astype(BF)
    for at in range(experts):
        here = slice(at * capacity, (at + 1) * capacity)
        out_ref[at, :, 128:] = sent[here]
        out_ref[at, :, :128] = named[here]


def token_front_kernel(spread, me_ref, attn_ref, tok_ref, aux_ref, places_ref, *refs):
    w_refs = refs[:spread]
    attention_ref, resid_ref, normed_ref = refs[spread : spread + 3]
    buffers = refs[spread + 3 : -2]
    whole, arrived = refs[-2:]
    collect(w_refs, me_ref[0], whole, arrived)
    blocks = attn_ref.shape[0]
    attention = jnp.concatenate([attn_ref[at] for at in range(blocks)], axis=1)
    attention_ref[...] = attention
    width = attention.shape[1]
    gain = gain_row(aux_ref[...], 1)
    collected(w_refs, whole, arrived)
    resid = tok_ref[...].astype(F32) + dot(attention, whole[...].reshape(width, width))
    resid_ref[...] = resid
    r = lax.rsqrt(jnp.mean(resid * resid, axis=1, keepdims=True) + EPSILON)
    normed = (resid * r * gain).astype(BF)
    normed_ref[...] = normed
    slots = buffers[0].shape[0]
    slot = lax.broadcasted_iota(jnp.int32, (slots * len(buffers), normed.shape[0]), 0)
    named = (slot == places_ref[2:3, :]) | (slot == places_ref[3:4, :])
    sent = dot(jnp.where(named, 1.0, 0.0).astype(BF), normed).astype(BF)
    for k, buffer in enumerate(buffers):
        buffer[...] = sent[k * slots : (k + 1) * slots]


def token_middle_kernel(returned_ref, resid_ref, normed_ref, aux_ref, ids_ref, grad_ref,
                        mixed_ref, logit_ref, route_ref):
    slots = returned_ref.shape[0]
    rows = resid_ref.shape[0]
    slot = lax.broadcasted_iota(jnp.int32, (rows, slots), 1)
    first = jnp.where(slot == ids_ref[:, 0:1], 1.0, 0.0).astype(BF)
    second = jnp.where(slot == ids_ref[:, 1:2], 1.0, 0.0).astype(BF)
    returned = returned_ref[...]
    first_out = dot(first, returned)
    second_out = dot(second, returned)
    normed = normed_ref[...]
    logits = dot(normed, aux_ref[...])
    lane = lax.broadcasted_iota(jnp.int32, logits.shape, 1) - ROUTER_AT
    at_first = lane == ids_ref[:, 2:3]
    at_second = lane == ids_ref[:, 3:4]
    gap = jnp.sum(
        jnp.where(at_first, logits, 0.0) - jnp.where(at_second, logits, 0.0),
        axis=1, keepdims=True,
    )
    gate_one = 1.0 / (1.0 + jnp.exp(-gap))
    gate_two = 1.0 / (1.0 + jnp.exp(gap))
    mixed_ref[...] = (resid_ref[...] + gate_one * first_out + gate_two * second_out).astype(BF)
    upstream = grad_ref[...].astype(F32)
    change = jnp.sum(upstream * (first_out - second_out), axis=1, keepdims=True)
    slope = gate_one * gate_two * change
    logit = jnp.where(at_first, slope, 0.0) - jnp.where(at_second, slope, 0.0)
    logit_ref[...] = logit
    high, low = halves(logit)
    route_ref[...] = dot(normed, high, ((0,), (0,))) + dot(normed, low, ((0,), (0,)))


def norm_back(values, gain, grad):
    r = lax.rsqrt(jnp.mean(values * values, axis=1, keepdims=True) + EPSILON)
    scaled = grad * gain
    slope = jnp.mean(values * scaled, axis=1, keepdims=True)
    return r * scaled - values * (r * r * r * slope), r


def token_back_kernel(spread, me_ref, logit_ref, aux_ref, ids_ref, resid_ref, grad_ref, back_ref,
                      *refs):
    w_refs = refs[:spread]
    attention_ref, route_ref = refs[spread : spread + 2]
    resid_grad_ref, attention_grad_ref, kept_ref, away_ref, whole, arrived = refs[-6:]
    collect(w_refs, me_ref[0], whole, arrived)
    resid = resid_ref[...]
    rows, width = resid.shape
    slots = back_ref.shape[0]
    slot = lax.broadcasted_iota(jnp.int32, (rows, slots), 1)
    named = (slot == ids_ref[:, 0:1]) | (slot == ids_ref[:, 1:2])
    normed_grad = dot(jnp.where(named, 1.0, 0.0).astype(BF), back_ref[...])
    high, low = halves(logit_ref[...])
    aux = aux_ref[...]
    gain = gain_row(aux, 1)
    normed_grad += dot(high, aux, ((1,), (1,))) + dot(low, aux, ((1,), (1,)))
    part, r = norm_back(resid, gain, normed_grad)
    resid_grad = grad_ref[...].astype(F32) + part
    resid_grad_ref[...] = resid_grad
    gain_grad = jnp.sum(normed_grad * resid * r, axis=0, keepdims=True)
    proj = resid_grad.astype(BF)
    blocks, _, lanes = attention_grad_ref.shape
    collected(w_refs, whole, arrived)
    grad = dot(proj, whole[...].reshape(width, width), ((1,), (1,))).astype(BF)
    for at in range(blocks):
        attention_grad_ref[at] = grad[:, at * lanes : (at + 1) * lanes]
    grad_proj = dot(attention_ref[...], proj, ((0,), (0,))).astype(BF)
    lane = lax.broadcasted_iota(jnp.int32, (width, AUX), 1)
    gain_grad = jnp.broadcast_to(gain_grad, (AUX, width)).T
    small = jnp.where(lane == GAIN_AT, gain_grad, route_ref[...]).astype(BF)
    split_store(kept_ref, away_ref, me_ref[0], jnp.concatenate([grad_proj, small], axis=1))


def token_last_kernel(blocks_ref, w_ref, tok_ref, aux_ref, resid_grad_ref, out_ref, grads, total):
    part = pl.program_id(0)
    blocks, _, wide = blocks_ref.shape
    lanes = wide // 3
    for number in range(3):
        @pl.when(part == number)
        def _():
            for at in range(blocks):
                grads[:, at * lanes : (at + 1) * lanes] = blocks_ref[
                    at, :, number * lanes : (number + 1) * lanes
                ]

    term = dot(grads[...], w_ref[...], ((1,), (1,)))

    @pl.when(part == 0)
    def _():
        total[...] = term

    @pl.when(part > 0)
    def _():
        total[...] += term

    @pl.when(part == 2)
    def _():
        change, _ = norm_back(tok_ref[...].astype(F32), gain_row(aux_ref[...], 0), total[...])
        out_ref[...] = resid_grad_ref[...] + change


def note_row(notes, hp, spread, head):
    lane = lax.broadcasted_iota(jnp.int32, (1, AUX), 1)
    rel = jnp.where(lane < BUCKETS, notes[head : head + 1, :AUX], 0.0)
    tops = notes[hp + head : hp + head + 1]
    high = jnp.where(lane < spread, tops[:, :AUX], 0.0)
    low = jnp.where(lane < spread, tops[:, AUX : 2 * AUX], 0.0)
    return rel, high, low


def join_kernel(hp, spread, own_ref, proj_kept_ref, proj_got_ref, cols_kept_ref, cols_got_ref,
                kept_ref, away_ref):
    rows, wide = proj_kept_ref.shape
    pairs, own_rows, _ = kept_ref.shape
    even = own_ref[0] % 2 == 0
    proj = proj_kept_ref[...].astype(F32) + proj_got_ref[...].astype(F32)
    cols = cols_kept_ref[...].astype(F32) + cols_got_ref[...].astype(F32)
    notes = cols[rows:]
    row = lax.broadcasted_iota(jnp.int32, (own_rows, AUX), 0)
    extra = jnp.zeros((own_rows, AUX), F32)
    for h in range(hp):
        rel, high, low = note_row(notes, hp, spread, h)
        line = pltpu.roll(rel, BIAS_AT, 1) + pltpu.roll(high, TOP_AT, 1)
        line += pltpu.roll(low, TOP_LOW_AT, 1)
        extra += jnp.where(row == h + hp * (own_ref[0] % 2), line, 0.0)
    extra = jnp.concatenate([jnp.zeros((own_rows, wide - AUX), F32), extra], axis=1)
    for pair in range(pairs):
        at = 2 * pair * own_rows
        one, two = slice(at, at + own_rows), slice(at + own_rows, at + 2 * own_rows)
        kept_ref[pair, :, :wide] = (jnp.where(even, proj[one], proj[two]) + extra).astype(BF)
        away_ref[pair, :, :wide] = (jnp.where(even, proj[two], proj[one]) + extra).astype(BF)
        kept_ref[pair, :, wide:] = jnp.where(even, cols[one], cols[two]).astype(BF)
        away_ref[pair, :, wide:] = jnp.where(even, cols[two], cols[one]).astype(BF)


def pair_kernel(wide, own_ref, kept_ref, got_ref, *sends):
    even = own_ref[0] % 2 == 0
    for k, send in enumerate(sends):
        pair = (own_ref[0] // 2) ^ k
        kept, got = kept_ref[pair], got_ref[pair]
        send[:, :wide] = (kept[:, :wide].astype(F32) + got[:, :wide].astype(F32)).astype(BF)
        columns = kept.shape[1] - wide
        send[:, wide : wide + columns] = jnp.where(even, kept[:, wide:], got[:, wide:])
        send[:, wide + columns :] = jnp.where(even, got[:, wide:], kept[:, wide:])


def join_plain(hp, spread, place, groups, proj_terms, cols_terms):
    proj, cols = joined(proj_terms), joined(cols_terms)
    rows, wide = proj.shape
    own_rows = rows // groups
    notes = cols[rows:]
    whole = jnp.concatenate([proj, cols[:rows]], axis=1).reshape(groups, own_rows, -1)
    lines = []
    for h in range(hp):
        rel, high, low = note_row(notes, hp, spread, h)
        line = jnp.roll(rel, BIAS_AT, 1) + jnp.roll(high, TOP_AT, 1) + jnp.roll(low, TOP_LOW_AT, 1)
        lines.append(line)
    extra = jnp.concatenate(lines, axis=0)
    extra = jnp.pad(extra, ((0, own_rows - hp), (wide - AUX, whole.shape[2] - wide)))
    whole = (whole + extra).astype(BF)
    return [
        lax.dynamic_index_in_dim(whole, place ^ k, axis=0, keepdims=False) for k in range(groups)
    ]


def owner_kernel(hp, sharers, spread, own_ref, q_ref, k_ref, v_ref, gain_ref, *refs):
    (proj_ref, route_ref, gain_two_ref, gq_ref, gk_ref, gv_ref, gain_one_ref, rel_ref,
     factor_ref, summary_ref) = refs[-10:]
    blocks = refs[:-10]
    experts = route_ref.shape[0]
    eye = lax.broadcasted_iota(jnp.int32, (proj_ref.shape[0],) * 2, 0)
    eye = eye == lax.broadcasted_iota(jnp.int32, eye.shape, 1)

    def as_row(column):
        return jnp.sum(jnp.where(eye, column, 0.0), axis=0, keepdims=True)

    width = proj_ref.shape[1]
    lanes = hp * HDIM
    sources = (blocks[0].shape[1] - width - AUX) // (3 * lanes)
    total = None
    for block in blocks:
        term = block[:, : width + AUX].astype(F32)
        total = term if total is None else total + term
    proj_ref[...] = total[:, :width]
    small = total[:, width:].T
    route_ref[...] = small[ROUTER_AT : ROUTER_AT + experts]
    gain_two_ref[...] = small[GAIN_AT : GAIN_AT + 1]
    outs = (gq_ref, gk_ref, gv_ref)
    for out in outs:
        out[...] = jnp.zeros_like(out)
    lane = lax.broadcasted_iota(jnp.int32, (1, 128), 1)
    summary_ref[...] = jnp.where(
        lax.broadcasted_iota(jnp.int32, summary_ref.shape, 1) == 64, MASKED, 0.0
    )
    for k, source in [(k, source) for k in range(len(blocks)) for source in range(sources)]:
        block = blocks[k]
        seat = (((own_ref[0] // sources) ^ k) * sources + source) % sharers
        at = pl.multiple_of(seat * lanes, lanes)
        for part, out in enumerate(outs):
            first = width + AUX + (3 * source + part) * lanes
            out[:, pl.ds(at, lanes)] += block[:, first : first + lanes].astype(F32)
        notes = block[:, width : width + AUX].astype(F32)
        for h in range(hp):
            note = notes[source * hp + h : source * hp + h + 1]
            rel = jnp.where(lane < BUCKETS, pltpu.roll(note, AUX - BIAS_AT, 1), 0.0)
            tops = pltpu.roll(note, AUX - TOP_AT, 1) + pltpu.roll(note, AUX - TOP_LOW_AT, 1)
            top = jnp.max(jnp.where(lane < spread, tops, MASKED), axis=1, keepdims=True)
            old = summary_ref[pl.ds(seat * hp + h, 1), :]
            new = jnp.where(lane == 64, jnp.maximum(old, top), old + rel)
            summary_ref[pl.ds(seat * hp + h, 1), :] = new
    rel_ref[...] = summary_ref[:, :BUCKETS]
    factor_ref[...] = jnp.sqrt(CLIP_LEVEL / jnp.maximum(summary_ref[...].T[64:65], 1.0))
    grad = jnp.zeros((proj_ref.shape[0], 1), F32)
    for out, w_ref in zip(outs, (q_ref, k_ref, v_ref)):
        grad += jnp.sum(out[...] * w_ref[...].astype(F32), axis=1, keepdims=True)
    gain_one_ref[...] = as_row(grad) / gain_ref[...]


GELU_A = 0.7978845608028654
GELU_B = 0.044715


def expert_kernel(groups, own_ref, upstream_ref, aux_ref, gate_ref, up_ref, down_ref, *refs):
    blocks = refs[:groups]
    (gate_pre_ref, up_pre_ref, out_ref, rows_ref, slot_grad_ref, grad_down_ref, total) = refs[groups:]
    f = pl.program_id(0)
    capacity, width = blocks[0].shape

    @pl.when(f == 0)
    def _():
        total[...] = jnp.zeros_like(total)
        for k, block in enumerate(blocks):
            rows_ref[k * capacity : (k + 1) * capacity, :] = block[...]
        all_logits = dot(rows_ref[...], aux_ref[...])
        for k in range(groups):
            here = slice(k * capacity, (k + 1) * capacity)
            logits = all_logits[here]
            lane = lax.broadcasted_iota(jnp.int32, logits.shape, 1) - ROUTER_AT
            upstream = upstream_ref[own_ref[0] ^ k]
            other = upstream[:, 0:1].astype(F32).astype(jnp.int32)
            gap = jnp.sum(
                jnp.where(lane == other, logits, 0.0) - jnp.where(lane == own_ref[0], logits, 0.0),
                axis=1, keepdims=True,
            )
            gate = 1.0 / (1.0 + jnp.exp(gap))
            slot_grad_ref[here, :] = (gate * upstream[:, 128:].astype(F32)).astype(BF)

    rows = rows_ref[...]
    gate_pre = dot(rows, gate_ref[...])
    up_pre = dot(rows, up_ref[...])
    gate_pre_ref[...] = gate_pre
    up_pre_ref[...] = up_pre
    inner = jnp.tanh(GELU_A * (gate_pre + GELU_B * gate_pre * gate_pre * gate_pre))
    hidden = (0.5 * gate_pre * (1.0 + inner) * up_pre).astype(BF)
    total[...] += dot(hidden, down_ref[...])
    grad_down_ref[...] = dot(hidden, slot_grad_ref[...], ((0,), (0,))).astype(BF)

    @pl.when(f == pl.num_programs(0) - 1)
    def _():
        for k in range(groups):
            out_ref[own_ref[0] ^ k] = total[k * capacity : (k + 1) * capacity, :].astype(BF)


def expert_forward(own, upstream, aux, blocks, gate, up, down, tile):
    groups = len(blocks)
    capacity, width = blocks[0].shape
    count = groups * capacity
    ff = gate.shape[1]
    fixed = lambda f: (0, 0)
    cols = lambda f: (0, f)
    return call(
        lambda *refs: expert_kernel(groups, *refs),
        (
            struct((count, ff), F32),
            struct((count, ff), F32),
            struct((groups, capacity, width), BF),
            struct((count, width), BF),
            struct((count, width), BF),
            struct((ff, width), BF),
        ),
        24e9,
        6 * width * ff + 10 * count * ff,
        grid=(ff // tile,),
        in_specs=[
            pl.BlockSpec(memory_space=pltpu.SMEM),
            pl.BlockSpec(upstream.shape, lambda f: (0, 0, 0)),
            pl.BlockSpec(aux.shape, fixed),
            pl.BlockSpec((width, tile), cols),
            pl.BlockSpec((width, tile), cols),
            pl.BlockSpec((tile, width), lambda f: (f, 0)),
        ]
        + [pl.BlockSpec((capacity, width), fixed)] * groups,
        out_specs=[
            pl.BlockSpec((count, tile), cols),
            pl.BlockSpec((count, tile), cols),
            pl.BlockSpec((groups, capacity, width), lambda f: (0, 0, 0)),
            pl.BlockSpec((count, width), fixed),
            pl.BlockSpec((count, width), fixed),
            pl.BlockSpec((tile, width), lambda f: (f, 0)),
        ],
        scratch_shapes=[pltpu.VMEM((count, width), F32)],
    )(own, upstream, aux, gate, up, down, *blocks)


def split_store(kept_ref, away_ref, me, values):
    rows = values.shape[0] // (2 * kept_ref.shape[0])
    for d in range(2 * kept_ref.shape[0]):
        block = values[d * rows : (d + 1) * rows]
        @pl.when(me % 2 == d % 2)
        def _():
            kept_ref[d // 2, :rows] = block

        @pl.when(me % 2 != d % 2)
        def _():
            away_ref[d // 2, :rows] = block


def expert_back_kernel(own_ref, me_ref, slot_grad_ref, rows_ref, gate_pre_ref, up_pre_ref, down_ref,
                       gate_ref, up_ref, row_grad_ref, grad_gate_ref, up_kept_ref, up_away_ref,
                       total, pre_grads, split_rows):
    f = pl.program_id(0)
    tiles = pl.num_programs(0) - 1
    tile = gate_ref.shape[1]
    groups, capacity, _ = row_grad_ref.shape

    def through_gelu(slot):
        hidden_grad = dot(slot_grad_ref[...], down_ref[...], ((1,), (1,)))
        v = gate_pre_ref[...]
        square = v * v
        inner = jnp.tanh(v * (GELU_A + GELU_A * GELU_B * square))
        half = 0.5 + 0.5 * inner
        slope = half + (0.5 * v) * (1.0 - inner * inner) * (
            GELU_A + 3.0 * GELU_A * GELU_B * square
        )
        pre_grads[slot, :, :tile] = (hidden_grad * up_pre_ref[...] * slope).astype(BF)
        pre_grads[slot, :, tile:] = (hidden_grad * (v * half)).astype(BF)

    def to_weights(slot):
        both = pre_grads[slot]
        weights = jnp.concatenate([gate_ref[...], up_ref[...]], axis=1)
        total[...] += dot(both, weights, ((1,), (1,)))
        grad_gate_ref[...] = dot(rows_ref[...], both[:, :tile], ((0,), (0,))).astype(BF)
        grads = dot(split_rows[...], both[:, tile:], ((0,), (0,))).astype(BF)
        half = grads.shape[0] // 2
        up_kept_ref[...] = grads[:half].reshape(up_kept_ref.shape)
        up_away_ref[...] = grads[half:].reshape(up_kept_ref.shape)

    @pl.when(f == 0)
    def _():
        total[...] = jnp.zeros_like(total)
        part = up_kept_ref.shape[1]
        half = rows_ref.shape[1] // 2
        even = me_ref[0] % 2 == 0
        for pair in range(up_kept_ref.shape[0]):
            one = rows_ref[:, 2 * pair * part : (2 * pair + 1) * part]
            two = rows_ref[:, (2 * pair + 1) * part : (2 * pair + 2) * part]
            at = pair * part
            split_rows[:, at : at + part] = jnp.where(even, one, two)
            split_rows[:, half + at : half + at + part] = jnp.where(even, two, one)
        through_gelu(0)

    @pl.when((f > 0) & (f < tiles))
    def _():
        to_weights((f - 1) % 2)
        through_gelu(f % 2)

    @pl.when(f == tiles)
    def _():
        to_weights((f - 1) % 2)
        for k in range(groups):
            row_grad_ref[own_ref[0] ^ k] = total[k * capacity : (k + 1) * capacity, :].astype(BF)


def expert_backward(own, me, slot_grad, rows, gate_pre, up_pre, gate, up, down, tile, groups,
                    spread):
    count, width = rows.shape
    ff = gate.shape[1]
    tiles = ff // tile
    fixed = lambda f: (0, 0)
    now = lambda f: (0, jnp.minimum(f, tiles - 1))
    before = lambda f: (0, jnp.maximum(f - 1, 0))
    owned = (spread // 2, width // spread)
    return call(
        expert_back_kernel,
        [
            struct((groups, count // groups, width), BF),
            struct((width, ff), BF),
        ]
        + [struct(owned + (ff,), BF)] * 2,
        30e9,
        12 * width * ff + 10 * count * ff,
        grid=(tiles + 1,),
        in_specs=[
            pl.BlockSpec(memory_space=pltpu.SMEM),
            pl.BlockSpec(memory_space=pltpu.SMEM),
            pl.BlockSpec((count, width), fixed),
            pl.BlockSpec((count, width), fixed),
            pl.BlockSpec((count, tile), now),
            pl.BlockSpec((count, tile), now),
            pl.BlockSpec((tile, width), lambda f: (jnp.minimum(f, tiles - 1), 0)),
            pl.BlockSpec((width, tile), before),
            pl.BlockSpec((width, tile), before),
        ],
        out_specs=[
            pl.BlockSpec((groups, count // groups, width), lambda f: (0, 0, 0)),
            pl.BlockSpec((width, tile), before),
        ]
        + [pl.BlockSpec(owned + (tile,), lambda f: (0, 0, jnp.maximum(f - 1, 0)))] * 2,
        scratch_shapes=[
            pltpu.VMEM((count, width), F32),
            pltpu.VMEM((2, count, 2 * tile), BF),
            pltpu.VMEM((count, width), BF),
        ],
    )(own, me, slot_grad, rows, gate_pre, up_pre, down, gate, up)


def slot_places(routes, experts, capacity):
    chosen = (routes[:, :, None] == jnp.arange(experts, dtype=jnp.int32)[None, None, :]).astype(
        jnp.int32
    )
    order = jnp.swapaxes(chosen, 0, 1).reshape(-1, experts)
    before = jnp.cumsum(order, axis=0) - order
    slots = jnp.sum(before * order, axis=1).reshape(TOP, -1).T
    return routes * capacity + slots


def flip(values, axis, mask):
    n = lax.axis_size(axis)
    return lax.ppermute(values, axis, [(k, k ^ mask) for k in range(n)])


def gather_parts(part, axis):
    return gather_rest({0: part}, axis, lax.axis_size(axis) // 2)


def gather_rest(held, axis, bit):
    while bit >= 1:
        held.update({j ^ bit: flip(values, axis, bit) for j, values in list(held.items())})
        bit //= 2
    return [held[j] for j in range(len(held))]


def swap_parts(parts, axis):
    return [parts[0]] + [flip(parts[k], axis, k) for k in range(1, len(parts))]


def ring_parts(tokens, before, between):
    devices = lax.axis_size("expert")
    line = list(range(0, devices, 2)) + list(range(devices - 1, 0, -2))
    spots = [line.index(k) for k in range(devices)]

    def move(values, step):
        pairs = [(line[k], line[(k + step) % devices]) for k in range(devices)]
        return lax.ppermute(values, "expert", pairs)

    ahead = [tokens]
    behind = [tokens]
    half = devices // 2
    for k in range(1, half):
        pair = (move(ahead[-1], 1), move(behind[-1], -1))
        if k == half - 2:
            *pair, first = lax.optimization_barrier((*pair, before[0]))
            before = (between(first),) + before[1:]
        elif k == half - 1:
            *pair, before = lax.optimization_barrier((*pair, before))
        else:
            pair = lax.optimization_barrier(pair)
        ahead.append(pair[0])
        behind.append(pair[1])
    cut = tokens.shape[0] // 2
    farthest = (move(ahead[-1][:cut], 1), move(behind[-1][cut:], -1))
    parts = ahead + behind[:0:-1] + list(farthest)
    spot = jnp.asarray(spots, jnp.int32)
    mine = jnp.sum(jnp.where(jnp.arange(devices) == lax.axis_index("expert"), spot, 0))
    gap = (mine - spot) % devices
    gap = jnp.where(gap == half, devices - 1, jnp.where(gap > half, gap - 1, gap))
    return gap.astype(jnp.int32), parts, before


def scatter_step(parts, axis, me, bit):
    pairs = parts.reshape((parts.shape[0] // 2, 2) + parts.shape[1:])
    mine = (me // bit) % 2
    away = lax.dynamic_index_in_dim(pairs, 1 - mine, axis=1, keepdims=False)
    kept = lax.dynamic_index_in_dim(pairs, mine, axis=1, keepdims=False)
    return kept, flip(away, axis, bit)


def joined(parts):
    return parts[0].astype(F32) + parts[1].astype(F32)


def scatter_rest(parts, axis):
    n = lax.axis_size(axis)
    me = lax.axis_index(axis)
    bit = 2
    while True:
        terms = scatter_step(parts, axis, me, bit)
        bit *= 2
        if bit >= n:
            return tuple(term[0] for term in terms)
        parts = joined(terms).astype(BF)


def body(tokens, gain_attn, w_query, w_key, w_value, w_output, rel_bias, gain_ffn, w_router,
         expert_gate, expert_up, expert_down, routes, doc_lengths, seq_valid, grad_output):
    length, width = tokens.shape
    groups = lax.axis_size("expert")
    spread = lax.axis_size("dp")
    place = lax.axis_index("expert")
    device = lax.axis_index("dp") * groups + place
    experts = w_router.shape[1]
    capacity = 5 * TOP * length // (4 * experts)
    slots = experts * capacity
    sharers = SEQ // length
    hp = HEADS // sharers
    lanes = hp * HDIM
    own_rows = w_query.shape[0]
    teams = None
    if groups != sharers:
        teams = [list(range(at, at + sharers)) for at in range(0, groups, sharers)]
    both = ("dp", "expert")

    def exchange(blocks):
        return lax.all_to_all(blocks, "expert", 0, 0, axis_index_groups=teams, tiled=True)

    def exchange_all(blocks):
        return lax.all_to_all(blocks, "expert", 0, 0, tiled=True)

    def columns(w):
        return w.reshape(own_rows, sharers, lanes).swapaxes(0, 1)

    extra = jnp.concatenate([gain_attn[:, None], gain_ffn[:, None], w_router], axis=1)
    extra = jnp.pad(extra, ((0, 0), (0, AUX - extra.shape[1])))
    sent = jnp.concatenate(
        [
            columns(w_query),
            columns(w_key),
            columns(w_value),
            jnp.broadcast_to(extra[None], (sharers, own_rows, AUX)),
        ],
        axis=2,
    )
    sent = jnp.tile(sent, (groups // sharers, 1, 1))
    gate_all = lax.all_gather(expert_gate[0], "dp", axis=0, tiled=True)
    up_all = lax.all_gather(expert_up[0], "dp", axis=0, tiled=True)
    down_all = lax.all_gather(expert_down[0], "dp", axis=0, tiled=True)

    places = slot_places(routes, experts, capacity)
    near_places = places + ((routes ^ place) - routes) * capacity
    ids = jnp.concatenate([places, routes, near_places], axis=1)
    ids = jnp.pad(ids, ((0, 0), (0, 128 - ids.shape[1])))
    places_row = jnp.pad(
        jnp.concatenate([places, near_places], axis=1).T, ((0, 4), (0, 0)), constant_values=-1
    )
    other = jnp.broadcast_to(routes.T[::-1, :, None], (TOP, length, 128)).astype(BF)
    upstream = call(
        upstream_kernel,
        struct((experts, capacity, width + 128), BF),
        3e9,
        4 * slots * width,
    )(places_row, other, grad_output)

    number = (device * length) // SEQ
    ends = jnp.cumsum(lax.dynamic_index_in_dim(doc_lengths, number, keepdims=False))
    ends = jnp.concatenate([ends, lax.dynamic_index_in_dim(seq_valid, number)]).astype(jnp.int32)
    block = length
    marks, inside = diagonal_tables(block, WINDOW, BUCKETS)
    head_at = (place % sharers) * hp
    own_bias = lax.dynamic_slice_in_dim(rel_bias, head_at, hp, axis=1)
    diag = jnp.dot(jnp.asarray(marks), own_bias, precision=lax.Precision.HIGHEST)
    diag = jnp.where(jnp.asarray(inside)[:, None], diag, MASKED)
    tiles = WINDOW // block + 1
    diag = diag.T.reshape(hp * tiles, 2 * block)
    packed = exchange_all(sent).reshape(groups * own_rows, 3 * lanes + AUX)
    mixed_rows = jnp.concatenate([tokens, w_output, w_query, w_key, w_value], axis=0)
    if teams is None:
        def between(values):
            return gather_parts(values, "dp")

        before = (packed, upstream, diag, ends, ids)
        pick, parts, before = ring_parts(mixed_rows, before, between)
        packed, upstream, diag, ends, ids = before
    else:
        whole = lax.all_gather(mixed_rows, "expert", axis=0, axis_index_groups=teams)
        pick = jnp.arange(sharers, dtype=jnp.int32)
        parts = [whole[at] for at in range(sharers)]
        packed = gather_parts(packed, "dp")
    me = lax.axis_index("dp").astype(jnp.int32).reshape(1)
    if teams is None:
        output_rows, qkv_rows = call(
            lambda *refs: output_rows_kernel(len(parts), length, own_rows, *refs),
            (struct((groups * own_rows, width), BF), struct((groups * own_rows, 3 * width), BF)),
            1e9,
            16 * groups * own_rows * width,
            in_specs=[pl.BlockSpec(memory_space=pltpu.SMEM)]
            + [pl.BlockSpec(memory_space=pl.ANY)] * len(parts),
            out_specs=[pl.BlockSpec(memory_space=pltpu.VMEM)] * 2,
            scratch_shapes=[pltpu.SemaphoreType.DMA((sharers, 4))],
        )(pick, *parts)
        output_rows, attend_parts = lax.optimization_barrier((output_rows, parts))
    else:
        output_rows = lax.all_gather(w_output, "expert", axis=0, tiled=True)
        qkv_rows = jnp.concatenate([w_query, w_key, w_value], axis=1)
        qkv_rows = lax.all_gather(qkv_rows, "expert", axis=0, tiled=True)
        attend_parts = parts
    output_parts = {0: output_rows, spread // 2: flip(output_rows, "dp", spread // 2)}

    upstream, _ = lax.optimization_barrier((upstream, parts))
    upstream = exchange_all(upstream)

    normed_one, qkv, weights, attn, top, aux = attend(
        pick, me, attend_parts, packed, diag, ends, hp, block
    )
    attn, upstream, output_parts = lax.optimization_barrier((attn, upstream, output_parts))
    output_parts = gather_rest(output_parts, "dp", spread // 4)
    attn_blocks = exchange(attn.reshape(sharers, length, lanes))

    vmem = pl.BlockSpec(memory_space=pltpu.VMEM)
    smem = pl.BlockSpec(memory_space=pltpu.SMEM)
    loose = pl.BlockSpec(memory_space=pl.ANY)
    gathered = [
        pltpu.VMEM((spread,) + output_parts[0].shape, BF),
        pltpu.SemaphoreType.DMA((spread,)),
    ]
    attention, resid, normed_two, *buffers = call(
        lambda *refs: token_front_kernel(spread, *refs),
        [
            struct((length, width), BF),
            struct((length, width), F32),
            struct((length, width), BF),
        ]
        + [struct((capacity, width), BF)] * groups,
        5e9,
        2 * width * width + 8 * length * width,
        in_specs=[smem] + [vmem] * 4 + [loose] * spread,
        scratch_shapes=gathered,
    )(me, attn_blocks, tokens, aux, places_row, *output_parts)
    rows = swap_parts(buffers, "expert")
    qkv_rows, _ = lax.optimization_barrier((qkv_rows, attn))
    qkv_all = lax.all_gather(qkv_rows, "dp", axis=0, tiled=True)

    tile = 256 if expert_gate.shape[2] % 256 == 0 else 128
    own = place.astype(jnp.int32).reshape(1)
    gate_pre, up_pre, expert_out, rows, slot_grad, grad_down = expert_forward(
        own, upstream, aux, rows, gate_all, up_all, down_all, tile
    )
    expert_out, qkv_all = lax.optimization_barrier((expert_out, qkv_all))
    returned = exchange_all(expert_out)
    row_grad, *expert_grads = expert_backward(
        own, me, slot_grad, rows, gate_pre, up_pre, gate_all, up_all, down_all, tile, groups,
        spread,
    )
    returned, row_grad, expert_grads = lax.optimization_barrier(
        (returned, row_grad, expert_grads)
    )
    grad_gate, up_kept, up_away = expert_grads
    up_first = joined((up_kept, flip(up_away, "dp", 1))).astype(BF)
    owned_down = lax.psum_scatter(grad_down, "dp", scatter_dimension=0, tiled=True)
    returned = returned.reshape(slots, width)
    back = exchange_all(row_grad)
    mixed, logit_grad, route_grad = call(
        token_middle_kernel,
        (
            struct((length, width), BF),
            struct((length, 128), F32),
            struct((width, 128), F32),
        ),
        5e9,
        2 * slots * width + 8 * length * width,
    )(returned, resid, normed_two, aux, ids, grad_output)
    back, owned_down = lax.optimization_barrier((back, owned_down))
    owned_down = owned_down.astype(F32)
    back = back.reshape(slots, width)
    cores = [list(range(core, spread, 2)) for core in range(2)]

    def scatter_chips(parts):
        parts = parts.reshape((-1,) + parts.shape[2:])
        return lax.psum_scatter(
            parts, "dp", scatter_dimension=0, axis_index_groups=cores, tiled=True
        )

    owned_gate = lax.psum_scatter(grad_gate, "dp", scatter_dimension=0, tiled=True)
    owned_up = scatter_chips(up_first)
    resid_grad, attention_grad, proj_kept, proj_away = call(
        lambda *refs: token_back_kernel(spread, *refs),
        (
            struct((length, width), F32),
            struct((sharers, length, lanes), BF),
            struct((spread // 2, width // spread, width + AUX), BF),
            struct((spread // 2, width // spread, width + AUX), BF),
        ),
        6e9,
        2 * width * width + 2 * slots * width + 8 * length * width,
        in_specs=[smem] + [vmem] * 6 + [loose] * spread + [vmem] * 2,
        scratch_shapes=gathered,
    )(me, logit_grad, aux, ids, resid, grad_output, back, *output_parts, attention, route_grad)
    attention_grad = exchange(attention_grad).reshape(SEQ, lanes)
    proj_first = proj_kept.astype(F32) + flip(proj_away, "dp", 1).astype(F32)
    attention_grad, proj_first, _ = lax.optimization_barrier(
        (attention_grad, proj_first.astype(BF), up_first)
    )
    proj_terms = scatter_rest(proj_first, "dp")

    grad_qkv_rows, cols_kept, cols_away = attend_back(
        me, attention_grad, weights, qkv, normed_one, jnp.asarray(marks, BF), top, hp, block, spread
    )
    grad_qkv_rows, cols_away, proj_terms, owned_gate = lax.optimization_barrier(
        (grad_qkv_rows, cols_away, proj_terms, owned_gate)
    )
    grads_here = exchange(grad_qkv_rows.reshape(sharers, length, 3 * lanes))
    owned_gate = owned_gate.astype(F32)
    fixed = lambda part: (0, 0)
    grad_tokens = call(
        token_last_kernel,
        struct((length, width), F32),
        60e9,
        6 * width * width + 12 * length * width,
        grid=(3,),
        mib=24, in_specs=[
            pl.BlockSpec(grads_here.shape, lambda part: (0, 0, 0)),
            pl.BlockSpec((width, width), lambda part: (0, part)),
            pl.BlockSpec((length, width), fixed),
            pl.BlockSpec(aux.shape, fixed),
            pl.BlockSpec((length, width), fixed),
        ],
        out_specs=pl.BlockSpec((length, width), fixed),
        scratch_shapes=[pltpu.VMEM((length, width), BF), pltpu.VMEM((length, width), F32)],
    )(grads_here, qkv_all, tokens, aux, resid_grad)

    cols_first = cols_kept.astype(F32) + flip(cols_away, "dp", 1).astype(F32)
    cols_terms = scatter_rest(cols_first.astype(BF), "dp")
    if own_rows % 16 == 0:
        pairs = groups // 2
        blocks = struct((pairs, own_rows, width + AUX + 3 * lanes), BF)
        pairs_kept, pairs_away = call(
            lambda *refs: join_kernel(hp, spread, *refs),
            [blocks] * 2,
            1e9,
            8 * groups * own_rows * width,
            mib=12, in_specs=[smem] + [vmem] * 4,
        )(own, *proj_terms, *cols_terms)
        sends = call(
            lambda *refs: pair_kernel(width + AUX, *refs),
            [struct((own_rows, width + AUX + 6 * lanes), BF)] * pairs,
            1e9,
            8 * groups * own_rows * width,
            mib=12, in_specs=[smem] + [vmem] * 2,
        )(own, pairs_kept, flip(pairs_away, "expert", 1))
        owned = [sends[0]] + [flip(sends[k], "expert", 2 * k) for k in range(1, pairs)]
    else:
        sends = join_plain(hp, spread, place, groups, proj_terms, cols_terms)
        owned = swap_parts(sends, "expert")
    grad_tokens, owned_up = lax.optimization_barrier((grad_tokens, owned_up))
    owned_up = owned_up.astype(F32)
    *owned, grad_tokens = lax.optimization_barrier((*owned, grad_tokens))
    grad_proj, route, gain_two, grad_q, grad_k, grad_v, gain_one, rel, factor = call(
        lambda *refs: owner_kernel(hp, sharers, spread, *refs),
        (
            struct((own_rows, width), F32),
            struct((experts, own_rows), F32),
            struct((1, own_rows), F32),
            struct((own_rows, width), F32),
            struct((own_rows, width), F32),
            struct((own_rows, width), F32),
            struct((1, own_rows), F32),
            struct((HEADS, BUCKETS), F32),
            struct((1, HEADS), F32),
        ),
        2e9,
        8 * own_rows * width,
        mib=12, in_specs=[smem] + [vmem] * (4 + len(owned)),
        scratch_shapes=[pltpu.VMEM((HEADS, 128), F32)],
    )(own, w_query, w_key, w_value, gain_attn.astype(F32)[None], *owned)
    return (
        mixed,
        grad_tokens,
        gain_one[0],
        grad_q,
        grad_k,
        grad_v,
        grad_proj,
        rel.T,
        gain_two[0],
        route.T,
        owned_gate[None],
        owned_up[None],
        owned_down[None],
        factor[0],
    )


def solution(mesh):
    rows = P(("dp", "expert"), None)
    vector = P(("dp", "expert"))
    expert = P("expert", "dp", None)
    return jax.shard_map(
        body,
        mesh=mesh,
        in_specs=(
            rows, vector, rows, rows, rows, rows, P(), vector, rows,
            expert, expert, expert, rows, P(), P(), rows,
        ),
        out_specs=(
            rows, rows, vector, rows, rows, rows, rows, P(), vector, rows,
            expert, expert, expert, P(),
        ),
        check_vma=False,
    )
```

```python
import jax
import jax.numpy as jnp
import numpy as np
from jax import lax
from jax.experimental import pallas as pl
from jax.experimental.pallas import tpu as pltpu
from jax.sharding import PartitionSpec as P

HEADS = 16
HDIM = 64
BUCKETS = 32
WINDOW = 1024
SEQ = 2048
DOCS = 4
TOP = 2

EPSILON = 1e-06
CLIP_LEVEL = 4.0
BF = jnp.bfloat16
F32 = jnp.float32
MASKED = -1e30
AUX = 128
ROUTER_AT = 2
GAIN_AT = 63
BIAS_AT = 64
TOP_AT = 96
TOP_LOW_AT = 112


def dot(left, right, dims=((1,), (0,))):
    return lax.dot_general(left, right, (dims, ((), ())), preferred_element_type=F32)


def halves(values):
    high = values.astype(BF)
    return high, (values - high.astype(F32)).astype(BF)


def call(kernel, out_shape, flops, nbytes, mib=56, **kwargs):
    return pl.pallas_call(
        kernel,
        out_shape=out_shape,
        compiler_params=pltpu.CompilerParams(vmem_limit_bytes=mib * 1024 * 1024),
        cost_estimate=pl.CostEstimate(
            flops=int(flops), bytes_accessed=int(nbytes), transcendentals=0
        ),
        **kwargs,
    )


def struct(shape, dtype):
    return jax.ShapeDtypeStruct(shape, dtype)


def bucket_of(span, buckets):
    distance = np.arange(span) * 1.0
    exact = buckets // 2
    safe = np.maximum(distance, 1.0)
    spread = exact + np.floor(np.log(safe / exact) / np.log(128.0 / exact) * (buckets - exact))
    return np.where(distance < exact, distance, np.minimum(spread, buckets - 1.0)).astype(np.int64)


def diagonal_tables(block, window, buckets):
    tiles = window // block + 1
    j = np.arange(2 * block)
    offset = np.where(j < block, -j, 2 * block - j)
    distance = np.arange(tiles)[:, None] * block + offset[None, :]
    inside = (distance >= 0) & (distance < window) & (j != block)[None, :]
    bucket = bucket_of(window, buckets)[np.clip(distance, 0, window - 1)]
    marks = (bucket[..., None] == np.arange(buckets)) & inside[..., None]
    return marks.astype(np.float32).reshape(-1, buckets), inside.reshape(-1)


def collect(parts, me, whole, arrived):
    for j, part in enumerate(parts):
        pltpu.make_async_copy(part, whole.at[me ^ j], arrived.at[j]).start()


def collected(parts, whole, arrived):
    for j, part in enumerate(parts):
        pltpu.make_async_copy(part, whole.at[0], arrived.at[j]).wait()


def part_copies(parts, source, first, rows, to, semaphore):
    cut = parts[-1].shape[0]
    if cut == parts[0].shape[0] or source < len(parts) - 2:
        return [pltpu.make_async_copy(parts[source].at[pl.ds(first, rows)], to, semaphore)]
    copies = []
    low = max(0, min(rows, cut - first))
    if low:
        copies.append(
            pltpu.make_async_copy(
                parts[source].at[pl.ds(first, low)], to.at[pl.ds(0, low)], semaphore
            )
        )
    if low < rows:
        copies.append(
            pltpu.make_async_copy(
                parts[source + 1].at[pl.ds(first + low - cut, rows - low)],
                to.at[pl.ds(low, rows - low)],
                semaphore,
            )
        )
    return copies


def gain_row(aux, at):
    rows = lax.broadcasted_iota(jnp.int32, (8, AUX), 0)
    lanes = lax.broadcasted_iota(jnp.int32, (8, AUX), 1)
    pick = jnp.where((rows == 0) & (lanes == at), 1.0, 0.0).astype(BF)
    return dot(pick, aux, ((1,), (1,)))[0:1]


def head_lanes(rows, lanes, head):
    lane = lax.broadcasted_iota(jnp.int32, (rows, lanes), 1)
    return lane // HDIM == head


def fold(values, combine):
    parts = [values[:, at : at + 128] for at in range(0, values.shape[1], 128)]
    total = parts[0]
    for part in parts[1:]:
        total = combine(total, part)
    return total


def attend_kernel(tiles, hp, sources, spread, pick_ref, me_ref, *refs):
    tok_refs = refs[:sources]
    w_refs = refs[sources : sources + spread]
    (diag_ref, ends_ref, normed_ref, qkv_ref, p_ref, out_ref, top_ref, aux_ref,
     bias, keys, values, tok, arrived, packed, w_arrived, gain) = refs[sources + spread :]
    i = pl.program_id(0)
    block, lanes = out_ref.shape
    width = normed_ref.shape[1]

    @pl.when(i == 0)
    def _():
        collect(w_refs, me_ref[0], packed, w_arrived)
        for at in range(tok.shape[0]):
            for source in range(sources - (tok_refs[-1].shape[0] != tok_refs[0].shape[0])):
                @pl.when(pick_ref[at] == source)
                def _():
                    for copy in part_copies(
                        tok_refs, source, 0, block, tok.at[at], arrived.at[at]
                    ):
                        copy.start()
        for h in range(hp):
            for m in range(tiles):
                at = h * tiles + m
                row = jnp.broadcast_to(diag_ref[at : at + 1, :], (block, 2 * block))
                at = (tiles - 1 - m) * block
                bias[h, :, at : at + block] = pltpu.roll(
                    row, 0, 1, stride=1, stride_axis=0
                )[:, :block]
        top_ref[...] = jnp.full_like(top_ref, MASKED)
        collected(w_refs, packed, w_arrived)
        aux_ref[...] = packed[:, :, 3 * lanes :].reshape(width, AUX)
        gain[...] = gain_row(aux_ref[...], 0)

    pltpu.make_async_copy(tok_refs[0].at[pl.ds(0, block)], tok.at[i], arrived.at[i]).wait()
    x = tok[i].astype(F32)
    r = lax.rsqrt(jnp.mean(x * x, axis=1, keepdims=True) + EPSILON)
    normed = (x * r * gain[...]).astype(BF)
    normed_ref[...] = normed
    w_cols = packed[:, :, : 3 * lanes].reshape(width, 3 * lanes)
    qkv = dot(normed, w_cols).astype(BF)
    qkv_ref[...] = qkv
    here = pl.multiple_of(i * block, block)
    keys[pl.ds(here, block), :] = qkv[:, lanes : 2 * lanes]
    values[pl.ds(here, block), :] = qkv[:, 2 * lanes :]
    query = qkv[:, :lanes] * jnp.asarray(HDIM ** -0.5, BF)
    masks = [head_lanes(block, lanes, h) for h in range(hp)]
    heads = [jnp.where(masks[h], query, jnp.zeros_like(query)) for h in range(hp)]

    def label_of(positions):
        label = jnp.zeros(positions.shape, jnp.int32)
        for at in range(DOCS):
            label += jnp.where(positions >= ends_ref[at], 1, 0)
        return label

    qlab = label_of(lax.broadcasted_iota(jnp.int32, (block, 1), 0) + i * block)

    def rows_of(span):
        wide = span * block
        first = pl.multiple_of((i - span + 1) * block, block)
        column = (tiles - span) * block
        key = keys[pl.ds(first, wide), :]
        value = values[pl.ds(first, wide), :]
        position = lax.broadcasted_iota(jnp.int32, (1, wide), 1) + first
        same = qlab == jnp.where(position < ends_ref[DOCS], label_of(position), -1)
        row = lax.broadcasted_iota(jnp.int32, (block, block), 0)
        diagonal = row == lax.broadcasted_iota(jnp.int32, (block, block), 1)
        out = None
        for h in range(hp):
            s = dot(heads[h], key, ((1,), (1,))) + bias[h, :, column:]
            last = wide - block
            own = jnp.where(same[:, last:] | diagonal, s[:, last:], MASKED)
            if span > 1:
                own = jnp.concatenate([jnp.where(same[:, :last], s[:, :last], MASKED), own], axis=1)
            best = jnp.max(own, axis=1, keepdims=True)
            top_ref[h : h + 1, :] = jnp.maximum(
                top_ref[h : h + 1, :], jnp.max(best, axis=0, keepdims=True)
            )
            p = jnp.exp(own - best)
            p = (p * (1.0 / jnp.sum(p, axis=1, keepdims=True))).astype(BF)
            p_ref[0, h, :, column:] = p
            part = dot(p, value)
            out = part if out is None else jnp.where(masks[h], part, out)
        out_ref[...] = out.astype(BF)

    for span in range(1, tiles):
        @pl.when(i == span - 1)
        def _():
            rows_of(span)

    @pl.when(i >= tiles - 1)
    def _():
        rows_of(tiles)


def attend(pick, me, parts, packed, diag, ends, hp, block):
    width = parts[0].shape[1]
    count = pick.shape[0]
    seq = count * block
    lanes = hp * HDIM
    tiles = diag.shape[0] // hp
    row = lambda i: (i, 0)
    fixed = lambda i: (0, 0)
    pairs = count * tiles * hp * block * block
    return call(
        lambda *refs: attend_kernel(tiles, hp, len(parts), len(packed), *refs),
        (
            struct((seq, width), BF),
            struct((seq, 3 * lanes), BF),
            struct((count, hp, block, tiles * block), BF),
            struct((seq, lanes), BF),
            struct((8, 128), F32),
            struct((width, AUX), BF),
        ),
        24e9,
        8 * seq * width + 2 * pairs,
        grid=(count,),
        in_specs=[pl.BlockSpec(memory_space=pltpu.SMEM)] * 2
        + [pl.BlockSpec(memory_space=pl.ANY)] * (len(parts) + len(packed))
        + [
            pl.BlockSpec(diag.shape, fixed),
            pl.BlockSpec(memory_space=pltpu.SMEM),
        ],
        out_specs=[
            pl.BlockSpec((block, width), row),
            pl.BlockSpec((block, 3 * lanes), row),
            pl.BlockSpec((1, hp, block, tiles * block), lambda i: (i, 0, 0, 0)),
            pl.BlockSpec((block, lanes), row),
            pl.BlockSpec((8, 128), fixed),
            pl.BlockSpec((width, AUX), fixed),
        ],
        scratch_shapes=[
            pltpu.VMEM((hp, block, tiles * block), F32),
            pltpu.VMEM((seq, lanes), BF),
            pltpu.VMEM((seq, lanes), BF),
            pltpu.VMEM((count, block, width), BF),
            pltpu.SemaphoreType.DMA((count,)),
            pltpu.VMEM((len(packed),) + packed[0].shape, BF),
            pltpu.SemaphoreType.DMA((len(packed),)),
            pltpu.VMEM((1, width), F32),
        ],
    )(pick, me, *parts, *packed, diag, ends)


def output_rows_kernel(sources, first, rows, pick_ref, *refs):
    parts = refs[:sources]
    out_ref, qkv_ref, arrived = refs[sources:]
    width = out_ref.shape[1]

    def place(at, number):
        here = pl.ds(at * rows, rows)
        if number == 0:
            return out_ref.at[here]
        return qkv_ref.at[here, pl.ds((number - 1) * width, width)]

    for at in range(pick_ref.shape[0]):
        for source in range(len(parts) - (parts[-1].shape[0] != parts[0].shape[0])):
            @pl.when(pick_ref[at] == source)
            def _():
                for number in range(4):
                    for copy in part_copies(
                        parts, source, first + number * rows, rows, place(at, number),
                        arrived.at[at, number],
                    ):
                        copy.start()
    for at in range(pick_ref.shape[0]):
        for number in range(4):
            pltpu.make_async_copy(
                parts[0].at[pl.ds(0, rows)], place(at, number), arrived.at[at, number]
            ).wait()


def attend_back_kernel(tiles, hp, me_ref, grad_ref, p_ref, qkv_ref, normed_ref, marks_ref, top_ref,
                       out_ref, kept_ref, away_ref, bias_grad, key_grad, value_grad):
    i = pl.program_id(0)
    block, lanes = grad_ref.shape

    @pl.when(i == 0)
    def _():
        bias_grad[...] = jnp.zeros_like(bias_grad)
        key_grad[...] = jnp.zeros_like(key_grad)
        value_grad[...] = jnp.zeros_like(value_grad)

    here = pl.multiple_of(i * block, block)
    query = qkv_ref[pl.ds(here, block), :lanes] * jnp.asarray(HDIM ** -0.5, BF)
    grad = grad_ref[...]
    masks = [head_lanes(block, lanes, h) for h in range(hp)]

    def rows_of(span):
        wide = span * block
        first = pl.multiple_of((i - span + 1) * block, block)
        column = (tiles - span) * block
        key = qkv_ref[pl.ds(first, wide), lanes : 2 * lanes]
        value = qkv_ref[pl.ds(first, wide), 2 * lanes :]
        out = key_part = value_part = None
        for h in range(hp):
            head = jnp.where(masks[h], query, jnp.zeros_like(query))
            head_grad = jnp.where(masks[h], grad, jnp.zeros_like(grad))
            weight = p_ref[0, h, :, column:]
            wide_weight = weight.astype(F32)
            t = wide_weight * dot(head_grad, value, ((1,), (1,)))
            s = t - wide_weight * jnp.sum(t, axis=1, keepdims=True)
            bias_grad[h, :, column:] += s
            s = s.astype(BF)
            part = dot(s, key)
            out = part if out is None else jnp.where(masks[h], part, out)
            part = dot(s, head, ((0,), (0,)))
            key_part = part if key_part is None else key_part + part
            part = dot(weight, head_grad, ((0,), (0,)))
            value_part = part if value_part is None else value_part + part
        key_grad[pl.ds(first, wide), :] += key_part
        value_grad[pl.ds(first, wide), :] += value_part
        out_ref[pl.ds(here, block), :lanes] = (out * HDIM ** -0.5).astype(BF)

    for span in range(1, tiles):
        @pl.when(i == span - 1)
        def _():
            rows_of(span)

    @pl.when(i >= tiles - 1)
    def _():
        rows_of(tiles)

    @pl.when(i == pl.num_programs(0) - 1)
    def _():
        out_ref[:, lanes : 2 * lanes] = key_grad[...].astype(BF)
        out_ref[:, 2 * lanes :] = value_grad[...].astype(BF)
        grad_cols = dot(normed_ref[...], out_ref[...], ((0,), (0,))).astype(BF)
        split_store(kept_ref, away_ref, me_ref[0], grad_cols)
        bins = marks_ref.shape[1]
        wide = 3 * lanes
        notes = []
        for h in range(hp):
            total = jnp.zeros((1, bins), F32)
            for m in range(tiles):
                at = (tiles - 1 - m) * block
                x = bias_grad[h, :, at : at + block]
                x = jnp.concatenate([x, jnp.zeros((block, block), F32)], axis=1)
                half = block // 2
                while half >= 1:
                    x = x[:half] + pltpu.roll(x[half : 2 * half], 2 * block - half, 1)
                    half //= 2
                high, low = halves(x)
                part = marks_ref[m * 2 * block : (m + 1) * 2 * block, :]
                total += dot(high, part) + dot(low, part)
            notes.append(jnp.concatenate([total, jnp.zeros((1, wide - bins), F32)], axis=1))
        spot = lax.broadcasted_iota(jnp.int32, (1, AUX), 1) == me_ref[0]
        for h in range(hp):
            top = top_ref[h : h + 1, :]
            high = top.astype(BF).astype(F32)
            notes.append(
                jnp.concatenate(
                    [jnp.where(spot, high, 0.0), jnp.where(spot, top - high, 0.0)]
                    + [jnp.zeros((1, wide - 2 * AUX), F32)],
                    axis=1,
                )
            )
        notes.append(jnp.zeros((16 - 2 * hp, wide), F32))
        notes = jnp.concatenate(notes, axis=0).astype(BF)
        for ref in (kept_ref, away_ref):
            for at in range(ref.shape[0]):
                ref[at, ref.shape[1] - 16 :] = notes


def attend_back(me, attention_grad, weights, qkv, normed, marks, top, hp, block, spread):
    seq, lanes = attention_grad.shape
    count = seq // block
    width = normed.shape[1]
    tiles = weights.shape[3] // block
    fixed = lambda i: (0, 0)
    pairs = count * tiles * hp * block * block
    owned = (spread // 2, width // spread + 16, 3 * lanes)
    return call(
        lambda *refs: attend_back_kernel(tiles, hp, *refs),
        (struct((seq, 3 * lanes), BF), struct(owned, BF), struct(owned, BF)),
        60e9,
        10 * seq * lanes + 2 * pairs,
        grid=(count,),
        in_specs=[
            pl.BlockSpec(memory_space=pltpu.SMEM),
            pl.BlockSpec((block, lanes), lambda i: (i, 0)),
            pl.BlockSpec((1, hp, block, tiles * block), lambda i: (i, 0, 0, 0)),
            pl.BlockSpec((seq, 3 * lanes), fixed),
            pl.BlockSpec((seq, width), fixed),
            pl.BlockSpec(marks.shape, fixed),
            pl.BlockSpec(top.shape, fixed),
        ],
        out_specs=[pl.BlockSpec((seq, 3 * lanes), fixed)]
        + [pl.BlockSpec(owned, lambda i: (0, 0, 0))] * 2,
        scratch_shapes=[
            pltpu.VMEM((hp, block, tiles * block), F32),
            pltpu.VMEM((seq, lanes), F32),
            pltpu.VMEM((seq, lanes), F32),
        ],
    )(me, attention_grad, weights, qkv, normed, marks, top)


def upstream_kernel(places_ref, other_ref, grad_ref, out_ref):
    experts, capacity, _ = out_ref.shape
    rows = grad_ref.shape[0]
    slots = experts * capacity
    other = other_ref[...]
    slot = lax.broadcasted_iota(jnp.int32, (slots, rows), 0)
    first = jnp.where(slot == places_ref[0:1, :], 1.0, 0.0).astype(BF)
    second = jnp.where(slot == places_ref[1:2, :], 1.0, 0.0).astype(BF)
    sent = dot(first + second, grad_ref[...]).astype(BF)
    named = (dot(first, other[0]) + dot(second, other[1])).astype(BF)
    for at in range(experts):
        here = slice(at * capacity, (at + 1) * capacity)
        out_ref[at, :, 128:] = sent[here]
        out_ref[at, :, :128] = named[here]


def token_front_kernel(spread, me_ref, attn_ref, tok_ref, aux_ref, places_ref, *refs):
    w_refs = refs[:spread]
    attention_ref, resid_ref, normed_ref = refs[spread : spread + 3]
    buffers = refs[spread + 3 : -2]
    whole, arrived = refs[-2:]
    collect(w_refs, me_ref[0], whole, arrived)
    blocks = attn_ref.shape[0]
    attention = jnp.concatenate([attn_ref[at] for at in range(blocks)], axis=1)
    attention_ref[...] = attention
    width = attention.shape[1]
    gain = gain_row(aux_ref[...], 1)
    collected(w_refs, whole, arrived)
    resid = tok_ref[...].astype(F32) + dot(attention, whole[...].reshape(width, width))
    resid_ref[...] = resid
    r = lax.rsqrt(jnp.mean(resid * resid, axis=1, keepdims=True) + EPSILON)
    normed = (resid * r * gain).astype(BF)
    normed_ref[...] = normed
    slots = buffers[0].shape[0]
    slot = lax.broadcasted_iota(jnp.int32, (slots * len(buffers), normed.shape[0]), 0)
    named = (slot == places_ref[2:3, :]) | (slot == places_ref[3:4, :])
    sent = dot(jnp.where(named, 1.0, 0.0).astype(BF), normed).astype(BF)
    for k, buffer in enumerate(buffers):
        buffer[...] = sent[k * slots : (k + 1) * slots]


def token_middle_kernel(returned_ref, resid_ref, normed_ref, aux_ref, ids_ref, grad_ref,
                        mixed_ref, logit_ref, route_ref):
    slots = returned_ref.shape[0]
    rows = resid_ref.shape[0]
    slot = lax.broadcasted_iota(jnp.int32, (rows, slots), 1)
    first = jnp.where(slot == ids_ref[:, 0:1], 1.0, 0.0).astype(BF)
    second = jnp.where(slot == ids_ref[:, 1:2], 1.0, 0.0).astype(BF)
    returned = returned_ref[...]
    first_out = dot(first, returned)
    second_out = dot(second, returned)
    normed = normed_ref[...]
    logits = dot(normed, aux_ref[...])
    lane = lax.broadcasted_iota(jnp.int32, logits.shape, 1) - ROUTER_AT
    at_first = lane == ids_ref[:, 2:3]
    at_second = lane == ids_ref[:, 3:4]
    gap = jnp.sum(
        jnp.where(at_first, logits, 0.0) - jnp.where(at_second, logits, 0.0),
        axis=1, keepdims=True,
    )
    gate_one = 1.0 / (1.0 + jnp.exp(-gap))
    gate_two = 1.0 / (1.0 + jnp.exp(gap))
    mixed_ref[...] = (resid_ref[...] + gate_one * first_out + gate_two * second_out).astype(BF)
    upstream = grad_ref[...].astype(F32)
    change = jnp.sum(upstream * (first_out - second_out), axis=1, keepdims=True)
    slope = gate_one * gate_two * change
    logit = jnp.where(at_first, slope, 0.0) - jnp.where(at_second, slope, 0.0)
    logit_ref[...] = logit
    high, low = halves(logit)
    route_ref[...] = dot(normed, high, ((0,), (0,))) + dot(normed, low, ((0,), (0,)))


def norm_back(values, gain, grad):
    r = lax.rsqrt(jnp.mean(values * values, axis=1, keepdims=True) + EPSILON)
    scaled = grad * gain
    slope = jnp.mean(values * scaled, axis=1, keepdims=True)
    return r * scaled - values * (r * r * r * slope), r


def token_back_kernel(spread, me_ref, logit_ref, aux_ref, ids_ref, resid_ref, grad_ref, back_ref,
                      *refs):
    w_refs = refs[:spread]
    attention_ref, route_ref = refs[spread : spread + 2]
    resid_grad_ref, attention_grad_ref, kept_ref, away_ref, whole, arrived = refs[-6:]
    collect(w_refs, me_ref[0], whole, arrived)
    resid = resid_ref[...]
    rows, width = resid.shape
    slots = back_ref.shape[0]
    slot = lax.broadcasted_iota(jnp.int32, (rows, slots), 1)
    named = (slot == ids_ref[:, 0:1]) | (slot == ids_ref[:, 1:2])
    normed_grad = dot(jnp.where(named, 1.0, 0.0).astype(BF), back_ref[...])
    high, low = halves(logit_ref[...])
    aux = aux_ref[...]
    gain = gain_row(aux, 1)
    normed_grad += dot(high, aux, ((1,), (1,))) + dot(low, aux, ((1,), (1,)))
    part, r = norm_back(resid, gain, normed_grad)
    resid_grad = grad_ref[...].astype(F32) + part
    resid_grad_ref[...] = resid_grad
    gain_grad = jnp.sum(normed_grad * resid * r, axis=0, keepdims=True)
    proj = resid_grad.astype(BF)
    blocks, _, lanes = attention_grad_ref.shape
    collected(w_refs, whole, arrived)
    grad = dot(proj, whole[...].reshape(width, width), ((1,), (1,))).astype(BF)
    for at in range(blocks):
        attention_grad_ref[at] = grad[:, at * lanes : (at + 1) * lanes]
    grad_proj = dot(attention_ref[...], proj, ((0,), (0,))).astype(BF)
    lane = lax.broadcasted_iota(jnp.int32, (width, AUX), 1)
    gain_grad = jnp.broadcast_to(gain_grad, (AUX, width)).T
    small = jnp.where(lane == GAIN_AT, gain_grad, route_ref[...]).astype(BF)
    split_store(kept_ref, away_ref, me_ref[0], jnp.concatenate([grad_proj, small], axis=1))


def token_last_kernel(blocks_ref, w_ref, tok_ref, aux_ref, resid_grad_ref, out_ref, grads, total):
    part = pl.program_id(0)
    blocks, _, wide = blocks_ref.shape
    lanes = wide // 3
    for number in range(3):
        @pl.when(part == number)
        def _():
            for at in range(blocks):
                grads[:, at * lanes : (at + 1) * lanes] = blocks_ref[
                    at, :, number * lanes : (number + 1) * lanes
                ]

    term = dot(grads[...], w_ref[...], ((1,), (1,)))

    @pl.when(part == 0)
    def _():
        total[...] = term

    @pl.when(part > 0)
    def _():
        total[...] += term

    @pl.when(part == 2)
    def _():
        change, _ = norm_back(tok_ref[...].astype(F32), gain_row(aux_ref[...], 0), total[...])
        out_ref[...] = resid_grad_ref[...] + change


def note_row(notes, hp, spread, head):
    lane = lax.broadcasted_iota(jnp.int32, (1, AUX), 1)
    rel = jnp.where(lane < BUCKETS, notes[head : head + 1, :AUX], 0.0)
    tops = notes[hp + head : hp + head + 1]
    high = jnp.where(lane < spread, tops[:, :AUX], 0.0)
    low = jnp.where(lane < spread, tops[:, AUX : 2 * AUX], 0.0)
    return rel, high, low


def join_kernel(hp, spread, own_ref, proj_kept_ref, proj_got_ref, cols_kept_ref, cols_got_ref,
                kept_ref, away_ref):
    rows, wide = proj_kept_ref.shape
    pairs, own_rows, _ = kept_ref.shape
    even = own_ref[0] % 2 == 0
    proj = proj_kept_ref[...].astype(F32) + proj_got_ref[...].astype(F32)
    cols = cols_kept_ref[...].astype(F32) + cols_got_ref[...].astype(F32)
    notes = cols[rows:]
    row = lax.broadcasted_iota(jnp.int32, (own_rows, AUX), 0)
    extra = jnp.zeros((own_rows, AUX), F32)
    for h in range(hp):
        rel, high, low = note_row(notes, hp, spread, h)
        line = pltpu.roll(rel, BIAS_AT, 1) + pltpu.roll(high, TOP_AT, 1)
        line += pltpu.roll(low, TOP_LOW_AT, 1)
        extra += jnp.where(row == h + hp * (own_ref[0] % 2), line, 0.0)
    extra = jnp.concatenate([jnp.zeros((own_rows, wide - AUX), F32), extra], axis=1)
    for pair in range(pairs):
        at = 2 * pair * own_rows
        one, two = slice(at, at + own_rows), slice(at + own_rows, at + 2 * own_rows)
        kept_ref[pair, :, :wide] = (jnp.where(even, proj[one], proj[two]) + extra).astype(BF)
        away_ref[pair, :, :wide] = (jnp.where(even, proj[two], proj[one]) + extra).astype(BF)
        kept_ref[pair, :, wide:] = jnp.where(even, cols[one], cols[two]).astype(BF)
        away_ref[pair, :, wide:] = jnp.where(even, cols[two], cols[one]).astype(BF)


def pair_kernel(wide, own_ref, kept_ref, got_ref, *sends):
    even = own_ref[0] % 2 == 0
    for k, send in enumerate(sends):
        pair = (own_ref[0] // 2) ^ k
        kept, got = kept_ref[pair], got_ref[pair]
        send[:, :wide] = (kept[:, :wide].astype(F32) + got[:, :wide].astype(F32)).astype(BF)
        columns = kept.shape[1] - wide
        send[:, wide : wide + columns] = jnp.where(even, kept[:, wide:], got[:, wide:])
        send[:, wide + columns :] = jnp.where(even, got[:, wide:], kept[:, wide:])


def join_plain(hp, spread, place, groups, proj_terms, cols_terms):
    proj, cols = joined(proj_terms), joined(cols_terms)
    rows, wide = proj.shape
    own_rows = rows // groups
    notes = cols[rows:]
    whole = jnp.concatenate([proj, cols[:rows]], axis=1).reshape(groups, own_rows, -1)
    lines = []
    for h in range(hp):
        rel, high, low = note_row(notes, hp, spread, h)
        line = jnp.roll(rel, BIAS_AT, 1) + jnp.roll(high, TOP_AT, 1) + jnp.roll(low, TOP_LOW_AT, 1)
        lines.append(line)
    extra = jnp.concatenate(lines, axis=0)
    extra = jnp.pad(extra, ((0, own_rows - hp), (wide - AUX, whole.shape[2] - wide)))
    whole = (whole + extra).astype(BF)
    return [
        lax.dynamic_index_in_dim(whole, place ^ k, axis=0, keepdims=False) for k in range(groups)
    ]


def owner_kernel(hp, sharers, spread, own_ref, q_ref, k_ref, v_ref, gain_ref, *refs):
    (proj_ref, route_ref, gain_two_ref, gq_ref, gk_ref, gv_ref, gain_one_ref, rel_ref,
     factor_ref, summary_ref) = refs[-10:]
    blocks = refs[:-10]
    experts = route_ref.shape[0]
    eye = lax.broadcasted_iota(jnp.int32, (proj_ref.shape[0],) * 2, 0)
    eye = eye == lax.broadcasted_iota(jnp.int32, eye.shape, 1)

    def as_row(column):
        return jnp.sum(jnp.where(eye, column, 0.0), axis=0, keepdims=True)

    width = proj_ref.shape[1]
    lanes = hp * HDIM
    sources = (blocks[0].shape[1] - width - AUX) // (3 * lanes)
    total = None
    for block in blocks:
        term = block[:, : width + AUX].astype(F32)
        total = term if total is None else total + term
    proj_ref[...] = total[:, :width]
    small = total[:, width:].T
    route_ref[...] = small[ROUTER_AT : ROUTER_AT + experts]
    gain_two_ref[...] = small[GAIN_AT : GAIN_AT + 1]
    outs = (gq_ref, gk_ref, gv_ref)
    for out in outs:
        out[...] = jnp.zeros_like(out)
    lane = lax.broadcasted_iota(jnp.int32, (1, 128), 1)
    summary_ref[...] = jnp.where(
        lax.broadcasted_iota(jnp.int32, summary_ref.shape, 1) == 64, MASKED, 0.0
    )
    for k, source in [(k, source) for k in range(len(blocks)) for source in range(sources)]:
        block = blocks[k]
        seat = (((own_ref[0] // sources) ^ k) * sources + source) % sharers
        at = pl.multiple_of(seat * lanes, lanes)
        for part, out in enumerate(outs):
            first = width + AUX + (3 * source + part) * lanes
            out[:, pl.ds(at, lanes)] += block[:, first : first + lanes].astype(F32)
        notes = block[:, width : width + AUX].astype(F32)
        for h in range(hp):
            note = notes[source * hp + h : source * hp + h + 1]
            rel = jnp.where(lane < BUCKETS, pltpu.roll(note, AUX - BIAS_AT, 1), 0.0)
            tops = pltpu.roll(note, AUX - TOP_AT, 1) + pltpu.roll(note, AUX - TOP_LOW_AT, 1)
            top = jnp.max(jnp.where(lane < spread, tops, MASKED), axis=1, keepdims=True)
            old = summary_ref[pl.ds(seat * hp + h, 1), :]
            new = jnp.where(lane == 64, jnp.maximum(old, top), old + rel)
            summary_ref[pl.ds(seat * hp + h, 1), :] = new
    rel_ref[...] = summary_ref[:, :BUCKETS]
    factor_ref[...] = jnp.sqrt(CLIP_LEVEL / jnp.maximum(summary_ref[...].T[64:65], 1.0))
    grad = jnp.zeros((proj_ref.shape[0], 1), F32)
    for out, w_ref in zip(outs, (q_ref, k_ref, v_ref)):
        grad += jnp.sum(out[...] * w_ref[...].astype(F32), axis=1, keepdims=True)
    gain_one_ref[...] = as_row(grad) / gain_ref[...]


GELU_A = 0.7978845608028654
GELU_B = 0.044715


def expert_kernel(groups, own_ref, upstream_ref, aux_ref, gate_ref, up_ref, down_ref, *refs):
    blocks = refs[:groups]
    (gate_pre_ref, up_pre_ref, out_ref, rows_ref, slot_grad_ref, grad_down_ref, total) = refs[groups:]
    f = pl.program_id(0)
    capacity, width = blocks[0].shape

    @pl.when(f == 0)
    def _():
        total[...] = jnp.zeros_like(total)
        for k, block in enumerate(blocks):
            rows_ref[k * capacity : (k + 1) * capacity, :] = block[...]
        all_logits = dot(rows_ref[...], aux_ref[...])
        for k in range(groups):
            here = slice(k * capacity, (k + 1) * capacity)
            logits = all_logits[here]
            lane = lax.broadcasted_iota(jnp.int32, logits.shape, 1) - ROUTER_AT
            upstream = upstream_ref[own_ref[0] ^ k]
            other = upstream[:, 0:1].astype(F32).astype(jnp.int32)
            gap = jnp.sum(
                jnp.where(lane == other, logits, 0.0) - jnp.where(lane == own_ref[0], logits, 0.0),
                axis=1, keepdims=True,
            )
            gate = 1.0 / (1.0 + jnp.exp(gap))
            slot_grad_ref[here, :] = (gate * upstream[:, 128:].astype(F32)).astype(BF)

    rows = rows_ref[...]
    gate_pre = dot(rows, gate_ref[...])
    up_pre = dot(rows, up_ref[...])
    gate_pre_ref[...] = gate_pre
    up_pre_ref[...] = up_pre
    inner = jnp.tanh(GELU_A * (gate_pre + GELU_B * gate_pre * gate_pre * gate_pre))
    hidden = (0.5 * gate_pre * (1.0 + inner) * up_pre).astype(BF)
    total[...] += dot(hidden, down_ref[...])
    grad_down_ref[...] = dot(hidden, slot_grad_ref[...], ((0,), (0,))).astype(BF)

    @pl.when(f == pl.num_programs(0) - 1)
    def _():
        for k in range(groups):
            out_ref[own_ref[0] ^ k] = total[k * capacity : (k + 1) * capacity, :].astype(BF)


def expert_forward(own, upstream, aux, blocks, gate, up, down, tile):
    groups = len(blocks)
    capacity, width = blocks[0].shape
    count = groups * capacity
    ff = gate.shape[1]
    fixed = lambda f: (0, 0)
    cols = lambda f: (0, f)
    return call(
        lambda *refs: expert_kernel(groups, *refs),
        (
            struct((count, ff), F32),
            struct((count, ff), F32),
            struct((groups, capacity, width), BF),
            struct((count, width), BF),
            struct((count, width), BF),
            struct((ff, width), BF),
        ),
        24e9,
        6 * width * ff + 10 * count * ff,
        grid=(ff // tile,),
        in_specs=[
            pl.BlockSpec(memory_space=pltpu.SMEM),
            pl.BlockSpec(upstream.shape, lambda f: (0, 0, 0)),
            pl.BlockSpec(aux.shape, fixed),
            pl.BlockSpec((width, tile), cols),
            pl.BlockSpec((width, tile), cols),
            pl.BlockSpec((tile, width), lambda f: (f, 0)),
        ]
        + [pl.BlockSpec((capacity, width), fixed)] * groups,
        out_specs=[
            pl.BlockSpec((count, tile), cols),
            pl.BlockSpec((count, tile), cols),
            pl.BlockSpec((groups, capacity, width), lambda f: (0, 0, 0)),
            pl.BlockSpec((count, width), fixed),
            pl.BlockSpec((count, width), fixed),
            pl.BlockSpec((tile, width), lambda f: (f, 0)),
        ],
        scratch_shapes=[pltpu.VMEM((count, width), F32)],
    )(own, upstream, aux, gate, up, down, *blocks)


def split_store(kept_ref, away_ref, me, values):
    rows = values.shape[0] // (2 * kept_ref.shape[0])
    for d in range(2 * kept_ref.shape[0]):
        block = values[d * rows : (d + 1) * rows]
        @pl.when(me % 2 == d % 2)
        def _():
            kept_ref[d // 2, :rows] = block

        @pl.when(me % 2 != d % 2)
        def _():
            away_ref[d // 2, :rows] = block


def expert_back_kernel(own_ref, me_ref, slot_grad_ref, rows_ref, gate_pre_ref, up_pre_ref, down_ref,
                       gate_ref, up_ref, row_grad_ref, grad_gate_ref, up_kept_ref, up_away_ref,
                       total, pre_grads, split_rows):
    f = pl.program_id(0)
    tiles = pl.num_programs(0) - 1
    tile = gate_ref.shape[1]
    groups, capacity, _ = row_grad_ref.shape

    def through_gelu(slot):
        hidden_grad = dot(slot_grad_ref[...], down_ref[...], ((1,), (1,)))
        v = gate_pre_ref[...]
        square = v * v
        inner = jnp.tanh(v * (GELU_A + GELU_A * GELU_B * square))
        half = 0.5 + 0.5 * inner
        slope = half + (0.5 * v) * (1.0 - inner * inner) * (
            GELU_A + 3.0 * GELU_A * GELU_B * square
        )
        pre_grads[slot, :, :tile] = (hidden_grad * up_pre_ref[...] * slope).astype(BF)
        pre_grads[slot, :, tile:] = (hidden_grad * (v * half)).astype(BF)

    def to_weights(slot):
        both = pre_grads[slot]
        weights = jnp.concatenate([gate_ref[...], up_ref[...]], axis=1)
        total[...] += dot(both, weights, ((1,), (1,)))
        grad_gate_ref[...] = dot(rows_ref[...], both[:, :tile], ((0,), (0,))).astype(BF)
        grads = dot(split_rows[...], both[:, tile:], ((0,), (0,))).astype(BF)
        half = grads.shape[0] // 2
        up_kept_ref[...] = grads[:half].reshape(up_kept_ref.shape)
        up_away_ref[...] = grads[half:].reshape(up_kept_ref.shape)

    @pl.when(f == 0)
    def _():
        total[...] = jnp.zeros_like(total)
        part = up_kept_ref.shape[1]
        half = rows_ref.shape[1] // 2
        even = me_ref[0] % 2 == 0
        for pair in range(up_kept_ref.shape[0]):
            one = rows_ref[:, 2 * pair * part : (2 * pair + 1) * part]
            two = rows_ref[:, (2 * pair + 1) * part : (2 * pair + 2) * part]
            at = pair * part
            split_rows[:, at : at + part] = jnp.where(even, one, two)
            split_rows[:, half + at : half + at + part] = jnp.where(even, two, one)
        through_gelu(0)

    @pl.when((f > 0) & (f < tiles))
    def _():
        to_weights((f - 1) % 2)
        through_gelu(f % 2)

    @pl.when(f == tiles)
    def _():
        to_weights((f - 1) % 2)
        for k in range(groups):
            row_grad_ref[own_ref[0] ^ k] = total[k * capacity : (k + 1) * capacity, :].astype(BF)


def expert_backward(own, me, slot_grad, rows, gate_pre, up_pre, gate, up, down, tile, groups,
                    spread):
    count, width = rows.shape
    ff = gate.shape[1]
    tiles = ff // tile
    fixed = lambda f: (0, 0)
    now = lambda f: (0, jnp.minimum(f, tiles - 1))
    before = lambda f: (0, jnp.maximum(f - 1, 0))
    owned = (spread // 2, width // spread)
    return call(
        expert_back_kernel,
        [
            struct((groups, count // groups, width), BF),
            struct((width, ff), BF),
        ]
        + [struct(owned + (ff,), BF)] * 2,
        30e9,
        12 * width * ff + 10 * count * ff,
        grid=(tiles + 1,),
        in_specs=[
            pl.BlockSpec(memory_space=pltpu.SMEM),
            pl.BlockSpec(memory_space=pltpu.SMEM),
            pl.BlockSpec((count, width), fixed),
            pl.BlockSpec((count, width), fixed),
            pl.BlockSpec((count, tile), now),
            pl.BlockSpec((count, tile), now),
            pl.BlockSpec((tile, width), lambda f: (jnp.minimum(f, tiles - 1), 0)),
            pl.BlockSpec((width, tile), before),
            pl.BlockSpec((width, tile), before),
        ],
        out_specs=[
            pl.BlockSpec((groups, count // groups, width), lambda f: (0, 0, 0)),
            pl.BlockSpec((width, tile), before),
        ]
        + [pl.BlockSpec(owned + (tile,), lambda f: (0, 0, jnp.maximum(f - 1, 0)))] * 2,
        scratch_shapes=[
            pltpu.VMEM((count, width), F32),
            pltpu.VMEM((2, count, 2 * tile), BF),
            pltpu.VMEM((count, width), BF),
        ],
    )(own, me, slot_grad, rows, gate_pre, up_pre, down, gate, up)


def slot_places(routes, experts, capacity):
    chosen = (routes[:, :, None] == jnp.arange(experts, dtype=jnp.int32)[None, None, :]).astype(
        jnp.int32
    )
    order = jnp.swapaxes(chosen, 0, 1).reshape(-1, experts)
    before = jnp.cumsum(order, axis=0) - order
    slots = jnp.sum(before * order, axis=1).reshape(TOP, -1).T
    return routes * capacity + slots


def flip(values, axis, mask):
    n = lax.axis_size(axis)
    return lax.ppermute(values, axis, [(k, k ^ mask) for k in range(n)])


def gather_parts(part, axis):
    return gather_rest({0: part}, axis, lax.axis_size(axis) // 2)


def gather_rest(held, axis, bit):
    while bit >= 1:
        held.update({j ^ bit: flip(values, axis, bit) for j, values in list(held.items())})
        bit //= 2
    return [held[j] for j in range(len(held))]


def swap_parts(parts, axis):
    return [parts[0]] + [flip(parts[k], axis, k) for k in range(1, len(parts))]


def ring_parts(tokens, before, between):
    devices = lax.axis_size("expert")
    line = list(range(0, devices, 2)) + list(range(devices - 1, 0, -2))
    spots = [line.index(k) for k in range(devices)]

    def move(values, step):
        pairs = [(line[k], line[(k + step) % devices]) for k in range(devices)]
        return lax.ppermute(values, "expert", pairs)

    ahead = [tokens]
    behind = [tokens]
    half = devices // 2
    for k in range(1, half):
        pair = (move(ahead[-1], 1), move(behind[-1], -1))
        if k == half - 2:
            *pair, first = lax.optimization_barrier((*pair, before[0]))
            before = (between(first),) + before[1:]
        elif k == half - 1:
            *pair, before = lax.optimization_barrier((*pair, before))
        else:
            pair = lax.optimization_barrier(pair)
        ahead.append(pair[0])
        behind.append(pair[1])
    cut = tokens.shape[0] // 2
    farthest = (move(ahead[-1][:cut], 1), move(behind[-1][cut:], -1))
    parts = ahead + behind[:0:-1] + list(farthest)
    spot = jnp.asarray(spots, jnp.int32)
    mine = jnp.sum(jnp.where(jnp.arange(devices) == lax.axis_index("expert"), spot, 0))
    gap = (mine - spot) % devices
    gap = jnp.where(gap == half, devices - 1, jnp.where(gap > half, gap - 1, gap))
    return gap.astype(jnp.int32), parts, before


def scatter_step(parts, axis, me, bit):
    pairs = parts.reshape((parts.shape[0] // 2, 2) + parts.shape[1:])
    mine = (me // bit) % 2
    away = lax.dynamic_index_in_dim(pairs, 1 - mine, axis=1, keepdims=False)
    kept = lax.dynamic_index_in_dim(pairs, mine, axis=1, keepdims=False)
    return kept, flip(away, axis, bit)


def joined(parts):
    return parts[0].astype(F32) + parts[1].astype(F32)


def scatter_rest(parts, axis):
    n = lax.axis_size(axis)
    me = lax.axis_index(axis)
    bit = 2
    while True:
        terms = scatter_step(parts, axis, me, bit)
        bit *= 2
        if bit >= n:
            return tuple(term[0] for term in terms)
        parts = joined(terms).astype(BF)


def body(tokens, gain_attn, w_query, w_key, w_value, w_output, rel_bias, gain_ffn, w_router,
         expert_gate, expert_up, expert_down, routes, doc_lengths, seq_valid, grad_output):
    length, width = tokens.shape
    groups = lax.axis_size("expert")
    spread = lax.axis_size("dp")
    place = lax.axis_index("expert")
    device = lax.axis_index("dp") * groups + place
    experts = w_router.shape[1]
    capacity = 5 * TOP * length // (4 * experts)
    slots = experts * capacity
    sharers = SEQ // length
    hp = HEADS // sharers
    lanes = hp * HDIM
    own_rows = w_query.shape[0]
    teams = None
    if groups != sharers:
        teams = [list(range(at, at + sharers)) for at in range(0, groups, sharers)]
    both = ("dp", "expert")

    def exchange(blocks):
        return lax.all_to_all(blocks, "expert", 0, 0, axis_index_groups=teams, tiled=True)

    def exchange_all(blocks):
        return lax.all_to_all(blocks, "expert", 0, 0, tiled=True)

    def columns(w):
        return w.reshape(own_rows, sharers, lanes).swapaxes(0, 1)

    extra = jnp.concatenate([gain_attn[:, None], gain_ffn[:, None], w_router], axis=1)
    extra = jnp.pad(extra, ((0, 0), (0, AUX - extra.shape[1])))
    sent = jnp.concatenate(
        [
            columns(w_query),
            columns(w_key),
            columns(w_value),
            jnp.broadcast_to(extra[None], (sharers, own_rows, AUX)),
        ],
        axis=2,
    )
    sent = jnp.tile(sent, (groups // sharers, 1, 1))
    gate_all = lax.all_gather(expert_gate[0], "dp", axis=0, tiled=True)
    up_all = lax.all_gather(expert_up[0], "dp", axis=0, tiled=True)
    down_all = lax.all_gather(expert_down[0], "dp", axis=0, tiled=True)

    places = slot_places(routes, experts, capacity)
    near_places = places + ((routes ^ place) - routes) * capacity
    ids = jnp.concatenate([places, routes, near_places], axis=1)
    ids = jnp.pad(ids, ((0, 0), (0, 128 - ids.shape[1])))
    places_row = jnp.pad(
        jnp.concatenate([places, near_places], axis=1).T, ((0, 4), (0, 0)), constant_values=-1
    )
    other = jnp.broadcast_to(routes.T[::-1, :, None], (TOP, length, 128)).astype(BF)
    upstream = call(
        upstream_kernel,
        struct((experts, capacity, width + 128), BF),
        3e9,
        4 * slots * width,
    )(places_row, other, grad_output)

    number = (device * length) // SEQ
    ends = jnp.cumsum(lax.dynamic_index_in_dim(doc_lengths, number, keepdims=False))
    ends = jnp.concatenate([ends, lax.dynamic_index_in_dim(seq_valid, number)]).astype(jnp.int32)
    block = length
    marks, inside = diagonal_tables(block, WINDOW, BUCKETS)
    head_at = (place % sharers) * hp
    own_bias = lax.dynamic_slice_in_dim(rel_bias, head_at, hp, axis=1)
    diag = jnp.dot(jnp.asarray(marks), own_bias, precision=lax.Precision.HIGHEST)
    diag = jnp.where(jnp.asarray(inside)[:, None], diag, MASKED)
    tiles = WINDOW // block + 1
    diag = diag.T.reshape(hp * tiles, 2 * block)
    packed = exchange_all(sent).reshape(groups * own_rows, 3 * lanes + AUX)
    mixed_rows = jnp.concatenate([tokens, w_output, w_query, w_key, w_value], axis=0)
    if teams is None:
        def between(values):
            return gather_parts(values, "dp")

        before = (packed, upstream, diag, ends, ids)
        pick, parts, before = ring_parts(mixed_rows, before, between)
        packed, upstream, diag, ends, ids = before
    else:
        whole = lax.all_gather(mixed_rows, "expert", axis=0, axis_index_groups=teams)
        pick = jnp.arange(sharers, dtype=jnp.int32)
        parts = [whole[at] for at in range(sharers)]
        packed = gather_parts(packed, "dp")
    me = lax.axis_index("dp").astype(jnp.int32).reshape(1)
    if teams is None:
        output_rows, qkv_rows = call(
            lambda *refs: output_rows_kernel(len(parts), length, own_rows, *refs),
            (struct((groups * own_rows, width), BF), struct((groups * own_rows, 3 * width), BF)),
            1e9,
            16 * groups * own_rows * width,
            mib=12, in_specs=[pl.BlockSpec(memory_space=pltpu.SMEM)]
            + [pl.BlockSpec(memory_space=pl.ANY)] * len(parts),
            out_specs=[pl.BlockSpec(memory_space=pltpu.VMEM)] * 2,
            scratch_shapes=[pltpu.SemaphoreType.DMA((sharers, 4))],
        )(pick, *parts)
        output_rows, attend_parts = lax.optimization_barrier((output_rows, parts))
    else:
        output_rows = lax.all_gather(w_output, "expert", axis=0, tiled=True)
        qkv_rows = jnp.concatenate([w_query, w_key, w_value], axis=1)
        qkv_rows = lax.all_gather(qkv_rows, "expert", axis=0, tiled=True)
        attend_parts = parts
    output_parts = {0: output_rows, spread // 2: flip(output_rows, "dp", spread // 2)}

    upstream, _ = lax.optimization_barrier((upstream, parts))
    upstream = exchange_all(upstream)

    normed_one, qkv, weights, attn, top, aux = attend(
        pick, me, attend_parts, packed, diag, ends, hp, block
    )
    attn, upstream, output_parts = lax.optimization_barrier((attn, upstream, output_parts))
    output_parts = gather_rest(output_parts, "dp", spread // 4)
    attn_blocks = exchange(attn.reshape(sharers, length, lanes))

    vmem = pl.BlockSpec(memory_space=pltpu.VMEM)
    smem = pl.BlockSpec(memory_space=pltpu.SMEM)
    loose = pl.BlockSpec(memory_space=pl.ANY)
    gathered = [
        pltpu.VMEM((spread,) + output_parts[0].shape, BF),
        pltpu.SemaphoreType.DMA((spread,)),
    ]
    attention, resid, normed_two, *buffers = call(
        lambda *refs: token_front_kernel(spread, *refs),
        [
            struct((length, width), BF),
            struct((length, width), F32),
            struct((length, width), BF),
        ]
        + [struct((capacity, width), BF)] * groups,
        5e9,
        2 * width * width + 8 * length * width,
        mib=24, in_specs=[smem] + [vmem] * 4 + [loose] * spread,
        scratch_shapes=gathered,
    )(me, attn_blocks, tokens, aux, places_row, *output_parts)
    rows = swap_parts(buffers, "expert")
    qkv_rows, _ = lax.optimization_barrier((qkv_rows, attn))
    qkv_all = lax.all_gather(qkv_rows, "dp", axis=0, tiled=True)

    tile = 256 if expert_gate.shape[2] % 256 == 0 else 128
    own = place.astype(jnp.int32).reshape(1)
    gate_pre, up_pre, expert_out, rows, slot_grad, grad_down = expert_forward(
        own, upstream, aux, rows, gate_all, up_all, down_all, tile
    )
    expert_out, qkv_all = lax.optimization_barrier((expert_out, qkv_all))
    returned = exchange_all(expert_out)
    row_grad, *expert_grads = expert_backward(
        own, me, slot_grad, rows, gate_pre, up_pre, gate_all, up_all, down_all, tile, groups,
        spread,
    )
    returned, row_grad, expert_grads = lax.optimization_barrier(
        (returned, row_grad, expert_grads)
    )
    grad_gate, up_kept, up_away = expert_grads
    up_first = joined((up_kept, flip(up_away, "dp", 1))).astype(BF)
    owned_down = lax.psum_scatter(grad_down, "dp", scatter_dimension=0, tiled=True)
    returned = returned.reshape(slots, width)
    back = exchange_all(row_grad)
    mixed, logit_grad, route_grad = call(
        token_middle_kernel,
        (
            struct((length, width), BF),
            struct((length, 128), F32),
            struct((width, 128), F32),
        ),
        5e9,
        2 * slots * width + 8 * length * width,
    )(returned, resid, normed_two, aux, ids, grad_output)
    back, owned_down = lax.optimization_barrier((back, owned_down))
    owned_down = owned_down.astype(F32)
    back = back.reshape(slots, width)
    cores = [list(range(core, spread, 2)) for core in range(2)]

    def scatter_chips(parts):
        parts = parts.reshape((-1,) + parts.shape[2:])
        return lax.psum_scatter(
            parts, "dp", scatter_dimension=0, axis_index_groups=cores, tiled=True
        )

    owned_gate = lax.psum_scatter(grad_gate, "dp", scatter_dimension=0, tiled=True)
    owned_up = scatter_chips(up_first)
    resid_grad, attention_grad, proj_kept, proj_away = call(
        lambda *refs: token_back_kernel(spread, *refs),
        (
            struct((length, width), F32),
            struct((sharers, length, lanes), BF),
            struct((spread // 2, width // spread, width + AUX), BF),
            struct((spread // 2, width // spread, width + AUX), BF),
        ),
        6e9,
        2 * width * width + 2 * slots * width + 8 * length * width,
        in_specs=[smem] + [vmem] * 6 + [loose] * spread + [vmem] * 2,
        scratch_shapes=gathered,
    )(me, logit_grad, aux, ids, resid, grad_output, back, *output_parts, attention, route_grad)
    attention_grad = exchange(attention_grad).reshape(SEQ, lanes)
    proj_first = proj_kept.astype(F32) + flip(proj_away, "dp", 1).astype(F32)
    attention_grad, proj_first, _ = lax.optimization_barrier(
        (attention_grad, proj_first.astype(BF), up_first)
    )
    proj_terms = scatter_rest(proj_first, "dp")

    grad_qkv_rows, cols_kept, cols_away = attend_back(
        me, attention_grad, weights, qkv, normed_one, jnp.asarray(marks, BF), top, hp, block, spread
    )
    grad_qkv_rows, cols_away, proj_terms, owned_gate = lax.optimization_barrier(
        (grad_qkv_rows, cols_away, proj_terms, owned_gate)
    )
    grads_here = exchange(grad_qkv_rows.reshape(sharers, length, 3 * lanes))
    owned_gate = owned_gate.astype(F32)
    fixed = lambda part: (0, 0)
    grad_tokens = call(
        token_last_kernel,
        struct((length, width), F32),
        60e9,
        6 * width * width + 12 * length * width,
        grid=(3,),
        mib=24, in_specs=[
            pl.BlockSpec(grads_here.shape, lambda part: (0, 0, 0)),
            pl.BlockSpec((width, width), lambda part: (0, part)),
            pl.BlockSpec((length, width), fixed),
            pl.BlockSpec(aux.shape, fixed),
            pl.BlockSpec((length, width), fixed),
        ],
        out_specs=pl.BlockSpec((length, width), fixed),
        scratch_shapes=[pltpu.VMEM((length, width), BF), pltpu.VMEM((length, width), F32)],
    )(grads_here, qkv_all, tokens, aux, resid_grad)

    cols_first = cols_kept.astype(F32) + flip(cols_away, "dp", 1).astype(F32)
    cols_terms = scatter_rest(cols_first.astype(BF), "dp")
    if own_rows % 16 == 0:
        pairs = groups // 2
        blocks = struct((pairs, own_rows, width + AUX + 3 * lanes), BF)
        pairs_kept, pairs_away = call(
            lambda *refs: join_kernel(hp, spread, *refs),
            [blocks] * 2,
            1e9,
            8 * groups * own_rows * width,
            mib=12, in_specs=[smem] + [vmem] * 4,
        )(own, *proj_terms, *cols_terms)
        sends = call(
            lambda *refs: pair_kernel(width + AUX, *refs),
            [struct((own_rows, width + AUX + 6 * lanes), BF)] * pairs,
            1e9,
            8 * groups * own_rows * width,
            mib=12, in_specs=[smem] + [vmem] * 2,
        )(own, pairs_kept, flip(pairs_away, "expert", 1))
        owned = [sends[0]] + [flip(sends[k], "expert", 2 * k) for k in range(1, pairs)]
    else:
        sends = join_plain(hp, spread, place, groups, proj_terms, cols_terms)
        owned = swap_parts(sends, "expert")
    grad_tokens, owned_up = lax.optimization_barrier((grad_tokens, owned_up))
    owned_up = owned_up.astype(F32)
    *owned, grad_tokens = lax.optimization_barrier((*owned, grad_tokens))
    grad_proj, route, gain_two, grad_q, grad_k, grad_v, gain_one, rel, factor = call(
        lambda *refs: owner_kernel(hp, sharers, spread, *refs),
        (
            struct((own_rows, width), F32),
            struct((experts, own_rows), F32),
            struct((1, own_rows), F32),
            struct((own_rows, width), F32),
            struct((own_rows, width), F32),
            struct((own_rows, width), F32),
            struct((1, own_rows), F32),
            struct((HEADS, BUCKETS), F32),
            struct((1, HEADS), F32),
        ),
        2e9,
        8 * own_rows * width,
        mib=12, in_specs=[smem] + [vmem] * (4 + len(owned)),
        scratch_shapes=[pltpu.VMEM((HEADS, 128), F32)],
    )(own, w_query, w_key, w_value, gain_attn.astype(F32)[None], *owned)
    return (
        mixed,
        grad_tokens,
        gain_one[0],
        grad_q,
        grad_k,
        grad_v,
        grad_proj,
        rel.T,
        gain_two[0],
        route.T,
        owned_gate[None],
        owned_up[None],
        owned_down[None],
        factor[0],
    )


def solution(mesh):
    rows = P(("dp", "expert"), None)
    vector = P(("dp", "expert"))
    expert = P("expert", "dp", None)
    return jax.shard_map(
        body,
        mesh=mesh,
        in_specs=(
            rows, vector, rows, rows, rows, rows, P(), vector, rows,
            expert, expert, expert, rows, P(), P(), rows,
        ),
        out_specs=(
            rows, rows, vector, rows, rows, rows, rows, P(), vector, rows,
            expert, expert, expert, P(),
        ),
        check_vma=False,
    )
```

```python
import jax
import jax.numpy as jnp
import numpy as np
from jax import lax
from jax.experimental import pallas as pl
from jax.experimental.pallas import tpu as pltpu
from jax.sharding import PartitionSpec as P

HEADS = 16
HDIM = 64
BUCKETS = 32
WINDOW = 1024
SEQ = 2048
DOCS = 4
TOP = 2

EPSILON = 1e-06
CLIP_LEVEL = 4.0
BF = jnp.bfloat16
F32 = jnp.float32
MASKED = -1e30
AUX = 128
ROUTER_AT = 2
GAIN_AT = 63
BIAS_AT = 64
TOP_AT = 96
TOP_LOW_AT = 112


def dot(left, right, dims=((1,), (0,))):
    return lax.dot_general(left, right, (dims, ((), ())), preferred_element_type=F32)


def halves(values):
    high = values.astype(BF)
    return high, (values - high.astype(F32)).astype(BF)


def call(kernel, out_shape, flops, nbytes, mib=56, **kwargs):
    return pl.pallas_call(
        kernel,
        out_shape=out_shape,
        compiler_params=pltpu.CompilerParams(vmem_limit_bytes=mib * 1024 * 1024),
        cost_estimate=pl.CostEstimate(
            flops=int(flops), bytes_accessed=int(nbytes), transcendentals=0
        ),
        **kwargs,
    )


def struct(shape, dtype):
    return jax.ShapeDtypeStruct(shape, dtype)


def bucket_of(span, buckets):
    distance = np.arange(span) * 1.0
    exact = buckets // 2
    safe = np.maximum(distance, 1.0)
    spread = exact + np.floor(np.log(safe / exact) / np.log(128.0 / exact) * (buckets - exact))
    return np.where(distance < exact, distance, np.minimum(spread, buckets - 1.0)).astype(np.int64)


def diagonal_tables(block, window, buckets):
    tiles = window // block + 1
    j = np.arange(2 * block)
    offset = np.where(j < block, -j, 2 * block - j)
    distance = np.arange(tiles)[:, None] * block + offset[None, :]
    inside = (distance >= 0) & (distance < window) & (j != block)[None, :]
    bucket = bucket_of(window, buckets)[np.clip(distance, 0, window - 1)]
    marks = (bucket[..., None] == np.arange(buckets)) & inside[..., None]
    return marks.astype(np.float32).reshape(-1, buckets), inside.reshape(-1)


def collect(parts, me, whole, arrived):
    for j, part in enumerate(parts):
        pltpu.make_async_copy(part, whole.at[me ^ j], arrived.at[j]).start()


def collected(parts, whole, arrived):
    for j, part in enumerate(parts):
        pltpu.make_async_copy(part, whole.at[0], arrived.at[j]).wait()


def part_copies(parts, source, first, rows, to, semaphore):
    cut = parts[-1].shape[0]
    if cut == parts[0].shape[0] or source < len(parts) - 2:
        return [pltpu.make_async_copy(parts[source].at[pl.ds(first, rows)], to, semaphore)]
    copies = []
    low = max(0, min(rows, cut - first))
    if low:
        copies.append(
            pltpu.make_async_copy(
                parts[source].at[pl.ds(first, low)], to.at[pl.ds(0, low)], semaphore
            )
        )
    if low < rows:
        copies.append(
            pltpu.make_async_copy(
                parts[source + 1].at[pl.ds(first + low - cut, rows - low)],
                to.at[pl.ds(low, rows - low)],
                semaphore,
            )
        )
    return copies


def gain_row(aux, at):
    rows = lax.broadcasted_iota(jnp.int32, (8, AUX), 0)
    lanes = lax.broadcasted_iota(jnp.int32, (8, AUX), 1)
    pick = jnp.where((rows == 0) & (lanes == at), 1.0, 0.0).astype(BF)
    return dot(pick, aux, ((1,), (1,)))[0:1]


def head_lanes(rows, lanes, head):
    lane = lax.broadcasted_iota(jnp.int32, (rows, lanes), 1)
    return lane // HDIM == head


def fold(values, combine):
    parts = [values[:, at : at + 128] for at in range(0, values.shape[1], 128)]
    total = parts[0]
    for part in parts[1:]:
        total = combine(total, part)
    return total


def attend_kernel(tiles, hp, sources, spread, pick_ref, me_ref, *refs):
    tok_refs = refs[:sources]
    w_refs = refs[sources : sources + spread]
    (diag_ref, ends_ref, normed_ref, qkv_ref, p_ref, out_ref, top_ref, aux_ref,
     bias, keys, values, tok, arrived, packed, w_arrived, gain) = refs[sources + spread :]
    i = pl.program_id(0)
    block, lanes = out_ref.shape
    width = normed_ref.shape[1]

    @pl.when(i == 0)
    def _():
        collect(w_refs, me_ref[0], packed, w_arrived)
        for at in range(tok.shape[0]):
            for source in range(sources - (tok_refs[-1].shape[0] != tok_refs[0].shape[0])):
                @pl.when(pick_ref[at] == source)
                def _():
                    for copy in part_copies(
                        tok_refs, source, 0, block, tok.at[at], arrived.at[at]
                    ):
                        copy.start()
        for h in range(hp):
            for m in range(tiles):
                at = h * tiles + m
                row = jnp.broadcast_to(diag_ref[at : at + 1, :], (block, 2 * block))
                at = (tiles - 1 - m) * block
                bias[h, :, at : at + block] = pltpu.roll(
                    row, 0, 1, stride=1, stride_axis=0
                )[:, :block]
        top_ref[...] = jnp.full_like(top_ref, MASKED)
        collected(w_refs, packed, w_arrived)
        aux_ref[...] = packed[:, :, 3 * lanes :].reshape(width, AUX)
        gain[...] = gain_row(aux_ref[...], 0)

    pltpu.make_async_copy(tok_refs[0].at[pl.ds(0, block)], tok.at[i], arrived.at[i]).wait()
    x = tok[i].astype(F32)
    r = lax.rsqrt(jnp.mean(x * x, axis=1, keepdims=True) + EPSILON)
    normed = (x * r * gain[...]).astype(BF)
    normed_ref[...] = normed
    w_cols = packed[:, :, : 3 * lanes].reshape(width, 3 * lanes)
    qkv = dot(normed, w_cols).astype(BF)
    qkv_ref[...] = qkv
    here = pl.multiple_of(i * block, block)
    keys[pl.ds(here, block), :] = qkv[:, lanes : 2 * lanes]
    values[pl.ds(here, block), :] = qkv[:, 2 * lanes :]
    query = qkv[:, :lanes] * jnp.asarray(HDIM ** -0.5, BF)
    masks = [head_lanes(block, lanes, h) for h in range(hp)]
    heads = [jnp.where(masks[h], query, jnp.zeros_like(query)) for h in range(hp)]

    def label_of(positions):
        label = jnp.zeros(positions.shape, jnp.int32)
        for at in range(DOCS):
            label += jnp.where(positions >= ends_ref[at], 1, 0)
        return label

    qlab = label_of(lax.broadcasted_iota(jnp.int32, (block, 1), 0) + i * block)

    def rows_of(span):
        wide = span * block
        first = pl.multiple_of((i - span + 1) * block, block)
        column = (tiles - span) * block
        key = keys[pl.ds(first, wide), :]
        value = values[pl.ds(first, wide), :]
        position = lax.broadcasted_iota(jnp.int32, (1, wide), 1) + first
        same = qlab == jnp.where(position < ends_ref[DOCS], label_of(position), -1)
        row = lax.broadcasted_iota(jnp.int32, (block, block), 0)
        diagonal = row == lax.broadcasted_iota(jnp.int32, (block, block), 1)
        out = None
        for h in range(hp):
            s = dot(heads[h], key, ((1,), (1,))) + bias[h, :, column:]
            last = wide - block
            own = jnp.where(same[:, last:] | diagonal, s[:, last:], MASKED)
            if span > 1:
                own = jnp.concatenate([jnp.where(same[:, :last], s[:, :last], MASKED), own], axis=1)
            best = jnp.max(own, axis=1, keepdims=True)
            top_ref[h : h + 1, :] = jnp.maximum(
                top_ref[h : h + 1, :], jnp.max(best, axis=0, keepdims=True)
            )
            p = jnp.exp(own - best)
            p = (p * (1.0 / jnp.sum(p, axis=1, keepdims=True))).astype(BF)
            p_ref[0, h, :, column:] = p
            part = dot(p, value)
            out = part if out is None else jnp.where(masks[h], part, out)
        out_ref[...] = out.astype(BF)

    for span in range(1, tiles):
        @pl.when(i == span - 1)
        def _():
            rows_of(span)

    @pl.when(i >= tiles - 1)
    def _():
        rows_of(tiles)


def attend(pick, me, parts, packed, diag, ends, hp, block):
    width = parts[0].shape[1]
    count = pick.shape[0]
    seq = count * block
    lanes = hp * HDIM
    tiles = diag.shape[0] // hp
    row = lambda i: (i, 0)
    fixed = lambda i: (0, 0)
    pairs = count * tiles * hp * block * block
    return call(
        lambda *refs: attend_kernel(tiles, hp, len(parts), len(packed), *refs),
        (
            struct((seq, width), BF),
            struct((seq, 3 * lanes), BF),
            struct((count, hp, block, tiles * block), BF),
            struct((seq, lanes), BF),
            struct((8, 128), F32),
            struct((width, AUX), BF),
        ),
        24e9,
        8 * seq * width + 2 * pairs,
        grid=(count,),
        in_specs=[pl.BlockSpec(memory_space=pltpu.SMEM)] * 2
        + [pl.BlockSpec(memory_space=pl.ANY)] * (len(parts) + len(packed))
        + [
            pl.BlockSpec(diag.shape, fixed),
            pl.BlockSpec(memory_space=pltpu.SMEM),
        ],
        out_specs=[
            pl.BlockSpec((block, width), row),
            pl.BlockSpec((block, 3 * lanes), row),
            pl.BlockSpec((1, hp, block, tiles * block), lambda i: (i, 0, 0, 0)),
            pl.BlockSpec((block, lanes), row),
            pl.BlockSpec((8, 128), fixed),
            pl.BlockSpec((width, AUX), fixed),
        ],
        scratch_shapes=[
            pltpu.VMEM((hp, block, tiles * block), F32),
            pltpu.VMEM((seq, lanes), BF),
            pltpu.VMEM((seq, lanes), BF),
            pltpu.VMEM((count, block, width), BF),
            pltpu.SemaphoreType.DMA((count,)),
            pltpu.VMEM((len(packed),) + packed[0].shape, BF),
            pltpu.SemaphoreType.DMA((len(packed),)),
            pltpu.VMEM((1, width), F32),
        ],
    )(pick, me, *parts, *packed, diag, ends)


def output_rows_kernel(sources, first, rows, pick_ref, *refs):
    parts = refs[:sources]
    out_ref, qkv_ref, arrived = refs[sources:]
    width = out_ref.shape[1]

    def place(at, number):
        here = pl.ds(at * rows, rows)
        if number == 0:
            return out_ref.at[here]
        return qkv_ref.at[here, pl.ds((number - 1) * width, width)]

    for at in range(pick_ref.shape[0]):
        for source in range(len(parts) - (parts[-1].shape[0] != parts[0].shape[0])):
            @pl.when(pick_ref[at] == source)
            def _():
                for number in range(4):
                    for copy in part_copies(
                        parts, source, first + number * rows, rows, place(at, number),
                        arrived.at[at, number],
                    ):
                        copy.start()
    for at in range(pick_ref.shape[0]):
        for number in range(4):
            pltpu.make_async_copy(
                parts[0].at[pl.ds(0, rows)], place(at, number), arrived.at[at, number]
            ).wait()


def attend_back_kernel(tiles, hp, me_ref, grad_ref, p_ref, qkv_ref, normed_ref, marks_ref, top_ref,
                       out_ref, kept_ref, away_ref, bias_grad, key_grad, value_grad):
    i = pl.program_id(0)
    block, lanes = grad_ref.shape

    @pl.when(i == 0)
    def _():
        bias_grad[...] = jnp.zeros_like(bias_grad)
        key_grad[...] = jnp.zeros_like(key_grad)
        value_grad[...] = jnp.zeros_like(value_grad)

    here = pl.multiple_of(i * block, block)
    query = qkv_ref[pl.ds(here, block), :lanes] * jnp.asarray(HDIM ** -0.5, BF)
    grad = grad_ref[...]
    masks = [head_lanes(block, lanes, h) for h in range(hp)]

    def rows_of(span):
        wide = span * block
        first = pl.multiple_of((i - span + 1) * block, block)
        column = (tiles - span) * block
        key = qkv_ref[pl.ds(first, wide), lanes : 2 * lanes]
        value = qkv_ref[pl.ds(first, wide), 2 * lanes :]
        out = key_part = value_part = None
        for h in range(hp):
            head = jnp.where(masks[h], query, jnp.zeros_like(query))
            head_grad = jnp.where(masks[h], grad, jnp.zeros_like(grad))
            weight = p_ref[0, h, :, column:]
            wide_weight = weight.astype(F32)
            t = wide_weight * dot(head_grad, value, ((1,), (1,)))
            s = t - wide_weight * jnp.sum(t, axis=1, keepdims=True)
            bias_grad[h, :, column:] += s
            s = s.astype(BF)
            part = dot(s, key)
            out = part if out is None else jnp.where(masks[h], part, out)
            part = dot(s, head, ((0,), (0,)))
            key_part = part if key_part is None else key_part + part
            part = dot(weight, head_grad, ((0,), (0,)))
            value_part = part if value_part is None else value_part + part
        key_grad[pl.ds(first, wide), :] += key_part
        value_grad[pl.ds(first, wide), :] += value_part
        out_ref[pl.ds(here, block), :lanes] = (out * HDIM ** -0.5).astype(BF)

    for span in range(1, tiles):
        @pl.when(i == span - 1)
        def _():
            rows_of(span)

    @pl.when(i >= tiles - 1)
    def _():
        rows_of(tiles)

    @pl.when(i == pl.num_programs(0) - 1)
    def _():
        out_ref[:, lanes : 2 * lanes] = key_grad[...].astype(BF)
        out_ref[:, 2 * lanes :] = value_grad[...].astype(BF)
        grad_cols = dot(normed_ref[...], out_ref[...], ((0,), (0,))).astype(BF)
        split_store(kept_ref, away_ref, me_ref[0], grad_cols)
        bins = marks_ref.shape[1]
        wide = 3 * lanes
        notes = []
        for h in range(hp):
            total = jnp.zeros((1, bins), F32)
            for m in range(tiles):
                at = (tiles - 1 - m) * block
                x = bias_grad[h, :, at : at + block]
                x = jnp.concatenate([x, jnp.zeros((block, block), F32)], axis=1)
                half = block // 2
                while half >= 1:
                    x = x[:half] + pltpu.roll(x[half : 2 * half], 2 * block - half, 1)
                    half //= 2
                high, low = halves(x)
                part = marks_ref[m * 2 * block : (m + 1) * 2 * block, :]
                total += dot(high, part) + dot(low, part)
            notes.append(jnp.concatenate([total, jnp.zeros((1, wide - bins), F32)], axis=1))
        spot = lax.broadcasted_iota(jnp.int32, (1, AUX), 1) == me_ref[0]
        for h in range(hp):
            top = top_ref[h : h + 1, :]
            high = top.astype(BF).astype(F32)
            notes.append(
                jnp.concatenate(
                    [jnp.where(spot, high, 0.0), jnp.where(spot, top - high, 0.0)]
                    + [jnp.zeros((1, wide - 2 * AUX), F32)],
                    axis=1,
                )
            )
        notes.append(jnp.zeros((16 - 2 * hp, wide), F32))
        notes = jnp.concatenate(notes, axis=0).astype(BF)
        for ref in (kept_ref, away_ref):
            for at in range(ref.shape[0]):
                ref[at, ref.shape[1] - 16 :] = notes


def attend_back(me, attention_grad, weights, qkv, normed, marks, top, hp, block, spread):
    seq, lanes = attention_grad.shape
    count = seq // block
    width = normed.shape[1]
    tiles = weights.shape[3] // block
    fixed = lambda i: (0, 0)
    pairs = count * tiles * hp * block * block
    owned = (spread // 2, width // spread + 16, 3 * lanes)
    return call(
        lambda *refs: attend_back_kernel(tiles, hp, *refs),
        (struct((seq, 3 * lanes), BF), struct(owned, BF), struct(owned, BF)),
        60e9,
        10 * seq * lanes + 2 * pairs,
        grid=(count,),
        in_specs=[
            pl.BlockSpec(memory_space=pltpu.SMEM),
            pl.BlockSpec((block, lanes), lambda i: (i, 0)),
            pl.BlockSpec((1, hp, block, tiles * block), lambda i: (i, 0, 0, 0)),
            pl.BlockSpec((seq, 3 * lanes), fixed),
            pl.BlockSpec((seq, width), fixed),
            pl.BlockSpec(marks.shape, fixed),
            pl.BlockSpec(top.shape, fixed),
        ],
        out_specs=[pl.BlockSpec((seq, 3 * lanes), fixed)]
        + [pl.BlockSpec(owned, lambda i: (0, 0, 0))] * 2,
        scratch_shapes=[
            pltpu.VMEM((hp, block, tiles * block), F32),
            pltpu.VMEM((seq, lanes), F32),
            pltpu.VMEM((seq, lanes), F32),
        ],
    )(me, attention_grad, weights, qkv, normed, marks, top)


def upstream_kernel(places_ref, other_ref, grad_ref, out_ref):
    experts, capacity, _ = out_ref.shape
    rows = grad_ref.shape[0]
    slots = experts * capacity
    other = other_ref[...]
    slot = lax.broadcasted_iota(jnp.int32, (slots, rows), 0)
    first = jnp.where(slot == places_ref[0:1, :], 1.0, 0.0).astype(BF)
    second = jnp.where(slot == places_ref[1:2, :], 1.0, 0.0).astype(BF)
    sent = dot(first + second, grad_ref[...]).astype(BF)
    named = (dot(first, other[0]) + dot(second, other[1])).astype(BF)
    for at in range(experts):
        here = slice(at * capacity, (at + 1) * capacity)
        out_ref[at, :, 128:] = sent[here]
        out_ref[at, :, :128] = named[here]


def token_front_kernel(spread, me_ref, attn_ref, tok_ref, aux_ref, places_ref, *refs):
    w_refs = refs[:spread]
    attention_ref, resid_ref, normed_ref = refs[spread : spread + 3]
    buffers = refs[spread + 3 : -2]
    whole, arrived = refs[-2:]
    collect(w_refs, me_ref[0], whole, arrived)
    blocks = attn_ref.shape[0]
    attention = jnp.concatenate([attn_ref[at] for at in range(blocks)], axis=1)
    attention_ref[...] = attention
    width = attention.shape[1]
    gain = gain_row(aux_ref[...], 1)
    collected(w_refs, whole, arrived)
    resid = tok_ref[...].astype(F32) + dot(attention, whole[...].reshape(width, width))
    resid_ref[...] = resid
    r = lax.rsqrt(jnp.mean(resid * resid, axis=1, keepdims=True) + EPSILON)
    normed = (resid * r * gain).astype(BF)
    normed_ref[...] = normed
    slots = buffers[0].shape[0]
    slot = lax.broadcasted_iota(jnp.int32, (slots * len(buffers), normed.shape[0]), 0)
    named = (slot == places_ref[2:3, :]) | (slot == places_ref[3:4, :])
    sent = dot(jnp.where(named, 1.0, 0.0).astype(BF), normed).astype(BF)
    for k, buffer in enumerate(buffers):
        buffer[...] = sent[k * slots : (k + 1) * slots]


def token_middle_kernel(returned_ref, resid_ref, normed_ref, aux_ref, ids_ref, grad_ref,
                        mixed_ref, logit_ref, route_ref):
    slots = returned_ref.shape[0]
    rows = resid_ref.shape[0]
    slot = lax.broadcasted_iota(jnp.int32, (rows, slots), 1)
    first = jnp.where(slot == ids_ref[:, 0:1], 1.0, 0.0).astype(BF)
    second = jnp.where(slot == ids_ref[:, 1:2], 1.0, 0.0).astype(BF)
    returned = returned_ref[...]
    first_out = dot(first, returned)
    second_out = dot(second, returned)
    normed = normed_ref[...]
    logits = dot(normed, aux_ref[...])
    lane = lax.broadcasted_iota(jnp.int32, logits.shape, 1) - ROUTER_AT
    at_first = lane == ids_ref[:, 2:3]
    at_second = lane == ids_ref[:, 3:4]
    gap = jnp.sum(
        jnp.where(at_first, logits, 0.0) - jnp.where(at_second, logits, 0.0),
        axis=1, keepdims=True,
    )
    gate_one = 1.0 / (1.0 + jnp.exp(-gap))
    gate_two = 1.0 / (1.0 + jnp.exp(gap))
    mixed_ref[...] = (resid_ref[...] + gate_one * first_out + gate_two * second_out).astype(BF)
    upstream = grad_ref[...].astype(F32)
    change = jnp.sum(upstream * (first_out - second_out), axis=1, keepdims=True)
    slope = gate_one * gate_two * change
    logit = jnp.where(at_first, slope, 0.0) - jnp.where(at_second, slope, 0.0)
    logit_ref[...] = logit
    high, low = halves(logit)
    route_ref[...] = dot(normed, high, ((0,), (0,))) + dot(normed, low, ((0,), (0,)))


def norm_back(values, gain, grad):
    r = lax.rsqrt(jnp.mean(values * values, axis=1, keepdims=True) + EPSILON)
    scaled = grad * gain
    slope = jnp.mean(values * scaled, axis=1, keepdims=True)
    return r * scaled - values * (r * r * r * slope), r


def token_back_kernel(spread, me_ref, logit_ref, aux_ref, ids_ref, resid_ref, grad_ref, back_ref,
                      *refs):
    w_refs = refs[:spread]
    attention_ref, route_ref = refs[spread : spread + 2]
    resid_grad_ref, attention_grad_ref, kept_ref, away_ref, whole, arrived = refs[-6:]
    collect(w_refs, me_ref[0], whole, arrived)
    resid = resid_ref[...]
    rows, width = resid.shape
    slots = back_ref.shape[0]
    slot = lax.broadcasted_iota(jnp.int32, (rows, slots), 1)
    named = (slot == ids_ref[:, 0:1]) | (slot == ids_ref[:, 1:2])
    normed_grad = dot(jnp.where(named, 1.0, 0.0).astype(BF), back_ref[...])
    high, low = halves(logit_ref[...])
    aux = aux_ref[...]
    gain = gain_row(aux, 1)
    normed_grad += dot(high, aux, ((1,), (1,))) + dot(low, aux, ((1,), (1,)))
    part, r = norm_back(resid, gain, normed_grad)
    resid_grad = grad_ref[...].astype(F32) + part
    resid_grad_ref[...] = resid_grad
    gain_grad = jnp.sum(normed_grad * resid * r, axis=0, keepdims=True)
    proj = resid_grad.astype(BF)
    blocks, _, lanes = attention_grad_ref.shape
    collected(w_refs, whole, arrived)
    grad = dot(proj, whole[...].reshape(width, width), ((1,), (1,))).astype(BF)
    for at in range(blocks):
        attention_grad_ref[at] = grad[:, at * lanes : (at + 1) * lanes]
    grad_proj = dot(attention_ref[...], proj, ((0,), (0,))).astype(BF)
    lane = lax.broadcasted_iota(jnp.int32, (width, AUX), 1)
    gain_grad = jnp.broadcast_to(gain_grad, (AUX, width)).T
    small = jnp.where(lane == GAIN_AT, gain_grad, route_ref[...]).astype(BF)
    split_store(kept_ref, away_ref, me_ref[0], jnp.concatenate([grad_proj, small], axis=1))


def token_last_kernel(blocks_ref, w_ref, tok_ref, aux_ref, resid_grad_ref, out_ref, grads, total):
    part = pl.program_id(0)
    blocks, _, wide = blocks_ref.shape
    lanes = wide // 3
    for number in range(3):
        @pl.when(part == number)
        def _():
            for at in range(blocks):
                grads[:, at * lanes : (at + 1) * lanes] = blocks_ref[
                    at, :, number * lanes : (number + 1) * lanes
                ]

    term = dot(grads[...], w_ref[...], ((1,), (1,)))

    @pl.when(part == 0)
    def _():
        total[...] = term

    @pl.when(part > 0)
    def _():
        total[...] += term

    @pl.when(part == 2)
    def _():
        change, _ = norm_back(tok_ref[...].astype(F32), gain_row(aux_ref[...], 0), total[...])
        out_ref[...] = resid_grad_ref[...] + change


def note_row(notes, hp, spread, head):
    lane = lax.broadcasted_iota(jnp.int32, (1, AUX), 1)
    rel = jnp.where(lane < BUCKETS, notes[head : head + 1, :AUX], 0.0)
    tops = notes[hp + head : hp + head + 1]
    high = jnp.where(lane < spread, tops[:, :AUX], 0.0)
    low = jnp.where(lane < spread, tops[:, AUX : 2 * AUX], 0.0)
    return rel, high, low


def join_kernel(hp, spread, own_ref, proj_kept_ref, proj_got_ref, cols_kept_ref, cols_got_ref,
                kept_ref, away_ref):
    rows, wide = proj_kept_ref.shape
    pairs, own_rows, _ = kept_ref.shape
    even = own_ref[0] % 2 == 0
    proj = proj_kept_ref[...].astype(F32) + proj_got_ref[...].astype(F32)
    cols = cols_kept_ref[...].astype(F32) + cols_got_ref[...].astype(F32)
    notes = cols[rows:]
    row = lax.broadcasted_iota(jnp.int32, (own_rows, AUX), 0)
    extra = jnp.zeros((own_rows, AUX), F32)
    for h in range(hp):
        rel, high, low = note_row(notes, hp, spread, h)
        line = pltpu.roll(rel, BIAS_AT, 1) + pltpu.roll(high, TOP_AT, 1)
        line += pltpu.roll(low, TOP_LOW_AT, 1)
        extra += jnp.where(row == h + hp * (own_ref[0] % 2), line, 0.0)
    extra = jnp.concatenate([jnp.zeros((own_rows, wide - AUX), F32), extra], axis=1)
    for pair in range(pairs):
        at = 2 * pair * own_rows
        one, two = slice(at, at + own_rows), slice(at + own_rows, at + 2 * own_rows)
        kept_ref[pair, :, :wide] = (jnp.where(even, proj[one], proj[two]) + extra).astype(BF)
        away_ref[pair, :, :wide] = (jnp.where(even, proj[two], proj[one]) + extra).astype(BF)
        kept_ref[pair, :, wide:] = jnp.where(even, cols[one], cols[two]).astype(BF)
        away_ref[pair, :, wide:] = jnp.where(even, cols[two], cols[one]).astype(BF)


def pair_kernel(wide, own_ref, kept_ref, got_ref, *sends):
    even = own_ref[0] % 2 == 0
    for k, send in enumerate(sends):
        pair = (own_ref[0] // 2) ^ k
        kept, got = kept_ref[pair], got_ref[pair]
        send[:, :wide] = (kept[:, :wide].astype(F32) + got[:, :wide].astype(F32)).astype(BF)
        columns = kept.shape[1] - wide
        send[:, wide : wide + columns] = jnp.where(even, kept[:, wide:], got[:, wide:])
        send[:, wide + columns :] = jnp.where(even, got[:, wide:], kept[:, wide:])


def join_plain(hp, spread, place, groups, proj_terms, cols_terms):
    proj, cols = joined(proj_terms), joined(cols_terms)
    rows, wide = proj.shape
    own_rows = rows // groups
    notes = cols[rows:]
    whole = jnp.concatenate([proj, cols[:rows]], axis=1).reshape(groups, own_rows, -1)
    lines = []
    for h in range(hp):
        rel, high, low = note_row(notes, hp, spread, h)
        line = jnp.roll(rel, BIAS_AT, 1) + jnp.roll(high, TOP_AT, 1) + jnp.roll(low, TOP_LOW_AT, 1)
        lines.append(line)
    extra = jnp.concatenate(lines, axis=0)
    extra = jnp.pad(extra, ((0, own_rows - hp), (wide - AUX, whole.shape[2] - wide)))
    whole = (whole + extra).astype(BF)
    return [
        lax.dynamic_index_in_dim(whole, place ^ k, axis=0, keepdims=False) for k in range(groups)
    ]


def owner_kernel(hp, sharers, spread, own_ref, q_ref, k_ref, v_ref, gain_ref, *refs):
    (proj_ref, route_ref, gain_two_ref, gq_ref, gk_ref, gv_ref, gain_one_ref, rel_ref,
     factor_ref, summary_ref) = refs[-10:]
    blocks = refs[:-10]
    experts = route_ref.shape[0]
    eye = lax.broadcasted_iota(jnp.int32, (proj_ref.shape[0],) * 2, 0)
    eye = eye == lax.broadcasted_iota(jnp.int32, eye.shape, 1)

    def as_row(column):
        return jnp.sum(jnp.where(eye, column, 0.0), axis=0, keepdims=True)

    width = proj_ref.shape[1]
    lanes = hp * HDIM
    sources = (blocks[0].shape[1] - width - AUX) // (3 * lanes)
    total = None
    for block in blocks:
        term = block[:, : width + AUX].astype(F32)
        total = term if total is None else total + term
    proj_ref[...] = total[:, :width]
    small = total[:, width:].T
    route_ref[...] = small[ROUTER_AT : ROUTER_AT + experts]
    gain_two_ref[...] = small[GAIN_AT : GAIN_AT + 1]
    outs = (gq_ref, gk_ref, gv_ref)
    for out in outs:
        out[...] = jnp.zeros_like(out)
    lane = lax.broadcasted_iota(jnp.int32, (1, 128), 1)
    summary_ref[...] = jnp.where(
        lax.broadcasted_iota(jnp.int32, summary_ref.shape, 1) == 64, MASKED, 0.0
    )
    for k, source in [(k, source) for k in range(len(blocks)) for source in range(sources)]:
        block = blocks[k]
        seat = (((own_ref[0] // sources) ^ k) * sources + source) % sharers
        at = pl.multiple_of(seat * lanes, lanes)
        for part, out in enumerate(outs):
            first = width + AUX + (3 * source + part) * lanes
            out[:, pl.ds(at, lanes)] += block[:, first : first + lanes].astype(F32)
        notes = block[:, width : width + AUX].astype(F32)
        for h in range(hp):
            note = notes[source * hp + h : source * hp + h + 1]
            rel = jnp.where(lane < BUCKETS, pltpu.roll(note, AUX - BIAS_AT, 1), 0.0)
            tops = pltpu.roll(note, AUX - TOP_AT, 1) + pltpu.roll(note, AUX - TOP_LOW_AT, 1)
            top = jnp.max(jnp.where(lane < spread, tops, MASKED), axis=1, keepdims=True)
            old = summary_ref[pl.ds(seat * hp + h, 1), :]
            new = jnp.where(lane == 64, jnp.maximum(old, top), old + rel)
            summary_ref[pl.ds(seat * hp + h, 1), :] = new
    rel_ref[...] = summary_ref[:, :BUCKETS]
    factor_ref[...] = jnp.sqrt(CLIP_LEVEL / jnp.maximum(summary_ref[...].T[64:65], 1.0))
    grad = jnp.zeros((proj_ref.shape[0], 1), F32)
    for out, w_ref in zip(outs, (q_ref, k_ref, v_ref)):
        grad += jnp.sum(out[...] * w_ref[...].astype(F32), axis=1, keepdims=True)
    gain_one_ref[...] = as_row(grad) / gain_ref[...]


GELU_A = 0.7978845608028654
GELU_B = 0.044715


def expert_kernel(groups, own_ref, upstream_ref, aux_ref, gate_ref, up_ref, down_ref, *refs):
    blocks = refs[:groups]
    (gate_pre_ref, up_pre_ref, out_ref, rows_ref, slot_grad_ref, grad_down_ref, total) = refs[groups:]
    f = pl.program_id(0)
    capacity, width = blocks[0].shape

    @pl.when(f == 0)
    def _():
        total[...] = jnp.zeros_like(total)
        for k, block in enumerate(blocks):
            rows_ref[k * capacity : (k + 1) * capacity, :] = block[...]
        all_logits = dot(rows_ref[...], aux_ref[...])
        for k in range(groups):
            here = slice(k * capacity, (k + 1) * capacity)
            logits = all_logits[here]
            lane = lax.broadcasted_iota(jnp.int32, logits.shape, 1) - ROUTER_AT
            upstream = upstream_ref[own_ref[0] ^ k]
            other = upstream[:, 0:1].astype(F32).astype(jnp.int32)
            gap = jnp.sum(
                jnp.where(lane == other, logits, 0.0) - jnp.where(lane == own_ref[0], logits, 0.0),
                axis=1, keepdims=True,
            )
            gate = 1.0 / (1.0 + jnp.exp(gap))
            slot_grad_ref[here, :] = (gate * upstream[:, 128:].astype(F32)).astype(BF)

    rows = rows_ref[...]
    gate_pre = dot(rows, gate_ref[...])
    up_pre = dot(rows, up_ref[...])
    gate_pre_ref[...] = gate_pre
    up_pre_ref[...] = up_pre
    inner = jnp.tanh(GELU_A * (gate_pre + GELU_B * gate_pre * gate_pre * gate_pre))
    hidden = (0.5 * gate_pre * (1.0 + inner) * up_pre).astype(BF)
    total[...] += dot(hidden, down_ref[...])
    grad_down_ref[...] = dot(hidden, slot_grad_ref[...], ((0,), (0,))).astype(BF)

    @pl.when(f == pl.num_programs(0) - 1)
    def _():
        for k in range(groups):
            out_ref[own_ref[0] ^ k] = total[k * capacity : (k + 1) * capacity, :].astype(BF)


def expert_forward(own, upstream, aux, blocks, gate, up, down, tile):
    groups = len(blocks)
    capacity, width = blocks[0].shape
    count = groups * capacity
    ff = gate.shape[1]
    fixed = lambda f: (0, 0)
    cols = lambda f: (0, f)
    return call(
        lambda *refs: expert_kernel(groups, *refs),
        (
            struct((count, ff), F32),
            struct((count, ff), F32),
            struct((groups, capacity, width), BF),
            struct((count, width), BF),
            struct((count, width), BF),
            struct((ff, width), BF),
        ),
        24e9,
        6 * width * ff + 10 * count * ff,
        grid=(ff // tile,),
        in_specs=[
            pl.BlockSpec(memory_space=pltpu.SMEM),
            pl.BlockSpec(upstream.shape, lambda f: (0, 0, 0)),
            pl.BlockSpec(aux.shape, fixed),
            pl.BlockSpec((width, tile), cols),
            pl.BlockSpec((width, tile), cols),
            pl.BlockSpec((tile, width), lambda f: (f, 0)),
        ]
        + [pl.BlockSpec((capacity, width), fixed)] * groups,
        out_specs=[
            pl.BlockSpec((count, tile), cols),
            pl.BlockSpec((count, tile), cols),
            pl.BlockSpec((groups, capacity, width), lambda f: (0, 0, 0)),
            pl.BlockSpec((count, width), fixed),
            pl.BlockSpec((count, width), fixed),
            pl.BlockSpec((tile, width), lambda f: (f, 0)),
        ],
        scratch_shapes=[pltpu.VMEM((count, width), F32)],
    )(own, upstream, aux, gate, up, down, *blocks)


def split_store(kept_ref, away_ref, me, values):
    rows = values.shape[0] // (2 * kept_ref.shape[0])
    for d in range(2 * kept_ref.shape[0]):
        block = values[d * rows : (d + 1) * rows]
        @pl.when(me % 2 == d % 2)
        def _():
            kept_ref[d // 2, :rows] = block

        @pl.when(me % 2 != d % 2)
        def _():
            away_ref[d // 2, :rows] = block


def expert_back_kernel(own_ref, me_ref, slot_grad_ref, rows_ref, gate_pre_ref, up_pre_ref, down_ref,
                       gate_ref, up_ref, row_grad_ref, grad_gate_ref, up_kept_ref, up_away_ref,
                       total, pre_grads, split_rows):
    f = pl.program_id(0)
    tiles = pl.num_programs(0) - 1
    tile = gate_ref.shape[1]
    groups, capacity, _ = row_grad_ref.shape

    def through_gelu(slot):
        hidden_grad = dot(slot_grad_ref[...], down_ref[...], ((1,), (1,)))
        v = gate_pre_ref[...]
        square = v * v
        inner = jnp.tanh(v * (GELU_A + GELU_A * GELU_B * square))
        half = 0.5 + 0.5 * inner
        slope = half + (0.5 * v) * (1.0 - inner * inner) * (
            GELU_A + 3.0 * GELU_A * GELU_B * square
        )
        pre_grads[slot, :, :tile] = (hidden_grad * up_pre_ref[...] * slope).astype(BF)
        pre_grads[slot, :, tile:] = (hidden_grad * (v * half)).astype(BF)

    def to_weights(slot):
        both = pre_grads[slot]
        weights = jnp.concatenate([gate_ref[...], up_ref[...]], axis=1)
        total[...] += dot(both, weights, ((1,), (1,)))
        grad_gate_ref[...] = dot(rows_ref[...], both[:, :tile], ((0,), (0,))).astype(BF)
        grads = dot(split_rows[...], both[:, tile:], ((0,), (0,))).astype(BF)
        half = grads.shape[0] // 2
        up_kept_ref[...] = grads[:half].reshape(up_kept_ref.shape)
        up_away_ref[...] = grads[half:].reshape(up_kept_ref.shape)

    @pl.when(f == 0)
    def _():
        total[...] = jnp.zeros_like(total)
        part = up_kept_ref.shape[1]
        half = rows_ref.shape[1] // 2
        even = me_ref[0] % 2 == 0
        for pair in range(up_kept_ref.shape[0]):
            one = rows_ref[:, 2 * pair * part : (2 * pair + 1) * part]
            two = rows_ref[:, (2 * pair + 1) * part : (2 * pair + 2) * part]
            at = pair * part
            split_rows[:, at : at + part] = jnp.where(even, one, two)
            split_rows[:, half + at : half + at + part] = jnp.where(even, two, one)
        through_gelu(0)

    @pl.when((f > 0) & (f < tiles))
    def _():
        to_weights((f - 1) % 2)
        through_gelu(f % 2)

    @pl.when(f == tiles)
    def _():
        to_weights((f - 1) % 2)
        for k in range(groups):
            row_grad_ref[own_ref[0] ^ k] = total[k * capacity : (k + 1) * capacity, :].astype(BF)


def expert_backward(own, me, slot_grad, rows, gate_pre, up_pre, gate, up, down, tile, groups,
                    spread):
    count, width = rows.shape
    ff = gate.shape[1]
    tiles = ff // tile
    fixed = lambda f: (0, 0)
    now = lambda f: (0, jnp.minimum(f, tiles - 1))
    before = lambda f: (0, jnp.maximum(f - 1, 0))
    owned = (spread // 2, width // spread)
    return call(
        expert_back_kernel,
        [
            struct((groups, count // groups, width), BF),
            struct((width, ff), BF),
        ]
        + [struct(owned + (ff,), BF)] * 2,
        30e9,
        12 * width * ff + 10 * count * ff,
        grid=(tiles + 1,),
        in_specs=[
            pl.BlockSpec(memory_space=pltpu.SMEM),
            pl.BlockSpec(memory_space=pltpu.SMEM),
            pl.BlockSpec((count, width), fixed),
            pl.BlockSpec((count, width), fixed),
            pl.BlockSpec((count, tile), now),
            pl.BlockSpec((count, tile), now),
            pl.BlockSpec((tile, width), lambda f: (jnp.minimum(f, tiles - 1), 0)),
            pl.BlockSpec((width, tile), before),
            pl.BlockSpec((width, tile), before),
        ],
        out_specs=[
            pl.BlockSpec((groups, count // groups, width), lambda f: (0, 0, 0)),
            pl.BlockSpec((width, tile), before),
        ]
        + [pl.BlockSpec(owned + (tile,), lambda f: (0, 0, jnp.maximum(f - 1, 0)))] * 2,
        scratch_shapes=[
            pltpu.VMEM((count, width), F32),
            pltpu.VMEM((2, count, 2 * tile), BF),
            pltpu.VMEM((count, width), BF),
        ],
    )(own, me, slot_grad, rows, gate_pre, up_pre, down, gate, up)


def slot_places(routes, experts, capacity):
    chosen = (routes[:, :, None] == jnp.arange(experts, dtype=jnp.int32)[None, None, :]).astype(
        jnp.int32
    )
    order = jnp.swapaxes(chosen, 0, 1).reshape(-1, experts)
    before = jnp.cumsum(order, axis=0) - order
    slots = jnp.sum(before * order, axis=1).reshape(TOP, -1).T
    return routes * capacity + slots


def flip(values, axis, mask):
    n = lax.axis_size(axis)
    return lax.ppermute(values, axis, [(k, k ^ mask) for k in range(n)])


def gather_parts(part, axis):
    return gather_rest({0: part}, axis, lax.axis_size(axis) // 2)


def gather_rest(held, axis, bit):
    while bit >= 1:
        held.update({j ^ bit: flip(values, axis, bit) for j, values in list(held.items())})
        bit //= 2
    return [held[j] for j in range(len(held))]


def swap_parts(parts, axis):
    return [parts[0]] + [flip(parts[k], axis, k) for k in range(1, len(parts))]


def ring_parts(tokens, before, between):
    devices = lax.axis_size("expert")
    line = list(range(0, devices, 2)) + list(range(devices - 1, 0, -2))
    spots = [line.index(k) for k in range(devices)]

    def move(values, step):
        pairs = [(line[k], line[(k + step) % devices]) for k in range(devices)]
        return lax.ppermute(values, "expert", pairs)

    ahead = [tokens]
    behind = [tokens]
    half = devices // 2
    for k in range(1, half):
        pair = (move(ahead[-1], 1), move(behind[-1], -1))
        if k == half - 2:
            *pair, first = lax.optimization_barrier((*pair, before[0]))
            before = (between(first),) + before[1:]
        elif k == half - 1:
            *pair, before = lax.optimization_barrier((*pair, before))
        else:
            pair = lax.optimization_barrier(pair)
        ahead.append(pair[0])
        behind.append(pair[1])
    cut = tokens.shape[0] // 2
    farthest = (move(ahead[-1][:cut], 1), move(behind[-1][cut:], -1))
    parts = ahead + behind[:0:-1] + list(farthest)
    spot = jnp.asarray(spots, jnp.int32)
    mine = jnp.sum(jnp.where(jnp.arange(devices) == lax.axis_index("expert"), spot, 0))
    gap = (mine - spot) % devices
    gap = jnp.where(gap == half, devices - 1, jnp.where(gap > half, gap - 1, gap))
    return gap.astype(jnp.int32), parts, before


def scatter_step(parts, axis, me, bit):
    pairs = parts.reshape((parts.shape[0] // 2, 2) + parts.shape[1:])
    mine = (me // bit) % 2
    away = lax.dynamic_index_in_dim(pairs, 1 - mine, axis=1, keepdims=False)
    kept = lax.dynamic_index_in_dim(pairs, mine, axis=1, keepdims=False)
    return kept, flip(away, axis, bit)


def joined(parts):
    return parts[0].astype(F32) + parts[1].astype(F32)


def scatter_rest(parts, axis):
    n = lax.axis_size(axis)
    me = lax.axis_index(axis)
    bit = 2
    while True:
        terms = scatter_step(parts, axis, me, bit)
        bit *= 2
        if bit >= n:
            return tuple(term[0] for term in terms)
        parts = joined(terms).astype(BF)


def body(tokens, gain_attn, w_query, w_key, w_value, w_output, rel_bias, gain_ffn, w_router,
         expert_gate, expert_up, expert_down, routes, doc_lengths, seq_valid, grad_output):
    length, width = tokens.shape
    groups = lax.axis_size("expert")
    spread = lax.axis_size("dp")
    place = lax.axis_index("expert")
    device = lax.axis_index("dp") * groups + place
    experts = w_router.shape[1]
    capacity = 5 * TOP * length // (4 * experts)
    slots = experts * capacity
    sharers = SEQ // length
    hp = HEADS // sharers
    lanes = hp * HDIM
    own_rows = w_query.shape[0]
    teams = None
    if groups != sharers:
        teams = [list(range(at, at + sharers)) for at in range(0, groups, sharers)]
    both = ("dp", "expert")

    def exchange(blocks):
        return lax.all_to_all(blocks, "expert", 0, 0, axis_index_groups=teams, tiled=True)

    def exchange_all(blocks):
        return lax.all_to_all(blocks, "expert", 0, 0, tiled=True)

    def columns(w):
        return w.reshape(own_rows, sharers, lanes).swapaxes(0, 1)

    extra = jnp.concatenate([gain_attn[:, None], gain_ffn[:, None], w_router], axis=1)
    extra = jnp.pad(extra, ((0, 0), (0, AUX - extra.shape[1])))
    sent = jnp.concatenate(
        [
            columns(w_query),
            columns(w_key),
            columns(w_value),
            jnp.broadcast_to(extra[None], (sharers, own_rows, AUX)),
        ],
        axis=2,
    )
    sent = jnp.tile(sent, (groups // sharers, 1, 1))
    gate_all = lax.all_gather(expert_gate[0], "dp", axis=0, tiled=True)
    up_all = lax.all_gather(expert_up[0], "dp", axis=0, tiled=True)
    down_all = lax.all_gather(expert_down[0], "dp", axis=0, tiled=True)

    places = slot_places(routes, experts, capacity)
    near_places = places + ((routes ^ place) - routes) * capacity
    ids = jnp.concatenate([places, routes, near_places], axis=1)
    ids = jnp.pad(ids, ((0, 0), (0, 128 - ids.shape[1])))
    places_row = jnp.pad(
        jnp.concatenate([places, near_places], axis=1).T, ((0, 4), (0, 0)), constant_values=-1
    )
    other = jnp.broadcast_to(routes.T[::-1, :, None], (TOP, length, 128)).astype(BF)
    upstream = call(
        upstream_kernel,
        struct((experts, capacity, width + 128), BF),
        3e9,
        4 * slots * width,
    )(places_row, other, grad_output)

    number = (device * length) // SEQ
    ends = jnp.cumsum(lax.dynamic_index_in_dim(doc_lengths, number, keepdims=False))
    ends = jnp.concatenate([ends, lax.dynamic_index_in_dim(seq_valid, number)]).astype(jnp.int32)
    block = length
    marks, inside = diagonal_tables(block, WINDOW, BUCKETS)
    head_at = (place % sharers) * hp
    own_bias = lax.dynamic_slice_in_dim(rel_bias, head_at, hp, axis=1)
    diag = jnp.dot(jnp.asarray(marks), own_bias, precision=lax.Precision.HIGHEST)
    diag = jnp.where(jnp.asarray(inside)[:, None], diag, MASKED)
    tiles = WINDOW // block + 1
    diag = diag.T.reshape(hp * tiles, 2 * block)
    packed = exchange_all(sent).reshape(groups * own_rows, 3 * lanes + AUX)
    mixed_rows = jnp.concatenate([tokens, w_output, w_query, w_key, w_value], axis=0)
    if teams is None:
        def between(values):
            return gather_parts(values, "dp")

        before = (packed, upstream, diag, ends, ids)
        pick, parts, before = ring_parts(mixed_rows, before, between)
        packed, upstream, diag, ends, ids = before
    else:
        whole = lax.all_gather(mixed_rows, "expert", axis=0, axis_index_groups=teams)
        pick = jnp.arange(sharers, dtype=jnp.int32)
        parts = [whole[at] for at in range(sharers)]
        packed = gather_parts(packed, "dp")
    me = lax.axis_index("dp").astype(jnp.int32).reshape(1)
    if teams is None:
        output_rows, qkv_rows = call(
            lambda *refs: output_rows_kernel(len(parts), length, own_rows, *refs),
            (struct((groups * own_rows, width), BF), struct((groups * own_rows, 3 * width), BF)),
            1e9,
            16 * groups * own_rows * width,
            mib=12, in_specs=[pl.BlockSpec(memory_space=pltpu.SMEM)]
            + [pl.BlockSpec(memory_space=pl.ANY)] * len(parts),
            out_specs=[pl.BlockSpec(memory_space=pltpu.VMEM)] * 2,
            scratch_shapes=[pltpu.SemaphoreType.DMA((sharers, 4))],
        )(pick, *parts)
        output_rows, attend_parts = lax.optimization_barrier((output_rows, parts))
    else:
        output_rows = lax.all_gather(w_output, "expert", axis=0, tiled=True)
        qkv_rows = jnp.concatenate([w_query, w_key, w_value], axis=1)
        qkv_rows = lax.all_gather(qkv_rows, "expert", axis=0, tiled=True)
        attend_parts = parts
    output_parts = {0: output_rows, spread // 2: flip(output_rows, "dp", spread // 2)}

    upstream, _ = lax.optimization_barrier((upstream, parts))
    upstream = exchange_all(upstream)

    normed_one, qkv, weights, attn, top, aux = attend(
        pick, me, attend_parts, packed, diag, ends, hp, block
    )
    attn, upstream, output_parts = lax.optimization_barrier((attn, upstream, output_parts))
    output_parts = gather_rest(output_parts, "dp", spread // 4)
    attn_blocks = exchange(attn.reshape(sharers, length, lanes))

    vmem = pl.BlockSpec(memory_space=pltpu.VMEM)
    smem = pl.BlockSpec(memory_space=pltpu.SMEM)
    loose = pl.BlockSpec(memory_space=pl.ANY)
    gathered = [
        pltpu.VMEM((spread,) + output_parts[0].shape, BF),
        pltpu.SemaphoreType.DMA((spread,)),
    ]
    attention, resid, normed_two, *buffers = call(
        lambda *refs: token_front_kernel(spread, *refs),
        [
            struct((length, width), BF),
            struct((length, width), F32),
            struct((length, width), BF),
        ]
        + [struct((capacity, width), BF)] * groups,
        5e9,
        2 * width * width + 8 * length * width,
        mib=24, in_specs=[smem] + [vmem] * 4 + [loose] * spread,
        scratch_shapes=gathered,
    )(me, attn_blocks, tokens, aux, places_row, *output_parts)
    rows = swap_parts(buffers, "expert")
    qkv_rows, _ = lax.optimization_barrier((qkv_rows, attn))
    qkv_all = lax.all_gather(qkv_rows, "dp", axis=0, tiled=True)

    tile = 256 if expert_gate.shape[2] % 256 == 0 else 128
    own = place.astype(jnp.int32).reshape(1)
    gate_pre, up_pre, expert_out, rows, slot_grad, grad_down = expert_forward(
        own, upstream, aux, rows, gate_all, up_all, down_all, tile
    )
    expert_out, qkv_all = lax.optimization_barrier((expert_out, qkv_all))
    returned = exchange_all(expert_out)
    row_grad, *expert_grads = expert_backward(
        own, me, slot_grad, rows, gate_pre, up_pre, gate_all, up_all, down_all, tile, groups,
        spread,
    )
    returned, row_grad, expert_grads = lax.optimization_barrier(
        (returned, row_grad, expert_grads)
    )
    grad_gate, up_kept, up_away = expert_grads
    up_first = joined((up_kept, flip(up_away, "dp", 1))).astype(BF)
    owned_down = lax.psum_scatter(grad_down, "dp", scatter_dimension=0, tiled=True)
    returned = returned.reshape(slots, width)
    back = exchange_all(row_grad)
    mixed, logit_grad, route_grad = call(
        token_middle_kernel,
        (
            struct((length, width), BF),
            struct((length, 128), F32),
            struct((width, 128), F32),
        ),
        5e9,
        2 * slots * width + 8 * length * width,
    )(returned, resid, normed_two, aux, ids, grad_output)
    back, owned_down = lax.optimization_barrier((back, owned_down))
    owned_down = owned_down.astype(F32)
    back = back.reshape(slots, width)
    cores = [list(range(core, spread, 2)) for core in range(2)]

    def scatter_chips(parts):
        parts = parts.reshape((-1,) + parts.shape[2:])
        return lax.psum_scatter(
            parts, "dp", scatter_dimension=0, axis_index_groups=cores, tiled=True
        )

    owned_gate = lax.psum_scatter(grad_gate, "dp", scatter_dimension=0, tiled=True)
    owned_up = scatter_chips(up_first)
    resid_grad, attention_grad, proj_kept, proj_away = call(
        lambda *refs: token_back_kernel(spread, *refs),
        (
            struct((length, width), F32),
            struct((sharers, length, lanes), BF),
            struct((spread // 2, width // spread, width + AUX), BF),
            struct((spread // 2, width // spread, width + AUX), BF),
        ),
        6e9,
        2 * width * width + 2 * slots * width + 8 * length * width,
        in_specs=[smem] + [vmem] * 6 + [loose] * spread + [vmem] * 2,
        scratch_shapes=gathered,
    )(me, logit_grad, aux, ids, resid, grad_output, back, *output_parts, attention, route_grad)
    attention_grad = exchange(attention_grad).reshape(SEQ, lanes)
    proj_first = proj_kept.astype(F32) + flip(proj_away, "dp", 1).astype(F32)
    attention_grad, proj_first, _ = lax.optimization_barrier(
        (attention_grad, proj_first.astype(BF), up_first)
    )
    proj_terms = scatter_rest(proj_first, "dp")

    grad_qkv_rows, cols_kept, cols_away = attend_back(
        me, attention_grad, weights, qkv, normed_one, jnp.asarray(marks, BF), top, hp, block, spread
    )
    grad_qkv_rows, cols_away, proj_terms, owned_gate = lax.optimization_barrier(
        (grad_qkv_rows, cols_away, proj_terms, owned_gate)
    )
    grads_here = exchange(grad_qkv_rows.reshape(sharers, length, 3 * lanes))
    owned_gate = owned_gate.astype(F32)
    fixed = lambda part: (0, 0)
    grad_tokens = call(
        token_last_kernel,
        struct((length, width), F32),
        60e9,
        6 * width * width + 12 * length * width,
        grid=(3,),
        in_specs=[
            pl.BlockSpec(grads_here.shape, lambda part: (0, 0, 0)),
            pl.BlockSpec((width, width), lambda part: (0, part)),
            pl.BlockSpec((length, width), fixed),
            pl.BlockSpec(aux.shape, fixed),
            pl.BlockSpec((length, width), fixed),
        ],
        out_specs=pl.BlockSpec((length, width), fixed),
        scratch_shapes=[pltpu.VMEM((length, width), BF), pltpu.VMEM((length, width), F32)],
    )(grads_here, qkv_all, tokens, aux, resid_grad)

    cols_first = cols_kept.astype(F32) + flip(cols_away, "dp", 1).astype(F32)
    cols_terms = scatter_rest(cols_first.astype(BF), "dp")
    if own_rows % 16 == 0:
        pairs = groups // 2
        blocks = struct((pairs, own_rows, width + AUX + 3 * lanes), BF)
        pairs_kept, pairs_away = call(
            lambda *refs: join_kernel(hp, spread, *refs),
            [blocks] * 2,
            1e9,
            8 * groups * own_rows * width,
            mib=12, in_specs=[smem] + [vmem] * 4,
        )(own, *proj_terms, *cols_terms)
        sends = call(
            lambda *refs: pair_kernel(width + AUX, *refs),
            [struct((own_rows, width + AUX + 6 * lanes), BF)] * pairs,
            1e9,
            8 * groups * own_rows * width,
            mib=12, in_specs=[smem] + [vmem] * 2,
        )(own, pairs_kept, flip(pairs_away, "expert", 1))
        owned = [sends[0]] + [flip(sends[k], "expert", 2 * k) for k in range(1, pairs)]
    else:
        sends = join_plain(hp, spread, place, groups, proj_terms, cols_terms)
        owned = swap_parts(sends, "expert")
    grad_tokens, owned_up = lax.optimization_barrier((grad_tokens, owned_up))
    owned_up = owned_up.astype(F32)
    *owned, grad_tokens = lax.optimization_barrier((*owned, grad_tokens))
    grad_proj, route, gain_two, grad_q, grad_k, grad_v, gain_one, rel, factor = call(
        lambda *refs: owner_kernel(hp, sharers, spread, *refs),
        (
            struct((own_rows, width), F32),
            struct((experts, own_rows), F32),
            struct((1, own_rows), F32),
            struct((own_rows, width), F32),
            struct((own_rows, width), F32),
            struct((own_rows, width), F32),
            struct((1, own_rows), F32),
            struct((HEADS, BUCKETS), F32),
            struct((1, HEADS), F32),
        ),
        2e9,
        8 * own_rows * width,
        mib=12, in_specs=[smem] + [vmem] * (4 + len(owned)),
        scratch_shapes=[pltpu.VMEM((HEADS, 128), F32)],
    )(own, w_query, w_key, w_value, gain_attn.astype(F32)[None], *owned)
    return (
        mixed,
        grad_tokens,
        gain_one[0],
        grad_q,
        grad_k,
        grad_v,
        grad_proj,
        rel.T,
        gain_two[0],
        route.T,
        owned_gate[None],
        owned_up[None],
        owned_down[None],
        factor[0],
    )


def solution(mesh):
    rows = P(("dp", "expert"), None)
    vector = P(("dp", "expert"))
    expert = P("expert", "dp", None)
    return jax.shard_map(
        body,
        mesh=mesh,
        in_specs=(
            rows, vector, rows, rows, rows, rows, P(), vector, rows,
            expert, expert, expert, rows, P(), P(), rows,
        ),
        out_specs=(
            rows, rows, vector, rows, rows, rows, rows, P(), vector, rows,
            expert, expert, expert, P(),
        ),
        check_vma=False,
    )
```
